32 devices in a mesh: blk: 8 (over z, x), ma: 4 (over y, core).
Axes of the slice: x: 2, y: 2, z: 4, core: 2. Of those that a mesh axis runs over, the one named last changes fastest.
Arguments:
- weights: bfloat16 [32, 32, 8, 4, 128], P(('blk', 'ma')), may hold values from 0.099609375 to 0.3984375
- offsets: int32 [32, 32, 8, 128], P(('blk', 'ma')), may hold values from 0 to 127
- counts: int32 [32, 32], P(('blk', 'ma')), may hold values from 1 to 8, 144 in all within a row
- block_ids: int32 [32, 32, 8], P(('blk', 'ma')), may hold values from 0 to 127
- m_table: int32 [384], replicated, may hold values from 0 to 383, as said below
- legendre: bfloat16 [384, 1664, 128], P(('blk', 'ma')), as said below
Outputs:
- kappa_band: float32 [4, 128, 4096], P(None, ('blk', 'ma'))
- potential: float32 [4, 128, 4096], P(None, ('blk', 'ma'))
The draws below stay inside these ranges and needn't reach their ends.
Inputs may be any that keep to these rules, and one draw needn't show every extreme that they name: Groups with index below counts[d, e] are live, the others hold no particles; each row sums to (8 + 1) * 32 // 2 and reaches 8. `m_table`: a permutation of 0 to 383. legendre[j, l, q] is zero for every l below m_table[j].
All inputs are finite; a program needn't handle non-finite values.
Results may differ from the reference program's by a relative error of at most 0.0058.
Values may be sent and summed in bfloat16 or wider, within the bound.
No kernel may reach another device: no remote copies, remote signals or barrier semaphores. Data moves between devices by JAX's collectives and lax.ppermute only.
A program may use at most 128 MiB of HBM per device.

```python
import math
import jax
import jax.numpy as jnp
import numpy as np
from jax import lax

NPHI = 4096
L = 1664
NBIN = 4
M_DEV = 12
CAP = 8
CYCLES = 128
M = 384
BLK_DEV = 128
DEVICES = 32


def draw_offsets(key, part):
    width = 4
    center_key, spread_key, scatter_key, choose_key = jax.random.split(key, 4)
    shape = (DEVICES, DEVICES, CAP, 128)
    centers = jax.random.randint(center_key, (DEVICES, DEVICES, CAP, 1), 0, 128 - width + 1, dtype=jnp.int32)
    spreads = jax.random.randint(spread_key, shape, 0, width, dtype=jnp.int32)
    scattered = jax.random.randint(scatter_key, shape, 0, 128, dtype=jnp.int32)
    in_clump = jax.random.randint(choose_key, shape, 0, 4, dtype=jnp.int32) < 3
    return jnp.where(in_clump, centers + spreads, scattered).astype(jnp.int32)


def draw_m_table(key, part):
    owners = M // M_DEV
    rounds = M_DEV // 2
    subkeys = jax.random.split(key, rounds)
    shuffles = jnp.stack([jax.random.permutation(subkeys[round_index], owners) for round_index in range(rounds)])
    round_ids = jnp.arange(rounds, dtype=jnp.int32)[:, None]
    leading = 2 * round_ids * owners + shuffles
    trailing = (2 * round_ids + 1) * owners + owners - 1 - shuffles
    assignment = jnp.stack([leading, trailing], axis=2)
    return jnp.transpose(assignment, (1, 0, 2)).reshape(M).astype(jnp.int32)


def draw_legendre(key, part):
    orders = draw_m_table(key, part)
    value_key = jax.random.fold_in(key, 7301)
    spread = 0.6 * CYCLES ** (-0.5)
    ramp = jnp.sqrt(jnp.minimum(1.0, (jnp.arange(L, dtype=jnp.float32) + 1.0) / 512.0))[None, :, None]
    values = jax.random.normal(value_key, (M, L, CYCLES), jnp.float32) * spread
    values = values * ramp
    degrees = jnp.arange(L, dtype=jnp.int32)[None, :, None]
    kept = degrees >= orders[:, None, None]
    return jnp.where(kept, values, 0.0).astype(jnp.bfloat16)


def plant(result, key, least, largest):
    index_at = [jax.random.randint(jax.random.fold_in(key, axis), (), 0, length) for axis, length in enumerate(result.shape)]
    longest = result.shape.index(max(result.shape))
    next_to = index_at[:longest] + [(index_at[longest] + 1) % result.shape[longest]] + index_at[longest + 1:]
    return result.at[tuple(index_at)].set(least).at[tuple(next_to)].set(largest)


def steps_of(rng, shape, shards, low, largest):
    def one(dim, parts):
        draws = jax.random.uniform(jax.random.fold_in(jax.random.fold_in(rng, 6), dim), (parts,), jnp.float32, low / len(shards), largest / len(shards))
        return jnp.repeat(jnp.exp(draws), shape[dim] // parts).reshape((-1,) + (1,) * (len(shape) - dim - 1))

    level = one(*shards[0])
    for cut in shards[1:]:
        level = level * one(*cut)
    return level


def split_up(amount, total, most, skew):
    loads = [(1 << 20) // math.isqrt(standing ** skew) + 1 for standing in range(2, amount + 1)]
    surplus, holding = total - most - (amount - 1), [1] * (amount - 1)
    while surplus > 0:
        free = [i for i in range(amount - 1) if holding[i] < most]
        mass, left = sum([loads[i] for i in free]), surplus
        for i in free:
            more = min(most - holding[i], max(1, left * loads[i] // mass), surplus)
            holding[i] = holding[i] + more
            surplus = surplus - more
    return np.array([most] + holding)


def uneven_parts(rng, amount, total, limit, skew):
    if amount == 2:
        one = jax.random.randint(rng, (), max(1, total - limit), min(limit, total - 1) + 1)
        return jnp.stack([one, total - one])
    tallies = jnp.asarray(split_up(amount, total, limit, skew), jnp.int32)
    twos = (amount - 1) // 2
    source_of, taker = tallies[1:1 + 2 * twos:2], tallies[2:2 + 2 * twos:2]
    slack = jnp.minimum(source_of - 1, limit - taker)
    passed = jax.random.randint(jax.random.fold_in(rng, 1), (twos,), 0, 1 << 20) % (slack + 1)
    tallies = tallies.at[1:1 + 2 * twos:2].set(source_of - passed).at[2:2 + 2 * twos:2].set(taker + passed)
    return tallies[jax.random.permutation(jax.random.fold_in(rng, 2), amount)]


def setup_inputs(seed: int = 0) -> dict:
    streams_of = jax.random.split(jax.random.key(seed), 7)
    return {
        "weights": jnp.clip(jnp.exp(math.log(0.3984375) - 1.3862944 * jax.random.uniform(streams_of[0], (DEVICES, DEVICES, CAP, NBIN, 128), jnp.float32) ** steps_of(streams_of[0], (DEVICES, DEVICES, CAP, NBIN, 128), ((0, 32),), -0.2, 0.2)), 0.099609375, 0.3984375).astype(jnp.bfloat16),
        "offsets": draw_offsets(jax.random.fold_in(streams_of[6], 71), 0),
        "counts": jax.vmap(lambda own: uneven_parts(own, DEVICES, (CAP + 1) * DEVICES // 2, CAP, 2))(jax.random.split(streams_of[2], DEVICES)).reshape((DEVICES, DEVICES)).astype(jnp.int32),
        "block_ids": plant(jax.random.randint(streams_of[3], (DEVICES, DEVICES, CAP), 0, BLK_DEV), jax.random.fold_in(streams_of[3], 1), 0, BLK_DEV - 1).astype(jnp.int32),
        "m_table": draw_m_table(jax.random.fold_in(streams_of[6], 71), 0),
        "legendre": draw_legendre(jax.random.fold_in(streams_of[6], 71), 0),
    }


def reference(weights, offsets, counts, block_ids, m_table, legendre):
    live_mask = jnp.arange(CAP, dtype=jnp.int32)[None, None, :] < counts[:, :, None]
    owners = jnp.arange(DEVICES, dtype=jnp.int32)[None, :, None]
    block_start = (owners * BLK_DEV + block_ids) * 128
    flat_index = (block_start[:, :, :, None] + offsets).reshape(-1).astype(jnp.int32)
    masses = jnp.where(live_mask[:, :, :, None, None], weights.astype(jnp.float32), 0.0)
    columns = jnp.transpose(masses, (0, 1, 2, 4, 3)).reshape(-1, NBIN)
    counted = jax.ops.segment_sum(columns, flat_index, num_segments=CYCLES * NPHI)
    convergence = jnp.transpose(counted).reshape(NBIN, CYCLES, NPHI)
    spectrum = jnp.fft.rfft(convergence, axis=-1)
    chosen = jnp.take(spectrum, m_table, axis=2)
    real_part = jnp.real(chosen) / NPHI
    imag_part = jnp.imag(chosen) / NPHI
    parity = jnp.arange(CYCLES, dtype=jnp.int32)[:, None] % 2
    twists = (m_table[None, :] * parity).astype(jnp.float32) * (jnp.pi / NPHI)
    twist_cos = jnp.cos(twists)
    twist_sin = jnp.sin(twists)
    real_turned = real_part * twist_cos + imag_part * twist_sin
    imag_turned = imag_part * twist_cos - real_part * twist_sin
    coefficients = jnp.stack([real_turned, imag_turned], axis=2).astype(jnp.bfloat16)
    coefficients = lax.optimization_barrier(coefficients)
    mode_rows = jnp.transpose(coefficients, (3, 0, 2, 1)).reshape(DEVICES, M_DEV, NBIN, 2, CYCLES)
    tables = legendre.reshape(DEVICES, M_DEV, L, CYCLES)
    degrees = jnp.arange(L, dtype=jnp.float32)
    filter_gain = jnp.where(degrees > 0.5, -20000.0 / jnp.maximum(degrees * (degrees + 1.0), 1.0), 0.0)

    def owner_block(operands):
        basis_block, local_modes = operands
        basis_wide = basis_block.astype(jnp.float32)
        harmonic = jnp.einsum("jlr,jbcr->jbcl", basis_wide, local_modes.astype(jnp.float32), precision=lax.Precision.HIGHEST)
        filtered = jnp.stack([harmonic, harmonic * filter_gain], axis=1).astype(jnp.bfloat16)
        filtered = lax.optimization_barrier(filtered).astype(jnp.float32)
        return jnp.einsum("jlr,jfbcl->jfbcr", basis_wide, filtered, precision=lax.Precision.HIGHEST).astype(jnp.bfloat16)

    synthesis = lax.map(owner_block, (tables, mode_rows)).reshape(M, 2, NBIN, 2, CYCLES)
    values = lax.optimization_barrier(synthesis).astype(jnp.float32)
    real_in = values[:, :, :, 0, :]
    imag_in = values[:, :, :, 1, :]
    turn_cos = jnp.transpose(twist_cos)[:, None, None, :]
    turn_sin = jnp.transpose(twist_sin)[:, None, None, :]
    real_out = real_in * turn_cos - imag_in * turn_sin
    imag_out = real_in * turn_sin + imag_in * turn_cos
    full_real = jnp.zeros((NPHI // 2 + 1, 2, NBIN, CYCLES), jnp.float32).at[m_table].set(real_out)
    full_imag = jnp.zeros((NPHI // 2 + 1, 2, NBIN, CYCLES), jnp.float32).at[m_table].set(imag_out)
    spectrum_out = jnp.transpose(full_real + 1j * full_imag, (1, 2, 3, 0))
    sky_maps = (jnp.fft.irfft(spectrum_out, n=NPHI, axis=-1) * NPHI).astype(jnp.float32)
    return sky_maps[0], sky_maps[1]
```

```python
import functools

import jax
import jax.numpy as jnp
import numpy as np
from jax import lax
from jax.experimental import pallas as pl
from jax.experimental.pallas import tpu as pltpu
from jax.sharding import Mesh, PartitionSpec as P

NPHI = 4096
BLOCK = 128
SEGMENTS = NPHI // BLOCK
LANES = 128

NT = (((1,), (1,)), ((), ()))
TN = (((0,), (0,)), ((), ()))


def dot(a, b, dims=(((1,), (0,)), ((), ()))):
    return lax.dot_general(a, b, dims, preferred_element_type=jnp.float32)


def high_low(x):
    high = x.astype(jnp.bfloat16)
    return high, (x - high.astype(jnp.float32)).astype(jnp.bfloat16)


def np_high_low(x):
    high = x.astype(np.float32).astype(jnp.bfloat16)
    return high, (x - high.astype(np.float64)).astype(np.float32).astype(jnp.bfloat16)


def analysis_tables(orders):
    m = np.arange(orders, dtype=np.int64)[:, None]
    p = np.arange(BLOCK, dtype=np.int64)[None, :]
    angle = (m * p % NPHI) * (2 * np.pi / NPHI)
    inner = np.concatenate(np_high_low(np.cos(angle)) + np_high_low(-np.sin(angle)), 1)
    half = np.arange(2 * SEGMENTS, dtype=np.int64)[None, :]
    steps = 2 * BLOCK * (half % SEGMENTS) + half // SEGMENTS
    angle = (m * steps % (2 * NPHI)) * (np.pi / NPHI)
    outer = np.concatenate(np_high_low(np.cos(angle) / NPHI) + np_high_low(-np.sin(angle) / NPHI), 1)
    return inner, outer


def bit_groups(devices):
    bits = list(range(1, devices.bit_length() - 1))
    return [bits[i : i + 2] for i in range(0, len(bits), 2)]


def positions(devices):
    order = [0]
    for group in bit_groups(devices):
        order = [p | (v << group[0]) for p in order for v in range(1 << len(group))]
    return order


def slot_rows(orders, slots):
    out = np.zeros((orders // 2, orders), np.float32)
    for block, position in enumerate(positions(orders // slots)):
        for slot in range(slots):
            out[block * slots + slot, position * slots + slot] = 1
    return out.astype(jnp.bfloat16)


def rolled(x, shift):
    return jnp.concatenate([x[:, shift:], x[:, :shift]], 1)


def exclusive_or(table, me, slots):
    orders = table.shape[1]
    block = lax.div(lax.broadcasted_iota(jnp.int32, table.shape, 1), slots)
    for bit in range((orders // slots).bit_length() - 1):
        shift = slots << bit
        swapped = jnp.where((block >> bit) % 2 == 0, rolled(table, shift), rolled(table, orders - shift))
        table = jnp.where(jnp.broadcast_to((me >> bit) & 1, table.shape) == 1, swapped, table)
    return table


def hot(condition):
    return jnp.where(condition, 1.0, 0.0).astype(jnp.bfloat16)


def half_modes(table, rows_ref, inner_ref, outer_ref, deposits, phase_hot, cycle_hot, out_ref):
    count, orders = rows_ref.shape
    cycles = cycle_hot.shape[0]
    wide = 2 * BLOCK
    held = hot(lax.broadcasted_iota(jnp.int32, (orders, orders), 0) == table)
    chunk = 192
    for start in range(0, count, chunk):
        pick = dot(rows_ref[start : start + chunk, :], held, NT).astype(jnp.bfloat16)
        inner = dot(pick, inner_ref[...]).astype(jnp.bfloat16)
        outer = dot(pick, outer_ref[...]).astype(jnp.bfloat16)
        outer_cos = dot(outer[:, :BLOCK], phase_hot)
        outer_sin = dot(outer[:, BLOCK:], phase_hot)
        for b, deposit in enumerate(deposits):
            inner_cos = dot(inner[:, :wide], deposit, NT)
            inner_sin = dot(inner[:, wide:], deposit, NT)
            real = inner_cos * outer_cos - inner_sin * outer_sin
            imag = inner_cos * outer_sin + inner_sin * outer_cos
            for part, value in ((0, real), (1, imag)):
                value = dot(value.astype(jnp.bfloat16), cycle_hot, NT)
                for tile in range(cycles // LANES):
                    at = out_ref.at[b * (cycles // LANES) + tile]
                    at[pl.ds(2 * start + part, chunk, stride=2), :] = value[:, tile * LANES : (tile + 1) * LANES]


def twice(x):
    return jnp.concatenate([x, x], 1)


def first_kernel(slots, staged, w_hbm, off_hbm, cnt_hbm, ids_hbm, table_hbm, rows_hbm, inner_hbm, outer_hbm, *refs):
    if staged:
        legendre_hbm, *refs = refs
    out_ref, deposit_ref, phase_ref, cycle_ref, table_ref, rows_ref, inner_ref, outer_ref, *refs = refs
    if staged:
        legendre_ref, *refs = refs
    w_ref, off_ref, cnt_ref, ids_ref, flat_ref, wide_ref, half_ref, sems = refs
    pairs = (
        (off_hbm, off_ref), (w_hbm, w_ref), (cnt_hbm, cnt_ref), (ids_hbm, ids_ref),
        (table_hbm, flat_ref), (rows_hbm, rows_ref), (inner_hbm, inner_ref), (outer_hbm, outer_ref),
    )
    if staged:
        pairs = pairs + ((legendre_hbm, legendre_ref),)
    copies = [pltpu.make_async_copy(a, b, sems.at[i]) for i, (a, b) in enumerate(pairs)]
    for copy in copies:
        copy.start()
    groups = off_ref.shape[0]
    capacity, devices = ids_ref.shape
    bins = w_ref.shape[0] // groups
    cycles = cycle_ref.shape[0]
    blocks_here = cycles * SEGMENTS // devices

    pack = 16
    pixel = lax.broadcasted_iota(jnp.int32, (pack, BLOCK), 0)
    pixels = [(pixel + pack * k).astype(jnp.float32).astype(jnp.bfloat16) for k in range(BLOCK // pack)]
    own = [hot(lax.div(lax.broadcasted_iota(jnp.int32, (4 * bins, BLOCK), 0), bins) == i) for i in range(4)]
    one = jnp.ones((pack, BLOCK), jnp.bfloat16)
    zero = jnp.zeros((pack, BLOCK), jnp.bfloat16)
    for copy in copies[:2]:
        copy.wait()

    def deposit(step, carry):
        start = pl.multiple_of(step * (4 * bins), 4 * bins)
        rows = w_ref[pl.ds(start, 4 * bins), :]
        left, right = [], []
        for i in range(4):
            left.append(rows * own[i])
            at = off_ref[pl.ds(step * 4 + i, 1), :].astype(jnp.float32)
            at = jnp.broadcast_to(at, (pack, BLOCK)).astype(jnp.bfloat16)
            right.append(jnp.concatenate([jnp.where(at == x, one, zero) for x in pixels], 0))
        wide_ref[pl.ds(start, 4 * bins), :] = dot(jnp.concatenate(left, 1), jnp.concatenate(right, 1), NT)
        return carry

    lax.fori_loop(0, groups // 4, deposit, 0, unroll=16)
    for copy in copies[2:8]:
        copy.wait()

    me = lax.axis_index("blk")
    for axis in ("y", "core"):
        me = me * lax.axis_size(axis) + lax.axis_index(axis)
    table = exclusive_or(flat_ref[...].reshape(table_ref.shape), me, slots)
    table_ref[...] = table

    owner = lax.div(lax.broadcasted_iota(jnp.int32, (devices, groups), 1), capacity)
    spread = hot(owner == lax.broadcasted_iota(jnp.int32, (devices, groups), 0))
    ids = dot(ids_ref[...].astype(jnp.float32).astype(jnp.bfloat16), spread)
    member = lax.rem(lax.broadcasted_iota(jnp.int32, (capacity, groups), 1), capacity)
    ids = jnp.where(member == lax.broadcasted_iota(jnp.int32, (capacity, groups), 0), ids, 0.0)
    ids = jnp.sum(ids, axis=0, keepdims=True)
    counts = jnp.broadcast_to(cnt_ref[...].astype(jnp.float32), (8, devices)).astype(jnp.bfloat16)
    counts = dot(counts, spread)[0:1, :]
    block = ids.astype(jnp.int32) + owner[0:1, :] * blocks_here
    live = member[0:1, :].astype(jnp.float32) < counts
    cycle = lax.div(block, SEGMENTS)
    phase = lax.rem(cycle, 2) * SEGMENTS + lax.rem(block, SEGMENTS)
    cycle = jnp.where(live, cycle, -1)
    phase = jnp.where(live, phase, -1)
    cycle_hot = hot(lax.broadcasted_iota(jnp.int32, (cycles, groups), 0) == cycle)
    half_hot = hot(lax.broadcasted_iota(jnp.int32, (2 * SEGMENTS, groups), 0) == phase)
    phase_hot = jnp.concatenate([half_hot, half_hot], 0)
    cycle_ref[...] = cycle_hot
    phase_ref[...] = phase_hot

    deposits = []
    for b in range(bins):
        value = wide_ref[pl.ds(b, groups, stride=bins), :].astype(jnp.bfloat16)
        deposit_ref[b] = value
        deposits.append(twice(value))
    half_modes(rolled(table, slots), rows_ref, inner_ref, outer_ref, deposits, phase_hot, cycle_hot, half_ref)
    for tile in range(half_ref.shape[0]):
        out_ref[:, tile * LANES : (tile + 1) * LANES] = half_ref[tile].astype(jnp.bfloat16)
    for copy in copies[8:]:
        copy.wait()


def second_kernel(deposit_ref, phase_ref, cycle_ref, table_ref, rows_ref, inner_ref, outer_ref, out_ref):
    deposits = [twice(deposit_ref[b]) for b in range(deposit_ref.shape[0])]
    half_modes(table_ref[...], rows_ref, inner_ref, outer_ref, deposits, phase_ref[...], cycle_ref[...], out_ref)


def split_sum(parts, tile, keep_ref, send_refs):
    rows = keep_ref.shape[0]
    lanes = slice(tile * LANES, (tile + 1) * LANES)
    for i, out_ref in enumerate((keep_ref, *send_refs)):
        value = sum(part(slice(i * rows, (i + 1) * rows), lanes) for part in parts)
        out_ref[:, lanes] = value.astype(out_ref.dtype)


def pair_kernel(mine_ref, other_ref, keep_ref, *send_refs):
    for tile in range(mine_ref.shape[0]):
        parts = (
            lambda rows, lanes: mine_ref[tile, rows, :],
            lambda rows, lanes: other_ref[rows, lanes].astype(jnp.float32),
        )
        split_sum(parts, tile, keep_ref, send_refs)


def merge_kernel(count, kept_ref, *refs):
    arrived, outs = refs[:count], refs[count:]
    for tile in range(kept_ref.shape[1] // LANES):
        parts = [lambda rows, lanes, ref=ref: ref[rows, lanes].astype(jnp.float32) for ref in (kept_ref, *arrived)]
        split_sum(parts, tile, outs[0], outs[1:])


def gain_column(degrees):
    l = np.arange(degrees, dtype=np.float32)
    return np.where(l > 0.5, np.float32(-20000.0) / np.maximum(l * (l + 1), np.float32(1)), np.float32(0)).astype(np.float32)[:, None] * np.ones((1, BLOCK), np.float32)


def interleave(cycles, cycles_here):
    out = np.zeros((2 * cycles, 2 * cycles), np.float32)
    for f in range(2):
        for c in range(cycles):
            out[f * cycles + c, (c // cycles_here * 2 + f) * cycles_here + c % cycles_here] = 1
    return out.astype(jnp.bfloat16)


def response_kernel(start, staged, legendre_ref, gain_ref, order_ref, out_ref, *scratch):
    count = out_ref.shape[0]
    if not staged:
        source, (legendre_ref, sems) = legendre_ref, scratch
        copies = [pltpu.make_async_copy(source.at[start + i], legendre_ref.at[i], sems.at[i]) for i in range(count)]
        for copy in copies:
            copy.start()
        start = 0
    for slot in range(count):
        if not staged:
            copies[slot].wait()
        basis = legendre_ref[start + slot]
        cycles = basis.shape[1]
        gain = jnp.concatenate([gain_ref[...]] * (cycles // BLOCK), 1)
        gained = (basis.astype(jnp.float32) * gain).astype(jnp.bfloat16)
        high, low = high_low(dot(basis, jnp.concatenate([basis, gained], 1), TN))
        out_ref[slot, :cycles, :] = dot(high, order_ref[...]).astype(jnp.bfloat16)
        out_ref[slot, cycles:, :] = dot(low, order_ref[...]).astype(jnp.bfloat16)


def slot_order(slots, bins):
    out = np.zeros((slots * 2 * bins, slots * 2 * bins), np.float32)
    for b in range(bins):
        for c in range(2):
            for t in range(slots):
                out[(t * 2 + c) * bins + b, (b * slots + t) * 2 + c] = 1
    return out.astype(jnp.bfloat16)


def synthesis_kernel(arrivals, pieces, kept_ref, *refs):
    partials, refs = refs[:arrivals], refs[arrivals:]
    response_refs, (order_ref, out_ref) = refs[:pieces], refs[pieces:]
    cycles = response_refs[0].shape[1] // 2
    bins = kept_ref.shape[1] // cycles
    slots = kept_ref.shape[0] // 2
    responses = [ref.at[i] for ref in response_refs for i in range(ref.shape[0])]
    total = kept_ref[...]
    for ref in partials:
        total = total + ref[...].astype(jnp.float32)
    modes = jnp.concatenate([total[:, b * cycles : (b + 1) * cycles] for b in range(bins)], 0)
    high, low = high_low(modes)
    high = dot(order_ref[...], high)
    low = dot(order_ref[...], low)
    per_slot = 2 * bins
    parts = []
    for t in range(slots):
        rows = slice(t * per_slot, (t + 1) * per_slot)
        left = jnp.concatenate([high[rows, :], low[rows, :]], 0).astype(jnp.bfloat16)
        part = dot(twice(left), responses[t][...])
        parts.append(part[:per_slot, :] + part[per_slot:, :])
    parts.append(jnp.zeros((128 - slots * per_slot, 2 * cycles), jnp.float32))
    result = jnp.concatenate(parts, 0)
    out_ref[...] = jnp.transpose(result).astype(jnp.bfloat16)


def inverse_tables(orders):
    half = NPHI // 2
    k = np.arange(half, dtype=np.int64)[None, :]
    tables = []
    for parity in range(2):
        m = np.arange(parity, orders, 2, dtype=np.int64)[:, None]
        angle = (m * k % NPHI) * (2 * np.pi / NPHI)
        tables += [np.cos(angle), -np.sin(angle)]
    chunks = np.split(np.stack(tables), half // 512, axis=2)
    return np.concatenate(chunks).reshape(-1, 512).astype(np.float32).astype(jnp.bfloat16)


def order_lanes(orders):
    padded = -(-(orders // 2) // 128) * 128
    out = np.full((2, padded), -1, np.int32)
    for parity in range(2):
        out[parity, : orders // 2] = np.arange(parity, orders, 2)
    return out.reshape(1, 2 * padded)


def turn_rows(order_row):
    m = np.maximum(order_row[0], 0).astype(np.float64)
    weight = np.where(order_row[0] == 0, 1.0, 2.0)
    parts = np_high_low(np.cos(np.pi * m / NPHI) * weight) + np_high_low(np.sin(np.pi * m / NPHI) * weight)
    return np.stack(parts + (weight.astype(jnp.bfloat16),) + (np.zeros_like(parts[0]),) * 11)


def part_rows(part, bins, cycles_here):
    shape = (2 * bins * cycles_here, 4 * bins * cycles_here)
    row = lax.broadcasted_iota(jnp.int32, shape, 0)
    column = lax.broadcasted_iota(jnp.int32, shape, 1)
    cycle = lax.rem(row, cycles_here)
    bin_number = lax.rem(lax.div(row, cycles_here), bins)
    filter_number = lax.div(row, cycles_here * bins)
    return hot(column == ((filter_number * cycles_here + cycle) * 2 + part) * bins + bin_number)


def inverse_kernel(arrived_ref, slots_hbm, lanes_hbm, turn_hbm, table_hbm, kappa_ref, potential_ref,
                   slots_ref, lanes_ref, turn_ref, table_ref, wide_ref, sems):
    copies = [
        pltpu.make_async_copy(a, b, sems.at[i])
        for i, (a, b) in enumerate(((slots_hbm, slots_ref), (lanes_hbm, lanes_ref), (turn_hbm, turn_ref)))
    ]
    half = NPHI // 2
    chunk = table_ref.shape[1]
    chunks = half // chunk
    part = table_ref.shape[0] // chunks
    for i in range(chunks):
        rows = pl.ds(i * part, part)
        copies.append(pltpu.make_async_copy(table_hbm.at[rows], table_ref.at[rows], sems.at[3 + i]))
    for copy in copies:
        copy.start()
    devices, slots = slots_ref.shape
    bins, cycles_here, _ = kappa_ref.shape
    half_orders = part // 4
    per_slot = 2 * bins
    per_source = 2 * cycles_here
    wide_ref[...] = arrived_ref[...].astype(jnp.float32)
    turned = [jnp.transpose(wide_ref[pl.ds(i, devices, stride=per_source), :]) for i in range(per_source)]
    for copy in copies[:3]:
        copy.wait()
    orders = lanes_ref[...]
    spectrum = None
    for t in range(slots):
        left = jnp.concatenate([x[t * per_slot : (t + 1) * per_slot, :] for x in turned], 0).astype(jnp.bfloat16)
        term = dot(left, hot(slots_ref[:, t : t + 1] == orders))
        spectrum = term if spectrum is None else spectrum + term
    spectrum = spectrum.astype(jnp.bfloat16)
    real_in = dot(part_rows(0, bins, cycles_here), spectrum)
    imag_in = dot(part_rows(1, bins, cycles_here), spectrum)
    turn = turn_ref[...].astype(jnp.float32)
    odd = lax.rem(lax.rem(lax.broadcasted_iota(jnp.int32, real_in.shape, 0), cycles_here), 2) == 1
    turn_cos = jnp.where(odd, turn[0:1, :] + turn[1:2, :], turn[4:5, :])
    turn_sin = jnp.where(odd, turn[2:3, :] + turn[3:4, :], 0.0)
    real = jnp.concatenate(high_low(real_in * turn_cos - imag_in * turn_sin), 0)
    imag = jnp.concatenate(high_low(real_in * turn_sin + imag_in * turn_cos), 0)
    count = real_in.shape[0]
    padded = real.shape[1] // 2
    for index in range(chunks):
        copies[3 + index].wait()
        start = index * chunk
        sums = []
        for parity in range(2):
            lanes = slice(parity * padded, parity * padded + half_orders)
            row = index * part + 2 * parity * half_orders
            both = dot(real[:, lanes], table_ref[row : row + half_orders, :])
            both = both + dot(imag[:, lanes], table_ref[row + half_orders : row + 2 * half_orders, :])
            sums.append(both[:count, :] + both[count:, :])
        first = sums[0] + sums[1]
        second = sums[0] - sums[1]
        for f, out_ref in ((0, kappa_ref), (1, potential_ref)):
            for b in range(bins):
                rows = slice((f * bins + b) * cycles_here, (f * bins + b + 1) * cycles_here)
                out_ref[b, :, start : start + chunk] = first[rows, :]
                out_ref[b, :, half + start : half + start + chunk] = second[rows, :]


def in_hbm(x):
    return pltpu.with_memory_space_constraint(jnp.asarray(x), pltpu.HBM)


def params(orders):
    small = 14 if orders <= 512 else 56
    return pltpu.CompilerParams(vmem_limit_bytes=small * 1024 * 1024)


def per_device(weights, offsets, counts, block_ids, m_table, legendre):
    axes = ("blk", "y", "core")
    _, devices, capacity, bins, _ = weights.shape
    slots, degrees, cycles = legendre.shape
    orders = m_table.shape[0]
    groups = devices * capacity
    cycles_here = cycles // devices
    width = bins * cycles
    staged = legendre.size <= 4 * 1024 * 1024
    limits = params(orders)
    hbm = pl.BlockSpec(memory_space=pltpu.HBM)
    vmem = pl.BlockSpec(memory_space=pltpu.VMEM)

    def shaped(*shape, dtype=jnp.bfloat16):
        return jax.ShapeDtypeStruct(shape, dtype)

    rows = slot_rows(orders, slots)
    inner, outer = analysis_tables(orders)
    shapes = [
        shaped(orders, width),
        shaped(bins, groups, BLOCK),
        shaped(4 * SEGMENTS, groups),
        shaped(cycles, groups),
        shaped(1, orders, dtype=jnp.int32),
        shaped(*rows.shape),
        shaped(*inner.shape),
        shaped(*outer.shape),
    ]
    operands = [
        weights.reshape(groups * bins, BLOCK),
        offsets.reshape(groups, BLOCK),
        counts,
        jnp.transpose(block_ids[0]),
        m_table,
        rows,
        inner,
        outer,
    ]
    if staged:
        shapes.append(shaped(*legendre.shape))
        operands.append(legendre)
    theirs, *shared = pl.pallas_call(
        functools.partial(first_kernel, slots, staged),
        in_specs=[hbm] * len(operands),
        out_specs=(vmem,) * len(shapes),
        out_shape=tuple(shapes),
        scratch_shapes=[
            pltpu.VMEM((groups * bins, BLOCK), jnp.bfloat16),
            pltpu.VMEM((groups, BLOCK), jnp.int32),
            pltpu.VMEM((1, devices), jnp.int32),
            pltpu.VMEM((capacity, devices), jnp.int32),
            pltpu.VMEM((orders,), jnp.int32),
            pltpu.VMEM((groups * bins, BLOCK), jnp.float32),
            pltpu.VMEM((width // LANES, orders, LANES), jnp.float32),
            pltpu.SemaphoreType.DMA((len(operands),)),
        ],
        compiler_params=limits,
        name="deposit_and_other_half",
    )(*[in_hbm(x) for x in operands])
    basis = shared.pop() if staged else in_hbm(legendre)

    def swap(x, mask):
        return lax.ppermute(x, axes, [(i, i ^ mask) for i in range(devices)])

    other = swap(theirs, 1)
    mine = pl.pallas_call(
        second_kernel,
        in_specs=[vmem] * 7,
        out_specs=vmem,
        out_shape=shaped(width // LANES, orders, LANES, dtype=jnp.float32),
        compiler_params=limits,
        cost_estimate=pl.CostEstimate(flops=8 * orders * 256 * bins * groups, bytes_accessed=4 * orders * width, transcendentals=0),
        name="own_half",
    )(*shared)

    groups_of_bits = bit_groups(devices)
    stages = len(groups_of_bits)
    gain, order = gain_column(degrees), interleave(cycles, cycles_here)
    blocks = devices // 2
    kernel, inputs = pair_kernel, (mine, other)
    responses = []
    for stage, bits in enumerate(groups_of_bits):
        ways = 1 << len(bits)
        blocks //= ways
        rows_here = blocks * 2 * slots
        kept, *sends = pl.pallas_call(
            kernel,
            in_specs=[vmem] * len(inputs),
            out_specs=(vmem,) * ways,
            out_shape=(shaped(rows_here, width, dtype=jnp.float32),) + (shaped(rows_here, width),) * (ways - 1),
            compiler_params=limits,
            name="pair_sum" if stage == 0 else "merge",
        )(*inputs)
        *sends, basis = lax.optimization_barrier((*sends, basis))
        arrived = [swap(x, (i + 1) << bits[0]) for i, x in enumerate(sends)]
        first, last = (min(slots, slots * 2 * k * (2 * stages - k) // (2 * stages * stages)) for k in (stage, stage + 1))
        count = last - first
        scratch = [] if staged else [pltpu.VMEM((count, degrees, cycles), jnp.bfloat16), pltpu.SemaphoreType.DMA((count,))]
        response = pl.pallas_call(
            functools.partial(response_kernel, first, staged),
            in_specs=[vmem if staged else hbm, vmem, vmem],
            out_specs=vmem,
            out_shape=shaped(count, 2 * cycles, 2 * cycles),
            scratch_shapes=scratch,
            compiler_params=limits,
            cost_estimate=pl.CostEstimate(
                flops=6 * count * degrees * cycles * cycles, bytes_accessed=2 * count * degrees * cycles, transcendentals=0
            ),
            name="response",
        )(basis, gain, order)
        *arrived, response = lax.optimization_barrier((*arrived, response))
        responses.append(response)
        kernel, inputs = functools.partial(merge_kernel, len(arrived)), (kept, *arrived)

    outgoing = pl.pallas_call(
        functools.partial(synthesis_kernel, len(inputs) - 1, len(responses)),
        in_specs=[vmem] * (len(inputs) + len(responses) + 1),
        out_specs=vmem,
        out_shape=shaped(2 * cycles, 128),
        compiler_params=limits,
        name="synthesis",
    )(*inputs, *responses, slot_order(slots, bins))
    outgoing = outgoing.reshape(devices, 2 * cycles_here, 128)
    outgoing, held = lax.optimization_barrier((outgoing, m_table))
    arrived = lax.all_to_all(outgoing, axes, split_axis=0, concat_axis=0, tiled=True)
    arrived = arrived.reshape(2 * cycles, 128)
    if staged:
        arrived = pltpu.with_memory_space_constraint(arrived, pltpu.VMEM)

    lanes = order_lanes(orders)
    constants = [lanes, turn_rows(lanes), inverse_tables(orders)]
    map_shape = shaped(bins, cycles_here, NPHI, dtype=jnp.float32)
    return pl.pallas_call(
        inverse_kernel,
        in_specs=[vmem] + [hbm] * 4,
        out_specs=(vmem, vmem),
        out_shape=(map_shape, map_shape),
        scratch_shapes=[
            pltpu.VMEM((devices, slots), jnp.int32),
            *[pltpu.VMEM(x.shape, x.dtype) for x in constants],
            pltpu.VMEM((2 * cycles, 128), jnp.float32),
            pltpu.SemaphoreType.DMA((3 + NPHI // 2 // constants[-1].shape[1],)),
        ],
        compiler_params=limits,
        name="inverse",
    )(arrived, in_hbm(held.reshape(devices, slots)), *[in_hbm(x) for x in constants])


def solution(mesh):
    blocks, columns = mesh.devices.shape
    fine = Mesh(mesh.devices.reshape(blocks, columns // 2, 2), ("blk", "y", "core"))
    axes = ("blk", "y", "core")
    placed = (
        P(axes, None, None, None, None),
        P(axes, None, None, None),
        P(axes, None),
        P(axes, None, None),
        P(),
        P(axes, None, None),
    )
    return jax.shard_map(
        per_device,
        mesh=fine,
        in_specs=placed,
        out_specs=(P(None, axes, None), P(None, axes, None)),
        check_vma=False,
    )
```

```python
import functools

import jax
import jax.numpy as jnp
import numpy as np
from jax import lax
from jax.experimental import pallas as pl
from jax.experimental.pallas import tpu as pltpu
from jax.sharding import Mesh, PartitionSpec as P

NPHI = 4096
BLOCK = 128
SEGMENTS = NPHI // BLOCK
LANES = 128
CHUNK = 192

NT = (((1,), (1,)), ((), ()))
TN = (((0,), (0,)), ((), ()))


def dot(a, b, dims=(((1,), (0,)), ((), ()))):
    return lax.dot_general(a, b, dims, preferred_element_type=jnp.float32)


def high_low(x):
    high = x.astype(jnp.bfloat16)
    return high, (x - high.astype(jnp.float32)).astype(jnp.bfloat16)


def np_high_low(x):
    high = x.astype(np.float32).astype(jnp.bfloat16)
    return high, (x - high.astype(np.float64)).astype(np.float32).astype(jnp.bfloat16)


def analysis_tables(orders):
    m = np.arange(orders, dtype=np.int64)[:, None]
    p = np.arange(BLOCK, dtype=np.int64)[None, :]
    angle = (m * p % NPHI) * (2 * np.pi / NPHI)
    inner = np.concatenate(np_high_low(np.cos(angle)) + np_high_low(-np.sin(angle)), 1)
    half = np.arange(2 * SEGMENTS, dtype=np.int64)[None, :]
    steps = 2 * BLOCK * (half % SEGMENTS) + half // SEGMENTS
    angle = (m * steps % (2 * NPHI)) * (np.pi / NPHI)
    outer = np.concatenate(np_high_low(np.cos(angle) / NPHI) + np_high_low(-np.sin(angle) / NPHI), 1)
    return inner, outer


def bit_groups(devices):
    bits = list(range(1, devices.bit_length() - 1))
    return [bits[i : i + 2] for i in range(0, len(bits), 2)]


def positions(devices):
    order = [0]
    for group in bit_groups(devices):
        order = [p | (v << group[0]) for p in order for v in range(1 << len(group))]
    return order


def slot_rows(orders, slots):
    out = np.zeros((orders // 2, orders), np.float32)
    for block, position in enumerate(positions(orders // slots)):
        for slot in range(slots):
            out[block * slots + slot, position * slots + slot] = 1
    return out.astype(jnp.bfloat16)


def rolled(x, shift):
    return jnp.concatenate([x[:, shift:], x[:, :shift]], 1)


def exclusive_or(table, me, slots):
    orders = table.shape[1]
    block = lax.div(lax.broadcasted_iota(jnp.int32, table.shape, 1), slots)
    for bit in range((orders // slots).bit_length() - 1):
        shift = slots << bit
        swapped = jnp.where((block >> bit) % 2 == 0, rolled(table, shift), rolled(table, orders - shift))
        table = jnp.where(jnp.broadcast_to((me >> bit) & 1, table.shape) == 1, swapped, table)
    return table


def hot(condition):
    return jnp.where(condition, 1.0, 0.0).astype(jnp.bfloat16)


def twice(x):
    return jnp.concatenate([x, x], 1)


def first_kernel(slots, blocks_here, w_hbm, off_hbm, cnt_hbm, ids_hbm, table_hbm, rows_hbm, inner_hbm, outer_hbm,
                 out_ref, table_ref, rows_ref, inner_ref, outer_ref,
                 w_ref, off_ref, cnt_ref, ids_ref, flat_ref, wide_ref, live_w_ref, live_off_ref, sems):
    pairs = (
        (cnt_hbm, cnt_ref), (ids_hbm, ids_ref), (off_hbm, off_ref), (w_hbm, w_ref),
        (table_hbm, flat_ref), (rows_hbm, rows_ref), (inner_hbm, inner_ref), (outer_hbm, outer_ref),
    )
    copies = [pltpu.make_async_copy(a, b, sems.at[i]) for i, (a, b) in enumerate(pairs)]
    for copy in copies[:4]:
        copy.start()
    groups = off_ref.shape[0]
    capacity, devices = ids_ref.shape
    bins, live, _ = live_w_ref.shape
    pack = 16
    key_tiles = (out_ref.shape[0] - bins * live) // pack

    owner = lax.div(lax.broadcasted_iota(jnp.int32, (devices, groups), 1), capacity)
    source = lax.broadcasted_iota(jnp.int32, (devices, groups), 0)
    member = lax.rem(lax.broadcasted_iota(jnp.int32, (capacity, groups), 1), capacity)
    own_row = lax.broadcasted_iota(jnp.int32, (capacity, groups), 0) == member
    for copy in copies[:2]:
        copy.wait()
    counts = jnp.broadcast_to(cnt_ref[...].astype(jnp.float32), (8, devices)).astype(jnp.bfloat16)
    count = dot(counts, hot(source == owner))[0:1, :]
    before = dot(counts, hot(source < owner))[0:1, :]
    number = member[0:1, :].astype(jnp.float32)
    place = jnp.where(number < count, before + number, -1.0).astype(jnp.int32)
    packing = hot(lax.broadcasted_iota(jnp.int32, (key_tiles * LANES, groups), 0) == place)

    ids = dot(ids_ref[...].astype(jnp.float32).astype(jnp.bfloat16), hot(source == owner))
    ids = jnp.sum(jnp.where(own_row, ids, 0.0), axis=0, keepdims=True)
    block = ids.astype(jnp.int32) + owner[0:1, :] * blocks_here
    cycle = lax.div(block, SEGMENTS)
    phase = lax.rem(cycle, 2) * SEGMENTS + lax.rem(block, SEGMENTS)
    row = lax.broadcasted_iota(jnp.int32, (pack, groups), 0)
    keys = jnp.where(row == 0, lax.div(cycle, 16), jnp.where(row == 1, lax.rem(cycle, 16), phase))
    keys = dot(keys.astype(jnp.float32).astype(jnp.bfloat16), packing, NT).astype(jnp.bfloat16)
    for tile in range(key_tiles):
        out_ref[bins * live + tile * pack : bins * live + (tile + 1) * pack, :] = keys[:, tile * LANES : (tile + 1) * LANES]

    for copy in copies[2:4]:
        copy.wait()
    for copy in copies[4:]:
        copy.start()
    packing = packing[:live, :]
    live_off_ref[...] = dot(packing, off_ref[...].astype(jnp.float32).astype(jnp.bfloat16))
    wide_ref[...] = w_ref[...].astype(jnp.float32)
    for b in range(bins):
        live_w_ref[b] = dot(packing, wide_ref[pl.ds(b, groups, stride=bins), :].astype(jnp.bfloat16)).astype(jnp.bfloat16)

    pixel = lax.broadcasted_iota(jnp.int32, (pack, BLOCK), 0)
    pixels = [(pixel + pack * k).astype(jnp.float32).astype(jnp.bfloat16) for k in range(BLOCK // pack)]
    alone = [hot(pixel == i) for i in range(pack)]
    one = jnp.ones((pack, BLOCK), jnp.bfloat16)
    zero = jnp.zeros((pack, BLOCK), jnp.bfloat16)

    def deposit(step, carry):
        start = pl.multiple_of(step * pack, pack)
        weights = [live_w_ref[b, pl.ds(start, pack), :] for b in range(bins)]
        left, right = [], []
        for i in range(pack):
            left.append(jnp.concatenate([w * alone[i] for w in weights], 0))
            at = jnp.broadcast_to(live_off_ref[pl.ds(start + i, 1), :], (pack, BLOCK)).astype(jnp.bfloat16)
            right.append(jnp.concatenate([jnp.where(at == x, one, zero) for x in pixels], 0))
        out = dot(jnp.concatenate(left, 1), jnp.concatenate(right, 1), NT).astype(jnp.bfloat16)
        for b in range(bins):
            out_ref[pl.ds(pl.multiple_of(b * live + start, pack), pack), :] = out[b * pack : (b + 1) * pack, :]
        return carry

    lax.fori_loop(0, live // pack, deposit, 0, unroll=9)
    for copy in copies[4:]:
        copy.wait()
    me = lax.axis_index("blk")
    for axis in ("y", "core"):
        me = me * lax.axis_size(axis) + lax.axis_index(axis)
    table_ref[...] = exclusive_or(flat_ref[...].reshape(table_ref.shape), me, slots)


def add_modes(bins, groups, cycles, groups_ref, inner_ref, outer_ref, add):
    pack = 16
    keys = groups_ref[bins * groups :, :].astype(jnp.float32)
    keys = jnp.concatenate([keys[i * pack : (i + 1) * pack, :] for i in range(keys.shape[0] // pack)], 1)
    cycle = (keys[0:1, :groups] * 16.0 + keys[1:2, :groups]).astype(jnp.int32)
    phase = keys[2:3, :groups].astype(jnp.int32)
    cycle_hot = hot(lax.broadcasted_iota(jnp.int32, (cycles, groups), 0) == cycle)
    half_hot = hot(lax.broadcasted_iota(jnp.int32, (2 * SEGMENTS, groups), 0) == phase)
    phase_hot = jnp.concatenate([half_hot, half_hot], 0)
    deposits = [twice(groups_ref[b * groups : (b + 1) * groups, :]) for b in range(bins)]
    for start in range(0, inner_ref.shape[0], 2 * CHUNK):
        rows = slice(start, start + 2 * CHUNK)
        outer = dot(outer_ref[rows, :], phase_hot)
        outer_cos, outer_sin = outer[:CHUNK, :], outer[CHUNK:, :]
        for b, deposit in enumerate(deposits):
            inner = dot(inner_ref[rows, :], deposit, NT)
            inner_cos, inner_sin = inner[:CHUNK, :], inner[CHUNK:, :]
            real = inner_cos * outer_cos - inner_sin * outer_sin
            imag = inner_cos * outer_sin + inner_sin * outer_cos
            both = dot(jnp.concatenate([real, imag], 0).astype(jnp.bfloat16), cycle_hot, NT)
            for part in range(2):
                value = both[part * CHUNK : (part + 1) * CHUNK, :]
                for tile in range(cycles // LANES):
                    add(b * (cycles // LANES) + tile, start + part, value[:, tile * LANES : (tile + 1) * LANES])


def own_kernel(bins, groups, cycles, groups_ref, table_ref, rows_ref, inner_ref, outer_ref, out_ref, inner_out, outer_out):
    count, orders = rows_ref.shape
    held = hot(lax.broadcasted_iota(jnp.int32, (orders, orders), 0) == table_ref[...])
    for start in range(0, count, CHUNK):
        pick = dot(rows_ref[start : start + CHUNK, :], held, NT).astype(jnp.bfloat16)
        inner = dot(pick, inner_ref[...]).astype(jnp.bfloat16)
        outer = dot(pick, outer_ref[...]).astype(jnp.bfloat16)
        for part in range(2):
            rows = slice(2 * start + part * CHUNK, 2 * start + (part + 1) * CHUNK)
            inner_out[rows, :] = inner[:, part * 2 * BLOCK : (part + 1) * 2 * BLOCK]
            outer_out[rows, :] = outer[:, part * BLOCK : (part + 1) * BLOCK]

    def add(tile, first, value):
        out_ref.at[tile][pl.ds(first, value.shape[0], stride=2), :] = value

    add_modes(bins, groups, cycles, groups_ref, inner_out, outer_out, add)


def split_sum(parts, tile, keep_ref, send_refs):
    rows = keep_ref.shape[0]
    lanes = slice(tile * LANES, (tile + 1) * LANES)
    for i, out_ref in enumerate((keep_ref, *send_refs)):
        value = sum(part(slice(i * rows, (i + 1) * rows), lanes) for part in parts)
        out_ref[:, lanes] = value.astype(out_ref.dtype)


def other_kernel(bins, groups, cycles, groups_ref, inner_ref, outer_ref, own_ref, keep_ref, *refs):
    *send_refs, other_ref = refs

    def add(tile, first, value):
        other_ref.at[tile][pl.ds(first, value.shape[0], stride=2), :] = value

    add_modes(bins, groups, cycles, groups_ref, inner_ref, outer_ref, add)
    for tile in range(own_ref.shape[0]):
        parts = (lambda rows, lanes: own_ref[tile, rows, :], lambda rows, lanes: other_ref[tile, rows, :])
        split_sum(parts, tile, keep_ref, send_refs)


def merge_kernel(count, kept_ref, *refs):
    arrived, outs = refs[:count], refs[count:]
    for tile in range(kept_ref.shape[1] // LANES):
        parts = [lambda rows, lanes, ref=ref: ref[rows, lanes].astype(jnp.float32) for ref in (kept_ref, *arrived)]
        split_sum(parts, tile, outs[0], outs[1:])


def gain_column(degrees):
    l = np.arange(degrees, dtype=np.float32)
    return np.where(l > 0.5, np.float32(-20000.0) / np.maximum(l * (l + 1), np.float32(1)), np.float32(0)).astype(np.float32)[:, None] * np.ones((1, BLOCK), np.float32)


def interleave(cycles, cycles_here):
    out = np.zeros((2 * cycles, 2 * cycles), np.float32)
    for f in range(2):
        for c in range(cycles):
            out[f * cycles + c, (c // cycles_here * 2 + f) * cycles_here + c % cycles_here] = 1
    return out.astype(jnp.bfloat16)


def response_kernel(start, from_hbm, rest, legendre_ref, gain_ref, order_ref, out_ref, *refs):
    count = out_ref.shape[0]
    copies = []
    if from_hbm:
        source, (*rest_refs, legendre_ref, sems) = legendre_ref, refs
        copies = [pltpu.make_async_copy(source.at[start + i], legendre_ref.at[i], sems.at[i]) for i in range(count)]
        for ref in rest_refs:
            copies.append(pltpu.make_async_copy(source.at[pl.ds(start + count, rest)], ref, sems.at[count]))
        for copy in copies:
            copy.start()
        start = 0
    for slot in range(count):
        if from_hbm:
            copies[slot].wait()
        basis = legendre_ref[start + slot]
        cycles = basis.shape[1]
        gain = jnp.concatenate([gain_ref[...]] * (cycles // BLOCK), 1)
        gained = (basis.astype(jnp.float32) * gain).astype(jnp.bfloat16)
        high, low = high_low(dot(basis, jnp.concatenate([basis, gained], 1), TN))
        out_ref[slot, :cycles, :] = dot(high, order_ref[...]).astype(jnp.bfloat16)
        out_ref[slot, cycles:, :] = dot(low, order_ref[...]).astype(jnp.bfloat16)
    for copy in copies[count:]:
        copy.wait()


def slot_order(slots, bins):
    out = np.zeros((slots * 2 * bins, slots * 2 * bins), np.float32)
    for b in range(bins):
        for c in range(2):
            for t in range(slots):
                out[(t * 2 + c) * bins + b, (b * slots + t) * 2 + c] = 1
    return out.astype(jnp.bfloat16)


def synthesis_kernel(arrivals, pieces, kept_ref, *refs):
    partials, refs = refs[:arrivals], refs[arrivals:]
    response_refs, (order_ref, out_ref) = refs[:pieces], refs[pieces:]
    cycles = response_refs[0].shape[1] // 2
    bins = kept_ref.shape[1] // cycles
    slots = kept_ref.shape[0] // 2
    responses = [ref.at[i] for ref in response_refs for i in range(ref.shape[0])]
    total = kept_ref[...]
    for ref in partials:
        total = total + ref[...].astype(jnp.float32)
    modes = jnp.concatenate([total[:, b * cycles : (b + 1) * cycles] for b in range(bins)], 0)
    high, low = high_low(modes)
    high = dot(order_ref[...], high)
    low = dot(order_ref[...], low)
    per_slot = 2 * bins
    parts = []
    for t in range(slots):
        rows = slice(t * per_slot, (t + 1) * per_slot)
        left = jnp.concatenate([high[rows, :], low[rows, :]], 0).astype(jnp.bfloat16)
        part = dot(twice(left), responses[t][...])
        parts.append(part[:per_slot, :] + part[per_slot:, :])
    parts.append(jnp.zeros((128 - slots * per_slot, 2 * cycles), jnp.float32))
    result = jnp.concatenate(parts, 0)
    out_ref[...] = jnp.transpose(result).astype(jnp.bfloat16)


def order_classes(orders):
    return [np.arange(0, orders, 4), np.arange(2, orders, 4), np.arange(1, orders, 2)]


def inverse_tables(orders):
    quarter = NPHI // 4
    k = np.arange(quarter, dtype=np.int64)[None, :]
    rows = []
    for m in order_classes(orders):
        angle = (m[:, None] * k % NPHI) * (2 * np.pi / NPHI)
        rows += [np.cos(angle), -np.sin(angle)]
    return np.concatenate(np.split(np.concatenate(rows), quarter // 512, axis=1)).astype(np.float32).astype(jnp.bfloat16)


def padded(count):
    return -(-count // LANES) * LANES


def order_lanes(orders):
    out = []
    for m in order_classes(orders):
        out.append(np.concatenate([m, np.full(padded(len(m)) - len(m), -1)]))
    return np.concatenate(out).astype(np.int32)[None, :]


def turn_rows(order_row):
    m = np.maximum(order_row[0], 0).astype(np.float64)
    weight = np.where(order_row[0] == 0, 1.0, 2.0)
    sign = np.where(order_row[0] % 4 == 3, 1.0, -1.0)
    parts = np_high_low(np.cos(np.pi * m / NPHI) * weight) + np_high_low(np.sin(np.pi * m / NPHI) * weight)
    parts = parts + (weight.astype(jnp.bfloat16), sign.astype(jnp.bfloat16))
    return np.stack(parts + (np.zeros_like(parts[0]),) * 10)


def part_rows(part, bins, cycles_here):
    shape = (2 * bins * cycles_here, 4 * bins * cycles_here)
    row = lax.broadcasted_iota(jnp.int32, shape, 0)
    column = lax.broadcasted_iota(jnp.int32, shape, 1)
    cycle = lax.rem(row, cycles_here)
    bin_number = lax.rem(lax.div(row, cycles_here), bins)
    filter_number = lax.div(row, cycles_here * bins)
    return hot(column == ((filter_number * cycles_here + cycle) * 2 + part) * bins + bin_number)


def inverse_kernel(arrived_ref, slots_hbm, turn_hbm, table_hbm, kappa_hbm, potential_hbm,
                   slots_ref, turn_ref, table_ref, wide_ref, kappa_ref, potential_ref, sems, out_sems):
    copies = [
        pltpu.make_async_copy(a, b, sems.at[i])
        for i, (a, b) in enumerate(((slots_hbm, slots_ref), (turn_hbm, turn_ref)))
    ]
    quarter = NPHI // 4
    chunk = table_ref.shape[1]
    chunks = quarter // chunk
    part = table_ref.shape[0] // chunks
    for i in range(chunks):
        rows = pl.ds(i * part, part)
        copies.append(pltpu.make_async_copy(table_hbm.at[rows], table_ref.at[rows], sems.at[2 + i]))
    for copy in copies:
        copy.start()
    devices, slots = slots_ref.shape
    bins, cycles_here, _ = kappa_ref.shape
    order_count = part // 2
    per_slot = 2 * bins
    per_source = 2 * cycles_here
    wide_ref[...] = arrived_ref[...].astype(jnp.float32)
    turned = [jnp.transpose(wide_ref[pl.ds(i, devices, stride=per_source), :]) for i in range(per_source)]
    few, many = order_count // 4, order_count // 2
    starts = [0, padded(few), 2 * padded(few)]
    lane = lax.broadcasted_iota(jnp.int32, (1, turn_ref.shape[1]), 1)
    orders = jnp.where(lane < few, 4 * lane, -1)
    within = lane - starts[1]
    orders = jnp.where((within >= 0) & (within < few), 4 * within + 2, orders)
    within = lane - starts[2]
    orders = jnp.where((within >= 0) & (within < many), 2 * within + 1, orders)
    for copy in copies[:2]:
        copy.wait()
    lefts, picks = [], []
    for t in range(slots):
        lefts.append(jnp.concatenate([x[t * per_slot : (t + 1) * per_slot, :] for x in turned], 0))
        picks.append(hot(slots_ref[:, t : t + 1] == orders))
    spectrum = dot(jnp.concatenate(lefts, 1).astype(jnp.bfloat16), jnp.concatenate(picks, 0))
    spectrum = spectrum.astype(jnp.bfloat16)
    real_in = dot(part_rows(0, bins, cycles_here), spectrum)
    imag_in = dot(part_rows(1, bins, cycles_here), spectrum)
    turn = turn_ref[...].astype(jnp.float32)
    odd = lax.rem(lax.rem(lax.broadcasted_iota(jnp.int32, real_in.shape, 0), cycles_here), 2) == 1
    turn_cos = jnp.where(odd, turn[0:1, :] + turn[1:2, :], turn[4:5, :])
    turn_sin = jnp.where(odd, turn[2:3, :] + turn[3:4, :], 0.0)
    real = real_in * turn_cos - imag_in * turn_sin
    imag = real_in * turn_sin + imag_in * turn_cos
    sign = turn[5:6, starts[2] :]
    count = real.shape[0]
    lefts = []
    for index, start in enumerate(starts):
        lanes = slice(start, start + (few if index < 2 else many))
        cos_rows, sin_rows = [real[:, lanes]], [imag[:, lanes]]
        if index == 2:
            cos_rows.append(imag[:, lanes] * sign[:, :many])
            sin_rows.append(-real[:, lanes] * sign[:, :many])
        for rows in (cos_rows, sin_rows):
            lefts.append(jnp.concatenate([y for x in rows for y in high_low(x)], 0))
    results = []
    for index in range(chunks):
        copies[2 + index].wait()
        row = index * part
        sums = []
        for at in range(3):
            height = few if at < 2 else many
            both = dot(lefts[2 * at], table_ref[row : row + height, :])
            both = both + dot(lefts[2 * at + 1], table_ref[row + height : row + 2 * height, :])
            row += 2 * height
            sums += [both[i : i + count, :] + both[i + count : i + 2 * count, :] for i in range(0, both.shape[0], 2 * count)]
        even, other = sums[0] + sums[1], sums[0] - sums[1]
        values = (even + sums[2], other + sums[3], even - sums[2], other - sums[3])
        for j, value in enumerate(values):
            lanes = pl.ds(j * quarter + index * chunk, chunk)
            for f, (out_ref, out_hbm) in enumerate(((kappa_ref, kappa_hbm), (potential_ref, potential_hbm))):
                for b in range(bins):
                    at = (f * bins + b) * cycles_here
                    out_ref[b, :, lanes] = value[at : at + cycles_here, :]
                copy = pltpu.make_async_copy(out_ref.at[:, :, lanes], out_hbm.at[:, :, lanes], out_sems.at[len(results)])
                copy.start()
                results.append(copy)
    for copy in results:
        copy.wait()


def in_hbm(x):
    return pltpu.with_memory_space_constraint(jnp.asarray(x), pltpu.HBM)


def params(orders):
    small = 14 if orders <= 512 else 56
    return pltpu.CompilerParams(vmem_limit_bytes=small * 1024 * 1024)


def per_device(weights, offsets, counts, block_ids, m_table, legendre):
    axes = ("blk", "y", "core")
    _, devices, capacity, bins, _ = weights.shape
    slots, degrees, cycles = legendre.shape
    orders = m_table.shape[0]
    groups = devices * capacity
    cycles_here = cycles // devices
    width = bins * cycles
    staged = legendre.size <= 4 * 1024 * 1024
    limits = params(orders)
    hbm = pl.BlockSpec(memory_space=pltpu.HBM)
    vmem = pl.BlockSpec(memory_space=pltpu.VMEM)

    def shaped(*shape, dtype=jnp.bfloat16):
        return jax.ShapeDtypeStruct(shape, dtype)

    rows = slot_rows(orders, slots)
    inner, outer = analysis_tables(orders)
    live = (capacity + 1) * devices // 2
    key_rows = -(-live // LANES) * 16
    shapes = [
        shaped(bins * live + key_rows, BLOCK),
        shaped(1, orders, dtype=jnp.int32),
        shaped(*rows.shape),
        shaped(*inner.shape),
        shaped(*outer.shape),
    ]
    operands = [
        weights.reshape(groups * bins, BLOCK),
        offsets.reshape(groups, BLOCK),
        counts,
        jnp.transpose(block_ids[0]),
        m_table,
        rows,
        inner,
        outer,
    ]
    deposits, *shared = pl.pallas_call(
        functools.partial(first_kernel, slots, cycles_here * SEGMENTS),
        in_specs=[hbm] * len(operands),
        out_specs=(vmem,) * len(shapes),
        out_shape=tuple(shapes),
        scratch_shapes=[
            pltpu.VMEM((groups * bins, BLOCK), jnp.bfloat16),
            pltpu.VMEM((groups, BLOCK), jnp.int32),
            pltpu.VMEM((1, devices), jnp.int32),
            pltpu.VMEM((capacity, devices), jnp.int32),
            pltpu.VMEM((orders,), jnp.int32),
            pltpu.VMEM((groups * bins, BLOCK), jnp.float32),
            pltpu.VMEM((bins, live, BLOCK), jnp.bfloat16),
            pltpu.VMEM((live, BLOCK), jnp.float32),
            pltpu.SemaphoreType.DMA((len(operands),)),
        ],
        compiler_params=limits,
        name="deposit",
    )(*[in_hbm(x) for x in operands])
    basis, moved = legendre, 0

    def swap(x, mask):
        return lax.ppermute(x, axes, [(i, i ^ mask) for i in range(devices)])

    other = swap(deposits, 1)
    cost = pl.CostEstimate(flops=8 * orders * 256 * bins * live, bytes_accessed=4 * orders * width, transcendentals=0)
    modes_shape = (width // LANES, orders, LANES)
    own, own_inner, own_outer = pl.pallas_call(
        functools.partial(own_kernel, bins, live, cycles),
        in_specs=[vmem] * 5,
        out_specs=(vmem,) * 3,
        out_shape=(
            shaped(*modes_shape, dtype=jnp.float32),
            shaped(orders, inner.shape[1] // 2),
            shaped(orders, outer.shape[1] // 2),
        ),
        compiler_params=limits,
        cost_estimate=cost,
        name="own_groups",
    )(deposits, *shared)

    groups_of_bits = bit_groups(devices)
    stages = len(groups_of_bits)
    gain, order = gain_column(degrees), interleave(cycles, cycles_here)
    blocks = devices // 2
    kernel, inputs = functools.partial(other_kernel, bins, live, cycles), (other, own_inner, own_outer, own)
    scratch = [pltpu.VMEM(modes_shape, jnp.float32)]
    responses = []
    for stage, bits in enumerate(groups_of_bits):
        ways = 1 << len(bits)
        blocks //= ways
        rows_here = blocks * 2 * slots
        kept, *sends = pl.pallas_call(
            kernel,
            in_specs=[vmem] * len(inputs),
            out_specs=(vmem,) * ways,
            out_shape=(shaped(rows_here, width, dtype=jnp.float32),) + (shaped(rows_here, width),) * (ways - 1),
            scratch_shapes=scratch,
            compiler_params=limits,
            name="merge" if stage else "other_groups",
        )(*inputs)
        *sends, basis = lax.optimization_barrier((*sends, basis))
        if stage == 0 or not staged:
            basis = in_hbm(basis)
        arrived = [swap(x, (i + 1) << bits[0]) for i, x in reversed(list(enumerate(sends)))]
        first, last = (min(slots, slots * 2 * k * (2 * stages - k) // (2 * stages * stages)) for k in (stage, stage + 1))
        count = last - first
        from_hbm = stage == 0 or not staged
        rest = slots - last if stage == 0 and staged else 0
        scratch = [pltpu.VMEM((count, degrees, cycles), jnp.bfloat16), pltpu.SemaphoreType.DMA((count + 1,))]
        response, *rests = pl.pallas_call(
            functools.partial(response_kernel, first if from_hbm else first - moved, from_hbm, rest),
            in_specs=[hbm if from_hbm else vmem, vmem, vmem],
            out_specs=(vmem,) * (2 if rest else 1),
            out_shape=(shaped(count, 2 * cycles, 2 * cycles),) + ((shaped(rest, degrees, cycles),) if rest else ()),
            scratch_shapes=scratch if from_hbm else [],
            compiler_params=limits,
            cost_estimate=pl.CostEstimate(
                flops=6 * count * degrees * cycles * cycles, bytes_accessed=2 * count * degrees * cycles, transcendentals=0
            ),
            name="response",
        )(basis, gain, order)
        if rests:
            basis, moved = rests[0], last
        *arrived, response = lax.optimization_barrier((*arrived, response))
        responses.append(response)
        kernel, inputs, scratch = functools.partial(merge_kernel, len(arrived)), (kept, *arrived), []

    outgoing = pl.pallas_call(
        functools.partial(synthesis_kernel, len(inputs) - 1, len(responses)),
        in_specs=[vmem] * (len(inputs) + len(responses) + 1),
        out_specs=vmem,
        out_shape=shaped(2 * cycles, 128),
        compiler_params=limits,
        name="synthesis",
    )(*inputs, *responses, slot_order(slots, bins))
    outgoing = outgoing.reshape(devices, 2 * cycles_here, 128)
    outgoing, held = lax.optimization_barrier((outgoing, m_table))
    arrived = lax.all_to_all(outgoing, axes, split_axis=0, concat_axis=0, tiled=True)
    arrived = arrived.reshape(2 * cycles, 128)
    if staged:
        arrived = pltpu.with_memory_space_constraint(arrived, pltpu.VMEM)

    lanes = order_lanes(orders)
    constants = [turn_rows(lanes), inverse_tables(orders)]
    chunks = NPHI // 4 // constants[-1].shape[1]
    map_shape = shaped(bins, cycles_here, NPHI, dtype=jnp.float32)
    return pl.pallas_call(
        inverse_kernel,
        in_specs=[vmem] + [hbm] * 3,
        out_specs=(hbm, hbm),
        out_shape=(map_shape, map_shape),
        scratch_shapes=[
            pltpu.VMEM((devices, slots), jnp.int32),
            *[pltpu.VMEM(x.shape, x.dtype) for x in constants],
            pltpu.VMEM((2 * cycles, 128), jnp.float32),
            pltpu.VMEM(map_shape.shape, jnp.float32),
            pltpu.VMEM(map_shape.shape, jnp.float32),
            pltpu.SemaphoreType.DMA((2 + chunks,)),
            pltpu.SemaphoreType.DMA((8 * chunks,)),
        ],
        compiler_params=limits,
        name="inverse",
    )(arrived, in_hbm(held.reshape(devices, slots)), *[in_hbm(x) for x in constants])


def solution(mesh):
    blocks, columns = mesh.devices.shape
    fine = Mesh(mesh.devices.reshape(blocks, columns // 2, 2), ("blk", "y", "core"))
    axes = ("blk", "y", "core")
    placed = (
        P(axes, None, None, None, None),
        P(axes, None, None, None),
        P(axes, None),
        P(axes, None, None),
        P(),
        P(axes, None, None),
    )
    return jax.shard_map(
        per_device,
        mesh=fine,
        in_specs=placed,
        out_specs=(P(None, axes, None), P(None, axes, None)),
        check_vma=False,
    )
```

```python
import functools

import jax
import jax.numpy as jnp
import numpy as np
from jax import lax
from jax.experimental import pallas as pl
from jax.experimental.pallas import tpu as pltpu
from jax.sharding import Mesh, PartitionSpec as P

NPHI = 4096
BLOCK = 128
SEGMENTS = NPHI // BLOCK
LANES = 128
CHUNK = 192

NT = (((1,), (1,)), ((), ()))
TN = (((0,), (0,)), ((), ()))


def dot(a, b, dims=(((1,), (0,)), ((), ()))):
    return lax.dot_general(a, b, dims, preferred_element_type=jnp.float32)


def high_low(x):
    high = x.astype(jnp.bfloat16)
    return high, (x - high.astype(jnp.float32)).astype(jnp.bfloat16)


def np_high_low(x):
    high = x.astype(np.float32).astype(jnp.bfloat16)
    return high, (x - high.astype(np.float64)).astype(np.float32).astype(jnp.bfloat16)


def analysis_tables(orders):
    m = np.arange(orders, dtype=np.int64)[:, None]
    p = np.arange(BLOCK, dtype=np.int64)[None, :]
    angle = (m * p % NPHI) * (2 * np.pi / NPHI)
    inner = np.concatenate(np_high_low(np.cos(angle)) + np_high_low(-np.sin(angle)), 1)
    half = np.arange(2 * SEGMENTS, dtype=np.int64)[None, :]
    steps = 2 * BLOCK * (half % SEGMENTS) + half // SEGMENTS
    angle = (m * steps % (2 * NPHI)) * (np.pi / NPHI)
    outer = np.concatenate(np_high_low(np.cos(angle) / NPHI) + np_high_low(-np.sin(angle) / NPHI), 1)
    return inner, outer


def bit_groups(devices):
    bits = list(range(1, devices.bit_length() - 1))
    return [bits[i : i + 2] for i in range(0, len(bits), 2)]


def positions(devices):
    order = [0]
    for group in bit_groups(devices):
        order = [p | (v << group[0]) for p in order for v in range(1 << len(group))]
    return order


def slot_rows(orders, slots):
    out = np.zeros((orders // 2, orders), np.float32)
    for block, position in enumerate(positions(orders // slots)):
        for slot in range(slots):
            out[block * slots + slot, position * slots + slot] = 1
    return out.astype(jnp.bfloat16)


def rolled(x, shift):
    return jnp.concatenate([x[:, shift:], x[:, :shift]], 1)


def exclusive_or(table, me, slots):
    orders = table.shape[1]
    block = lax.div(lax.broadcasted_iota(jnp.int32, table.shape, 1), slots)
    for bit in range((orders // slots).bit_length() - 1):
        shift = slots << bit
        swapped = jnp.where((block >> bit) % 2 == 0, rolled(table, shift), rolled(table, orders - shift))
        table = jnp.where(jnp.broadcast_to((me >> bit) & 1, table.shape) == 1, swapped, table)
    return table


def hot(condition):
    return jnp.where(condition, 1.0, 0.0).astype(jnp.bfloat16)


def twice(x):
    return jnp.concatenate([x, x], 1)


def first_kernel(slots, blocks_here, staged, w_hbm, off_hbm, cnt_hbm, ids_hbm, table_hbm, rows_hbm, inner_hbm, outer_hbm, *refs):
    if staged:
        legendre_hbm, *refs = refs
    out_ref, table_ref, rows_ref, inner_ref, outer_ref, *refs = refs
    if staged:
        legendre_ref, *refs = refs
    w_ref, off_ref, cnt_ref, ids_ref, flat_ref, wide_ref, live_w_ref, live_off_ref, sems = refs
    pairs = (
        (cnt_hbm, cnt_ref), (ids_hbm, ids_ref), (off_hbm, off_ref), (w_hbm, w_ref),
        (table_hbm, flat_ref), (rows_hbm, rows_ref), (inner_hbm, inner_ref), (outer_hbm, outer_ref),
    )
    if staged:
        pairs = pairs + ((legendre_hbm.at[pl.ds(0, staged)], legendre_ref),)
    copies = [pltpu.make_async_copy(a, b, sems.at[i]) for i, (a, b) in enumerate(pairs)]
    for copy in copies[:4]:
        copy.start()
    groups = off_ref.shape[0]
    capacity, devices = ids_ref.shape
    bins, live, _ = live_w_ref.shape
    pack = 16
    key_tiles = (out_ref.shape[0] - bins * live) // pack

    owner = lax.div(lax.broadcasted_iota(jnp.int32, (devices, groups), 1), capacity)
    source = lax.broadcasted_iota(jnp.int32, (devices, groups), 0)
    member = lax.rem(lax.broadcasted_iota(jnp.int32, (capacity, groups), 1), capacity)
    own_row = lax.broadcasted_iota(jnp.int32, (capacity, groups), 0) == member
    for copy in copies[:2]:
        copy.wait()
    counts = jnp.broadcast_to(cnt_ref[...].astype(jnp.float32), (8, devices)).astype(jnp.bfloat16)
    count = dot(counts, hot(source == owner))[0:1, :]
    before = dot(counts, hot(source < owner))[0:1, :]
    number = member[0:1, :].astype(jnp.float32)
    place = jnp.where(number < count, before + number, -1.0).astype(jnp.int32)
    packing = hot(lax.broadcasted_iota(jnp.int32, (key_tiles * LANES, groups), 0) == place)

    ids = dot(ids_ref[...].astype(jnp.float32).astype(jnp.bfloat16), hot(source == owner))
    ids = jnp.sum(jnp.where(own_row, ids, 0.0), axis=0, keepdims=True)
    block = ids.astype(jnp.int32) + owner[0:1, :] * blocks_here
    cycle = lax.div(block, SEGMENTS)
    phase = lax.rem(cycle, 2) * SEGMENTS + lax.rem(block, SEGMENTS)
    row = lax.broadcasted_iota(jnp.int32, (pack, groups), 0)
    keys = jnp.where(row == 0, lax.div(cycle, 16), jnp.where(row == 1, lax.rem(cycle, 16), phase))
    keys = dot(keys.astype(jnp.float32).astype(jnp.bfloat16), packing, NT).astype(jnp.bfloat16)
    for tile in range(key_tiles):
        out_ref[bins * live + tile * pack : bins * live + (tile + 1) * pack, :] = keys[:, tile * LANES : (tile + 1) * LANES]

    for copy in copies[2:4]:
        copy.wait()
    for copy in copies[4:]:
        copy.start()
    packing = packing[:live, :]
    live_off_ref[...] = dot(packing, off_ref[...].astype(jnp.float32).astype(jnp.bfloat16))
    wide_ref[...] = w_ref[...].astype(jnp.float32)
    for b in range(bins):
        live_w_ref[b] = dot(packing, wide_ref[pl.ds(b, groups, stride=bins), :].astype(jnp.bfloat16)).astype(jnp.bfloat16)

    pixel = lax.broadcasted_iota(jnp.int32, (pack, BLOCK), 0)
    pixels = [(pixel + pack * k).astype(jnp.float32).astype(jnp.bfloat16) for k in range(BLOCK // pack)]
    alone = [hot(pixel == i) for i in range(pack)]
    one = jnp.ones((pack, BLOCK), jnp.bfloat16)
    zero = jnp.zeros((pack, BLOCK), jnp.bfloat16)

    def deposit(step, carry):
        start = pl.multiple_of(step * pack, pack)
        weights = [live_w_ref[b, pl.ds(start, pack), :] for b in range(bins)]
        left, right = [], []
        for i in range(pack):
            left.append(jnp.concatenate([w * alone[i] for w in weights], 0))
            at = jnp.broadcast_to(live_off_ref[pl.ds(start + i, 1), :], (pack, BLOCK)).astype(jnp.bfloat16)
            right.append(jnp.concatenate([jnp.where(at == x, one, zero) for x in pixels], 0))
        out = dot(jnp.concatenate(left, 1), jnp.concatenate(right, 1), NT).astype(jnp.bfloat16)
        for b in range(bins):
            out_ref[pl.ds(pl.multiple_of(b * live + start, pack), pack), :] = out[b * pack : (b + 1) * pack, :]
        return carry

    lax.fori_loop(0, live // pack, deposit, 0, unroll=9)
    for copy in copies[4:8]:
        copy.wait()
    me = lax.axis_index("blk")
    for axis in ("y", "core"):
        me = me * lax.axis_size(axis) + lax.axis_index(axis)
    table_ref[...] = exclusive_or(flat_ref[...].reshape(table_ref.shape), me, slots)
    for copy in copies[8:]:
        copy.wait()


def add_modes(bins, groups, cycles, groups_ref, inner_ref, outer_ref, add):
    pack = 16
    keys = groups_ref[bins * groups :, :].astype(jnp.float32)
    keys = jnp.concatenate([keys[i * pack : (i + 1) * pack, :] for i in range(keys.shape[0] // pack)], 1)
    cycle = (keys[0:1, :groups] * 16.0 + keys[1:2, :groups]).astype(jnp.int32)
    phase = keys[2:3, :groups].astype(jnp.int32)
    cycle_hot = hot(lax.broadcasted_iota(jnp.int32, (cycles, groups), 0) == cycle)
    half_hot = hot(lax.broadcasted_iota(jnp.int32, (2 * SEGMENTS, groups), 0) == phase)
    phase_hot = jnp.concatenate([half_hot, half_hot], 0)
    deposits = [twice(groups_ref[b * groups : (b + 1) * groups, :]) for b in range(bins)]
    for start in range(0, inner_ref.shape[0], 2 * CHUNK):
        rows = slice(start, start + 2 * CHUNK)
        outer = dot(outer_ref[rows, :], phase_hot)
        outer_cos, outer_sin = outer[:CHUNK, :], outer[CHUNK:, :]
        for b, deposit in enumerate(deposits):
            inner = dot(inner_ref[rows, :], deposit, NT)
            inner_cos, inner_sin = inner[:CHUNK, :], inner[CHUNK:, :]
            real = inner_cos * outer_cos - inner_sin * outer_sin
            imag = inner_cos * outer_sin + inner_sin * outer_cos
            both = dot(jnp.concatenate([real, imag], 0).astype(jnp.bfloat16), cycle_hot, NT)
            for part in range(2):
                value = both[part * CHUNK : (part + 1) * CHUNK, :]
                for tile in range(cycles // LANES):
                    add(b * (cycles // LANES) + tile, start + part, value[:, tile * LANES : (tile + 1) * LANES])


def own_kernel(bins, groups, cycles, groups_ref, table_ref, rows_ref, inner_ref, outer_ref, out_ref, inner_out, outer_out):
    count, orders = rows_ref.shape
    held = hot(lax.broadcasted_iota(jnp.int32, (orders, orders), 0) == table_ref[...])
    for start in range(0, count, CHUNK):
        pick = dot(rows_ref[start : start + CHUNK, :], held, NT).astype(jnp.bfloat16)
        inner = dot(pick, inner_ref[...]).astype(jnp.bfloat16)
        outer = dot(pick, outer_ref[...]).astype(jnp.bfloat16)
        for part in range(2):
            rows = slice(2 * start + part * CHUNK, 2 * start + (part + 1) * CHUNK)
            inner_out[rows, :] = inner[:, part * 2 * BLOCK : (part + 1) * 2 * BLOCK]
            outer_out[rows, :] = outer[:, part * BLOCK : (part + 1) * BLOCK]

    def add(tile, first, value):
        out_ref.at[tile][pl.ds(first, value.shape[0], stride=2), :] = value

    add_modes(bins, groups, cycles, groups_ref, inner_out, outer_out, add)


def split_sum(parts, tile, keep_ref, send_refs):
    rows = keep_ref.shape[0]
    lanes = slice(tile * LANES, (tile + 1) * LANES)
    for i, out_ref in enumerate((keep_ref, *send_refs)):
        value = sum(part(slice(i * rows, (i + 1) * rows), lanes) for part in parts)
        out_ref[:, lanes] = value.astype(out_ref.dtype)


def other_kernel(bins, groups, cycles, groups_ref, inner_ref, outer_ref, own_ref, keep_ref, *refs):
    *send_refs, other_ref = refs

    def add(tile, first, value):
        other_ref.at[tile][pl.ds(first, value.shape[0], stride=2), :] = value

    add_modes(bins, groups, cycles, groups_ref, inner_ref, outer_ref, add)
    for tile in range(own_ref.shape[0]):
        parts = (lambda rows, lanes: own_ref[tile, rows, :], lambda rows, lanes: other_ref[tile, rows, :])
        split_sum(parts, tile, keep_ref, send_refs)


def merge_kernel(count, kept_ref, *refs):
    arrived, outs = refs[:count], refs[count:]
    for tile in range(kept_ref.shape[1] // LANES):
        parts = [lambda rows, lanes, ref=ref: ref[rows, lanes].astype(jnp.float32) for ref in (kept_ref, *arrived)]
        split_sum(parts, tile, outs[0], outs[1:])


def gain_column(degrees):
    l = np.arange(degrees, dtype=np.float32)
    return np.where(l > 0.5, np.float32(-20000.0) / np.maximum(l * (l + 1), np.float32(1)), np.float32(0)).astype(np.float32)[:, None] * np.ones((1, BLOCK), np.float32)


def interleave(cycles, cycles_here):
    out = np.zeros((2 * cycles, 2 * cycles), np.float32)
    for f in range(2):
        for c in range(cycles):
            out[f * cycles + c, (c // cycles_here * 2 + f) * cycles_here + c % cycles_here] = 1
    return out.astype(jnp.bfloat16)


def respond(basis, gain_ref, order_ref, out_ref, slot):
    cycles = basis.shape[1]
    gain = jnp.concatenate([gain_ref[...]] * (cycles // BLOCK), 1)
    gained = (basis.astype(jnp.float32) * gain).astype(jnp.bfloat16)
    high, low = high_low(dot(basis, jnp.concatenate([basis, gained], 1), TN))
    out_ref[slot, :cycles, :] = dot(high, order_ref[...]).astype(jnp.bfloat16)
    out_ref[slot, cycles:, :] = dot(low, order_ref[...]).astype(jnp.bfloat16)


def first_response_kernel(staged_ref, legendre_hbm, gain_ref, order_ref, out_ref, rest_ref, sems):
    staged = staged_ref.shape[0]
    count = out_ref.shape[0]
    copies = []
    for i, (first, last) in enumerate(((staged, count), (count, staged + rest_ref.shape[0]))):
        target = rest_ref.at[pl.ds(first - staged, last - first)]
        copies.append(pltpu.make_async_copy(legendre_hbm.at[pl.ds(first, last - first)], target, sems.at[i]))
        copies[-1].start()
    for slot in range(staged):
        respond(staged_ref[slot], gain_ref, order_ref, out_ref, slot)
    copies[0].wait()
    for slot in range(staged, count):
        respond(rest_ref[slot - staged], gain_ref, order_ref, out_ref, slot)
    copies[1].wait()


def response_kernel(start, from_hbm, legendre_ref, gain_ref, order_ref, out_ref, *scratch):
    count = out_ref.shape[0]
    copies = []
    if from_hbm:
        source, (legendre_ref, sems) = legendre_ref, scratch
        copies = [pltpu.make_async_copy(source.at[start + i], legendre_ref.at[i], sems.at[i]) for i in range(count)]
        for copy in copies:
            copy.start()
        start = 0
    for slot in range(count):
        if from_hbm:
            copies[slot].wait()
        respond(legendre_ref[start + slot], gain_ref, order_ref, out_ref, slot)


def slot_order(slots, bins):
    out = np.zeros((slots * 2 * bins, slots * 2 * bins), np.float32)
    for b in range(bins):
        for c in range(2):
            for t in range(slots):
                out[(t * 2 + c) * bins + b, (b * slots + t) * 2 + c] = 1
    return out.astype(jnp.bfloat16)


def synthesis_kernel(arrivals, pieces, kept_ref, *refs):
    partials, refs = refs[:arrivals], refs[arrivals:]
    response_refs, (order_ref, out_ref) = refs[:pieces], refs[pieces:]
    cycles = response_refs[0].shape[1] // 2
    bins = kept_ref.shape[1] // cycles
    slots = kept_ref.shape[0] // 2
    responses = [ref.at[i] for ref in response_refs for i in range(ref.shape[0])]
    total = kept_ref[...]
    for ref in partials:
        total = total + ref[...].astype(jnp.float32)
    modes = jnp.concatenate([total[:, b * cycles : (b + 1) * cycles] for b in range(bins)], 0)
    high, low = high_low(modes)
    high = dot(order_ref[...], high)
    low = dot(order_ref[...], low)
    per_slot = 2 * bins
    parts = []
    for t in range(slots):
        rows = slice(t * per_slot, (t + 1) * per_slot)
        left = jnp.concatenate([high[rows, :], low[rows, :]], 0).astype(jnp.bfloat16)
        part = dot(twice(left), responses[t][...])
        parts.append(part[:per_slot, :] + part[per_slot:, :])
    parts.append(jnp.zeros((128 - slots * per_slot, 2 * cycles), jnp.float32))
    result = jnp.concatenate(parts, 0)
    out_ref[...] = jnp.transpose(result).astype(jnp.bfloat16)


def order_classes(orders):
    return [np.arange(0, orders, 4), np.arange(2, orders, 4), np.arange(1, orders, 2)]


def inverse_tables(orders):
    quarter = NPHI // 4
    k = np.arange(quarter, dtype=np.int64)[None, :]
    rows = []
    for m in order_classes(orders):
        angle = (m[:, None] * k % NPHI) * (2 * np.pi / NPHI)
        rows += [np.cos(angle), -np.sin(angle)]
    return np.concatenate(np.split(np.concatenate(rows), quarter // 512, axis=1)).astype(np.float32).astype(jnp.bfloat16)


def padded(count):
    return -(-count // LANES) * LANES


def order_lanes(orders):
    out = []
    for m in order_classes(orders):
        out.append(np.concatenate([m, np.full(padded(len(m)) - len(m), -1)]))
    return np.concatenate(out).astype(np.int32)[None, :]


def turn_rows(order_row):
    m = np.maximum(order_row[0], 0).astype(np.float64)
    weight = np.where(order_row[0] == 0, 1.0, 2.0)
    sign = np.where(order_row[0] % 4 == 3, 1.0, -1.0)
    parts = np_high_low(np.cos(np.pi * m / NPHI) * weight) + np_high_low(np.sin(np.pi * m / NPHI) * weight)
    parts = parts + (weight.astype(jnp.bfloat16), sign.astype(jnp.bfloat16))
    return np.stack(parts + (np.zeros_like(parts[0]),) * 10)


def part_rows(part, bins, cycles_here):
    shape = (2 * bins * cycles_here, 4 * bins * cycles_here)
    row = lax.broadcasted_iota(jnp.int32, shape, 0)
    column = lax.broadcasted_iota(jnp.int32, shape, 1)
    cycle = lax.rem(row, cycles_here)
    bin_number = lax.rem(lax.div(row, cycles_here), bins)
    filter_number = lax.div(row, cycles_here * bins)
    return hot(column == ((filter_number * cycles_here + cycle) * 2 + part) * bins + bin_number)


def inverse_kernel(arrived_ref, slots_hbm, turn_hbm, table_hbm, kappa_hbm, potential_hbm,
                   slots_ref, turn_ref, table_ref, wide_ref, kappa_ref, potential_ref, sems, out_sems):
    copies = [
        pltpu.make_async_copy(a, b, sems.at[i])
        for i, (a, b) in enumerate(((slots_hbm, slots_ref), (turn_hbm, turn_ref)))
    ]
    quarter = NPHI // 4
    chunk = table_ref.shape[1]
    chunks = quarter // chunk
    part = table_ref.shape[0] // chunks
    for i in range(chunks):
        rows = pl.ds(i * part, part)
        copies.append(pltpu.make_async_copy(table_hbm.at[rows], table_ref.at[rows], sems.at[2 + i]))
    for copy in copies:
        copy.start()
    devices, slots = slots_ref.shape
    bins, cycles_here, _ = kappa_ref.shape
    order_count = part // 2
    per_slot = 2 * bins
    per_source = 2 * cycles_here
    wide_ref[...] = arrived_ref[...].astype(jnp.float32)
    turned = [jnp.transpose(wide_ref[pl.ds(i, devices, stride=per_source), :]) for i in range(per_source)]
    few, many = order_count // 4, order_count // 2
    starts = [0, padded(few), 2 * padded(few)]
    lane = lax.broadcasted_iota(jnp.int32, (1, turn_ref.shape[1]), 1)
    orders = jnp.where(lane < few, 4 * lane, -1)
    within = lane - starts[1]
    orders = jnp.where((within >= 0) & (within < few), 4 * within + 2, orders)
    within = lane - starts[2]
    orders = jnp.where((within >= 0) & (within < many), 2 * within + 1, orders)
    for copy in copies[:2]:
        copy.wait()
    lefts, picks = [], []
    for t in range(slots):
        lefts.append(jnp.concatenate([x[t * per_slot : (t + 1) * per_slot, :] for x in turned], 0))
        picks.append(hot(slots_ref[:, t : t + 1] == orders))
    spectrum = dot(jnp.concatenate(lefts, 1).astype(jnp.bfloat16), jnp.concatenate(picks, 0))
    spectrum = spectrum.astype(jnp.bfloat16)
    real_in = dot(part_rows(0, bins, cycles_here), spectrum)
    imag_in = dot(part_rows(1, bins, cycles_here), spectrum)
    turn = turn_ref[...].astype(jnp.float32)
    odd = lax.rem(lax.rem(lax.broadcasted_iota(jnp.int32, real_in.shape, 0), cycles_here), 2) == 1
    turn_cos = jnp.where(odd, turn[0:1, :] + turn[1:2, :], turn[4:5, :])
    turn_sin = jnp.where(odd, turn[2:3, :] + turn[3:4, :], 0.0)
    real = real_in * turn_cos - imag_in * turn_sin
    imag = real_in * turn_sin + imag_in * turn_cos
    sign = turn[5:6, starts[2] :]
    count = real.shape[0]
    lefts = []
    for index, start in enumerate(starts):
        lanes = slice(start, start + (few if index < 2 else many))
        cos_rows, sin_rows = [real[:, lanes]], [imag[:, lanes]]
        if index == 2:
            cos_rows.append(imag[:, lanes] * sign[:, :many])
            sin_rows.append(-real[:, lanes] * sign[:, :many])
        for rows in (cos_rows, sin_rows):
            lefts.append(jnp.concatenate([y for x in rows for y in high_low(x)], 0))
    results = []
    for index in range(chunks):
        copies[2 + index].wait()
        row = index * part
        sums = []
        for at in range(3):
            height = few if at < 2 else many
            both = dot(lefts[2 * at], table_ref[row : row + height, :])
            both = both + dot(lefts[2 * at + 1], table_ref[row + height : row + 2 * height, :])
            row += 2 * height
            sums += [both[i : i + count, :] + both[i + count : i + 2 * count, :] for i in range(0, both.shape[0], 2 * count)]
        even, other = sums[0] + sums[1], sums[0] - sums[1]
        values = (even + sums[2], other + sums[3], even - sums[2], other - sums[3])
        for j, value in enumerate(values):
            lanes = pl.ds(j * quarter + index * chunk, chunk)
            for f, (out_ref, out_hbm) in enumerate(((kappa_ref, kappa_hbm), (potential_ref, potential_hbm))):
                for b in range(bins):
                    at = (f * bins + b) * cycles_here
                    out_ref[b, :, lanes] = value[at : at + cycles_here, :]
                copy = pltpu.make_async_copy(out_ref.at[:, :, lanes], out_hbm.at[:, :, lanes], out_sems.at[len(results)])
                copy.start()
                results.append(copy)
    for copy in results:
        copy.wait()


def in_hbm(x):
    return pltpu.with_memory_space_constraint(jnp.asarray(x), pltpu.HBM)


def params(orders):
    small = 14 if orders <= 512 else 56
    return pltpu.CompilerParams(vmem_limit_bytes=small * 1024 * 1024)


def per_device(weights, offsets, counts, block_ids, m_table, legendre):
    axes = ("blk", "y", "core")
    _, devices, capacity, bins, _ = weights.shape
    slots, degrees, cycles = legendre.shape
    orders = m_table.shape[0]
    groups = devices * capacity
    cycles_here = cycles // devices
    width = bins * cycles
    staged = legendre.size <= 4 * 1024 * 1024
    limits = params(orders)
    hbm = pl.BlockSpec(memory_space=pltpu.HBM)
    vmem = pl.BlockSpec(memory_space=pltpu.VMEM)

    def shaped(*shape, dtype=jnp.bfloat16):
        return jax.ShapeDtypeStruct(shape, dtype)

    rows = slot_rows(orders, slots)
    inner, outer = analysis_tables(orders)
    live = (capacity + 1) * devices // 2
    key_rows = -(-live // LANES) * 16
    shapes = [
        shaped(bins * live + key_rows, BLOCK),
        shaped(1, orders, dtype=jnp.int32),
        shaped(*rows.shape),
        shaped(*inner.shape),
        shaped(*outer.shape),
    ]
    operands = [
        weights.reshape(groups * bins, BLOCK),
        offsets.reshape(groups, BLOCK),
        counts,
        jnp.transpose(block_ids[0]),
        m_table,
        rows,
        inner,
        outer,
    ]
    ahead = slots // 2 if staged else 0
    if staged:
        shapes.append(shaped(ahead, degrees, cycles))
        operands.append(legendre)
    deposits, *shared = pl.pallas_call(
        functools.partial(first_kernel, slots, cycles_here * SEGMENTS, ahead),
        in_specs=[hbm] * len(operands),
        out_specs=(vmem,) * len(shapes),
        out_shape=tuple(shapes),
        scratch_shapes=[
            pltpu.VMEM((groups * bins, BLOCK), jnp.bfloat16),
            pltpu.VMEM((groups, BLOCK), jnp.int32),
            pltpu.VMEM((1, devices), jnp.int32),
            pltpu.VMEM((capacity, devices), jnp.int32),
            pltpu.VMEM((orders,), jnp.int32),
            pltpu.VMEM((groups * bins, BLOCK), jnp.float32),
            pltpu.VMEM((bins, live, BLOCK), jnp.bfloat16),
            pltpu.VMEM((live, BLOCK), jnp.float32),
            pltpu.SemaphoreType.DMA((len(operands),)),
        ],
        compiler_params=limits,
        name="deposit",
    )(*[in_hbm(x) for x in operands])
    early = shared.pop() if staged else None
    basis = legendre

    def swap(x, mask):
        return lax.ppermute(x, axes, [(i, i ^ mask) for i in range(devices)])

    other = swap(deposits, 1)
    cost = pl.CostEstimate(flops=8 * orders * 256 * bins * live, bytes_accessed=4 * orders * width, transcendentals=0)
    modes_shape = (width // LANES, orders, LANES)
    own, own_inner, own_outer = pl.pallas_call(
        functools.partial(own_kernel, bins, live, cycles),
        in_specs=[vmem] * 5,
        out_specs=(vmem,) * 3,
        out_shape=(
            shaped(*modes_shape, dtype=jnp.float32),
            shaped(orders, inner.shape[1] // 2),
            shaped(orders, outer.shape[1] // 2),
        ),
        compiler_params=limits,
        cost_estimate=cost,
        name="own_groups",
    )(deposits, *shared)

    groups_of_bits = bit_groups(devices)
    stages = len(groups_of_bits)
    gain, order = gain_column(degrees), interleave(cycles, cycles_here)
    blocks = devices // 2
    kernel, inputs = functools.partial(other_kernel, bins, live, cycles), (other, own_inner, own_outer, own)
    scratch = [pltpu.VMEM(modes_shape, jnp.float32)]
    responses = []
    for stage, bits in enumerate(groups_of_bits):
        ways = 1 << len(bits)
        blocks //= ways
        rows_here = blocks * 2 * slots
        kept, *sends = pl.pallas_call(
            kernel,
            in_specs=[vmem] * len(inputs),
            out_specs=(vmem,) * ways,
            out_shape=(shaped(rows_here, width, dtype=jnp.float32),) + (shaped(rows_here, width),) * (ways - 1),
            scratch_shapes=scratch,
            compiler_params=limits,
            name="merge" if stage else "other_groups",
        )(*inputs)
        *sends, basis = lax.optimization_barrier((*sends, basis))
        if stage == 0 or not staged:
            basis = in_hbm(basis)
        arrived = [swap(x, (i + 1) << bits[0]) for i, x in reversed(list(enumerate(sends)))]
        first, last = (min(slots, slots * 2 * k * (2 * stages - k) // (2 * stages * stages)) for k in (stage, stage + 1))
        count = last - first
        shape = shaped(count, 2 * cycles, 2 * cycles)
        cost = pl.CostEstimate(
            flops=6 * count * degrees * cycles * cycles, bytes_accessed=2 * count * degrees * cycles, transcendentals=0
        )
        if staged and stage == 0:
            response, basis = pl.pallas_call(
                first_response_kernel,
                in_specs=[vmem, hbm, vmem, vmem],
                out_specs=(vmem, vmem),
                out_shape=(shape, shaped(slots - ahead, degrees, cycles)),
                scratch_shapes=[pltpu.SemaphoreType.DMA((2,))],
                compiler_params=limits,
                cost_estimate=cost,
                name="response",
            )(early, basis, gain, order)
        else:
            response = pl.pallas_call(
                functools.partial(response_kernel, first - ahead, not staged),
                in_specs=[vmem if staged else hbm, vmem, vmem],
                out_specs=vmem,
                out_shape=shape,
                scratch_shapes=[] if staged else [pltpu.VMEM((count, degrees, cycles), jnp.bfloat16), pltpu.SemaphoreType.DMA((count,))],
                compiler_params=limits,
                cost_estimate=cost,
                name="response",
            )(basis, gain, order)
        *arrived, response = lax.optimization_barrier((*arrived, response))
        responses.append(response)
        kernel, inputs, scratch = functools.partial(merge_kernel, len(arrived)), (kept, *arrived), []

    outgoing = pl.pallas_call(
        functools.partial(synthesis_kernel, len(inputs) - 1, len(responses)),
        in_specs=[vmem] * (len(inputs) + len(responses) + 1),
        out_specs=vmem,
        out_shape=shaped(2 * cycles, 128),
        compiler_params=limits,
        name="synthesis",
    )(*inputs, *responses, slot_order(slots, bins))
    outgoing = outgoing.reshape(devices, 2 * cycles_here, 128)
    outgoing, held = lax.optimization_barrier((outgoing, m_table))
    arrived = lax.all_to_all(outgoing, axes, split_axis=0, concat_axis=0, tiled=True)
    arrived = arrived.reshape(2 * cycles, 128)
    if staged:
        arrived = pltpu.with_memory_space_constraint(arrived, pltpu.VMEM)

    lanes = order_lanes(orders)
    constants = [turn_rows(lanes), inverse_tables(orders)]
    chunks = NPHI // 4 // constants[-1].shape[1]
    map_shape = shaped(bins, cycles_here, NPHI, dtype=jnp.float32)
    return pl.pallas_call(
        inverse_kernel,
        in_specs=[vmem] + [hbm] * 3,
        out_specs=(hbm, hbm),
        out_shape=(map_shape, map_shape),
        scratch_shapes=[
            pltpu.VMEM((devices, slots), jnp.int32),
            *[pltpu.VMEM(x.shape, x.dtype) for x in constants],
            pltpu.VMEM((2 * cycles, 128), jnp.float32),
            pltpu.VMEM(map_shape.shape, jnp.float32),
            pltpu.VMEM(map_shape.shape, jnp.float32),
            pltpu.SemaphoreType.DMA((2 + chunks,)),
            pltpu.SemaphoreType.DMA((8 * chunks,)),
        ],
        compiler_params=limits,
        name="inverse",
    )(arrived, in_hbm(held.reshape(devices, slots)), *[in_hbm(x) for x in constants])


def solution(mesh):
    blocks, columns = mesh.devices.shape
    fine = Mesh(mesh.devices.reshape(blocks, columns // 2, 2), ("blk", "y", "core"))
    axes = ("blk", "y", "core")
    placed = (
        P(axes, None, None, None, None),
        P(axes, None, None, None),
        P(axes, None),
        P(axes, None, None),
        P(),
        P(axes, None, None),
    )
    return jax.shard_map(
        per_device,
        mesh=fine,
        in_specs=placed,
        out_specs=(P(None, axes, None), P(None, axes, None)),
        check_vma=False,
    )
```

```python
import functools

import jax
import jax.numpy as jnp
import numpy as np
from jax import lax
from jax.experimental import pallas as pl
from jax.experimental.pallas import tpu as pltpu
from jax.sharding import Mesh, PartitionSpec as P

NPHI = 4096
BLOCK = 128
SEGMENTS = NPHI // BLOCK
LANES = 128
CHUNK = 192

NT = (((1,), (1,)), ((), ()))
TN = (((0,), (0,)), ((), ()))


def dot(a, b, dims=(((1,), (0,)), ((), ()))):
    return lax.dot_general(a, b, dims, preferred_element_type=jnp.float32)


def high_low(x):
    high = x.astype(jnp.bfloat16)
    return high, (x - high.astype(jnp.float32)).astype(jnp.bfloat16)


def np_high_low(x):
    high = x.astype(np.float32).astype(jnp.bfloat16)
    return high, (x - high.astype(np.float64)).astype(np.float32).astype(jnp.bfloat16)


def analysis_tables(orders):
    m = np.arange(orders, dtype=np.int64)[:, None]
    p = np.arange(BLOCK, dtype=np.int64)[None, :]
    angle = (m * p % NPHI) * (2 * np.pi / NPHI)
    inner = np.concatenate(np_high_low(np.cos(angle)) + np_high_low(-np.sin(angle)), 1)
    half = np.arange(2 * SEGMENTS, dtype=np.int64)[None, :]
    steps = 2 * BLOCK * (half % SEGMENTS) + half // SEGMENTS
    angle = (m * steps % (2 * NPHI)) * (np.pi / NPHI)
    outer = np.concatenate(np_high_low(np.cos(angle) / NPHI) + np_high_low(-np.sin(angle) / NPHI), 1)
    return inner, outer


def bit_groups(devices):
    bits = list(range(1, devices.bit_length() - 1))
    return [bits[i : i + 2] for i in range(0, len(bits), 2)]


def positions(devices):
    order = [0]
    for group in bit_groups(devices):
        order = [p | (v << group[0]) for p in order for v in range(1 << len(group))]
    return order


def slot_rows(orders, slots):
    out = np.zeros((orders // 2, orders), np.float32)
    for block, position in enumerate(positions(orders // slots)):
        for slot in range(slots):
            out[block * slots + slot, position * slots + slot] = 1
    return out.astype(jnp.bfloat16)


def rolled(x, shift):
    return jnp.concatenate([x[:, shift:], x[:, :shift]], 1)


def exclusive_or(table, me, slots):
    orders = table.shape[1]
    block = lax.div(lax.broadcasted_iota(jnp.int32, table.shape, 1), slots)
    for bit in range((orders // slots).bit_length() - 1):
        shift = slots << bit
        swapped = jnp.where((block >> bit) % 2 == 0, rolled(table, shift), rolled(table, orders - shift))
        table = jnp.where(jnp.broadcast_to((me >> bit) & 1, table.shape) == 1, swapped, table)
    return table


def hot(condition):
    return jnp.where(condition, 1.0, 0.0).astype(jnp.bfloat16)


def twice(x):
    return jnp.concatenate([x, x], 1)


def first_kernel(slots, blocks_here, staged, w_hbm, off_hbm, cnt_hbm, ids_hbm, table_hbm, rows_hbm, inner_hbm, outer_hbm, *refs):
    if staged:
        legendre_hbm, *refs = refs
    out_ref, table_ref, rows_ref, inner_ref, outer_ref, *refs = refs
    if staged:
        legendre_ref, *refs = refs
    w_ref, off_ref, cnt_ref, ids_ref, flat_ref, wide_ref, live_w_ref, live_off_ref, sems = refs
    pairs = (
        (cnt_hbm, cnt_ref), (ids_hbm, ids_ref), (off_hbm, off_ref), (w_hbm, w_ref),
        (table_hbm, flat_ref), (rows_hbm, rows_ref), (inner_hbm, inner_ref), (outer_hbm, outer_ref),
    )
    if staged:
        pairs = pairs + ((legendre_hbm.at[pl.ds(0, staged)], legendre_ref),)
    copies = [pltpu.make_async_copy(a, b, sems.at[i]) for i, (a, b) in enumerate(pairs)]
    for copy in copies[:4]:
        copy.start()
    groups = off_ref.shape[0]
    capacity, devices = ids_ref.shape
    bins, live, _ = live_w_ref.shape
    pack = 16
    key_tiles = (out_ref.shape[0] - bins * live) // pack

    owner = lax.div(lax.broadcasted_iota(jnp.int32, (devices, groups), 1), capacity)
    source = lax.broadcasted_iota(jnp.int32, (devices, groups), 0)
    member = lax.rem(lax.broadcasted_iota(jnp.int32, (capacity, groups), 1), capacity)
    own_row = lax.broadcasted_iota(jnp.int32, (capacity, groups), 0) == member
    for copy in copies[:2]:
        copy.wait()
    counts = jnp.broadcast_to(cnt_ref[...].astype(jnp.float32), (8, devices)).astype(jnp.bfloat16)
    count = dot(counts, hot(source == owner))[0:1, :]
    before = dot(counts, hot(source < owner))[0:1, :]
    number = member[0:1, :].astype(jnp.float32)
    place = jnp.where(number < count, before + number, -1.0).astype(jnp.int32)
    packing = hot(lax.broadcasted_iota(jnp.int32, (key_tiles * LANES, groups), 0) == place)

    ids = dot(ids_ref[...].astype(jnp.float32).astype(jnp.bfloat16), hot(source == owner))
    ids = jnp.sum(jnp.where(own_row, ids, 0.0), axis=0, keepdims=True)
    block = ids.astype(jnp.int32) + owner[0:1, :] * blocks_here
    cycle = lax.div(block, SEGMENTS)
    phase = lax.rem(cycle, 2) * SEGMENTS + lax.rem(block, SEGMENTS)
    row = lax.broadcasted_iota(jnp.int32, (pack, groups), 0)
    keys = jnp.where(row == 0, lax.div(cycle, 16), jnp.where(row == 1, lax.rem(cycle, 16), phase))
    keys = dot(keys.astype(jnp.float32).astype(jnp.bfloat16), packing, NT).astype(jnp.bfloat16)
    for tile in range(key_tiles):
        out_ref[bins * live + tile * pack : bins * live + (tile + 1) * pack, :] = keys[:, tile * LANES : (tile + 1) * LANES]

    for copy in copies[2:4]:
        copy.wait()
    for copy in copies[4:]:
        copy.start()
    packing = packing[:live, :]
    live_off_ref[...] = dot(packing, off_ref[...].astype(jnp.float32).astype(jnp.bfloat16))
    wide_ref[...] = w_ref[...].astype(jnp.float32)
    for b in range(bins):
        live_w_ref[b] = dot(packing, wide_ref[pl.ds(b, groups, stride=bins), :].astype(jnp.bfloat16)).astype(jnp.bfloat16)

    pixel = lax.broadcasted_iota(jnp.int32, (pack, BLOCK), 0)
    pixels = [(pixel + pack * k).astype(jnp.float32).astype(jnp.bfloat16) for k in range(BLOCK // pack)]
    alone = [hot(pixel == i) for i in range(pack)]
    one = jnp.ones((pack, BLOCK), jnp.bfloat16)
    zero = jnp.zeros((pack, BLOCK), jnp.bfloat16)

    def deposit(step, carry):
        start = pl.multiple_of(step * pack, pack)
        weights = [live_w_ref[b, pl.ds(start, pack), :] for b in range(bins)]
        left, right = [], []
        for i in range(pack):
            left.append(jnp.concatenate([w * alone[i] for w in weights], 0))
            at = jnp.broadcast_to(live_off_ref[pl.ds(start + i, 1), :], (pack, BLOCK)).astype(jnp.bfloat16)
            right.append(jnp.concatenate([jnp.where(at == x, one, zero) for x in pixels], 0))
        out = dot(jnp.concatenate(left, 1), jnp.concatenate(right, 1), NT).astype(jnp.bfloat16)
        for b in range(bins):
            out_ref[pl.ds(pl.multiple_of(b * live + start, pack), pack), :] = out[b * pack : (b + 1) * pack, :]
        return carry

    lax.fori_loop(0, live // pack, deposit, 0, unroll=9)
    for copy in copies[4:8]:
        copy.wait()
    me = lax.axis_index("blk")
    for axis in ("y", "core"):
        me = me * lax.axis_size(axis) + lax.axis_index(axis)
    table_ref[...] = exclusive_or(flat_ref[...].reshape(table_ref.shape), me, slots)
    for copy in copies[8:]:
        copy.wait()


def add_modes(bins, groups, cycles, groups_ref, inner_ref, outer_ref, add):
    pack = 16
    keys = groups_ref[bins * groups :, :].astype(jnp.float32)
    keys = jnp.concatenate([keys[i * pack : (i + 1) * pack, :] for i in range(keys.shape[0] // pack)], 1)
    cycle = (keys[0:1, :groups] * 16.0 + keys[1:2, :groups]).astype(jnp.int32)
    phase = keys[2:3, :groups].astype(jnp.int32)
    cycle_hot = hot(lax.broadcasted_iota(jnp.int32, (cycles, groups), 0) == cycle)
    half_hot = hot(lax.broadcasted_iota(jnp.int32, (2 * SEGMENTS, groups), 0) == phase)
    phase_hot = jnp.concatenate([half_hot, half_hot], 0)
    deposits = [twice(groups_ref[b * groups : (b + 1) * groups, :]) for b in range(bins)]
    for start in range(0, inner_ref.shape[0], 2 * CHUNK):
        rows = slice(start, start + 2 * CHUNK)
        outer = dot(outer_ref[rows, :], phase_hot)
        outer_cos, outer_sin = outer[:CHUNK, :], outer[CHUNK:, :]
        for b, deposit in enumerate(deposits):
            inner = dot(inner_ref[rows, :], deposit, NT)
            inner_cos, inner_sin = inner[:CHUNK, :], inner[CHUNK:, :]
            real = inner_cos * outer_cos - inner_sin * outer_sin
            imag = inner_cos * outer_sin + inner_sin * outer_cos
            both = dot(jnp.concatenate([real, imag], 0).astype(jnp.bfloat16), cycle_hot, NT)
            for part in range(2):
                value = both[part * CHUNK : (part + 1) * CHUNK, :]
                for tile in range(cycles // LANES):
                    add(b * (cycles // LANES) + tile, start + part, value[:, tile * LANES : (tile + 1) * LANES])


def own_kernel(bins, groups, cycles, staged, groups_ref, table_ref, rows_ref, inner_ref, outer_ref, *refs):
    if staged:
        legendre_hbm, out_ref, inner_out, outer_out, legendre_ref, sem = refs
        late = pltpu.make_async_copy(legendre_hbm.at[pl.ds(staged, legendre_ref.shape[0])], legendre_ref, sem)
        late.start()
    else:
        out_ref, inner_out, outer_out = refs
    count, orders = rows_ref.shape
    held = hot(lax.broadcasted_iota(jnp.int32, (orders, orders), 0) == table_ref[...])
    for start in range(0, count, CHUNK):
        pick = dot(rows_ref[start : start + CHUNK, :], held, NT).astype(jnp.bfloat16)
        inner = dot(pick, inner_ref[...]).astype(jnp.bfloat16)
        outer = dot(pick, outer_ref[...]).astype(jnp.bfloat16)
        for part in range(2):
            rows = slice(2 * start + part * CHUNK, 2 * start + (part + 1) * CHUNK)
            inner_out[rows, :] = inner[:, part * 2 * BLOCK : (part + 1) * 2 * BLOCK]
            outer_out[rows, :] = outer[:, part * BLOCK : (part + 1) * BLOCK]

    def add(tile, first, value):
        out_ref.at[tile][pl.ds(first, value.shape[0], stride=2), :] = value

    add_modes(bins, groups, cycles, groups_ref, inner_out, outer_out, add)
    if staged:
        late.wait()


def split_sum(parts, tile, keep_ref, send_refs):
    rows = keep_ref.shape[0]
    lanes = slice(tile * LANES, (tile + 1) * LANES)
    for i, out_ref in enumerate((keep_ref, *send_refs)):
        value = sum(part(slice(i * rows, (i + 1) * rows), lanes) for part in parts)
        out_ref[:, lanes] = value.astype(out_ref.dtype)


def send_order(ways):
    return [(1, 2), (2, 1), (3, 3)] if ways == 4 else [(i, i) for i in range(1, ways)]


def other_kernel(bins, groups, cycles, groups_ref, inner_ref, outer_ref, own_ref, keep_ref, *refs):
    *send_refs, other_ref = refs

    def add(tile, first, value):
        other_ref.at[tile][pl.ds(first, value.shape[0], stride=2), :] = value

    add_modes(bins, groups, cycles, groups_ref, inner_ref, outer_ref, add)
    rows = keep_ref.shape[0]
    core = lax.axis_index("core")
    blocks = [(0, 0)] + send_order(len(send_refs) + 1)
    for (even, odd), out_ref in zip(blocks, (keep_ref, *send_refs)):
        first = even * rows if even == odd else pl.multiple_of((even + core * (odd - even)) * rows, rows)
        for tile in range(own_ref.shape[0]):
            value = own_ref[tile, pl.ds(first, rows), :] + other_ref[tile, pl.ds(first, rows), :]
            out_ref[:, tile * LANES : (tile + 1) * LANES] = value.astype(out_ref.dtype)


def merge_kernel(count, kept_ref, *refs):
    arrived, outs = refs[:count], refs[count:]
    for tile in range(kept_ref.shape[1] // LANES):
        parts = [lambda rows, lanes, ref=ref: ref[rows, lanes].astype(jnp.float32) for ref in (kept_ref, *arrived)]
        split_sum(parts, tile, outs[0], outs[1:])


def gain_column(degrees):
    l = np.arange(degrees, dtype=np.float32)
    return np.where(l > 0.5, np.float32(-20000.0) / np.maximum(l * (l + 1), np.float32(1)), np.float32(0)).astype(np.float32)[:, None] * np.ones((1, BLOCK), np.float32)


def interleave(cycles, cycles_here):
    out = np.zeros((2 * cycles, 2 * cycles), np.float32)
    for f in range(2):
        for c in range(cycles):
            out[f * cycles + c, (c // cycles_here * 2 + f) * cycles_here + c % cycles_here] = 1
    return out.astype(jnp.bfloat16)


def respond(basis, gain_ref, order_ref, out_ref, slot):
    cycles = basis.shape[1]
    gain = jnp.concatenate([gain_ref[...]] * (cycles // BLOCK), 1)
    gained = (basis.astype(jnp.float32) * gain).astype(jnp.bfloat16)
    high, low = high_low(dot(basis, jnp.concatenate([basis, gained], 1), TN))
    out_ref[slot, :cycles, :] = dot(high, order_ref[...]).astype(jnp.bfloat16)
    out_ref[slot, cycles:, :] = dot(low, order_ref[...]).astype(jnp.bfloat16)


def staged_response_kernel(start, early_ref, late_ref, gain_ref, order_ref, out_ref):
    early = early_ref.shape[0]
    for slot in range(out_ref.shape[0]):
        at = start + slot
        respond(early_ref[at] if at < early else late_ref[at - early], gain_ref, order_ref, out_ref, slot)


def response_kernel(start, legendre_hbm, gain_ref, order_ref, out_ref, legendre_ref, sems):
    count = out_ref.shape[0]
    copies = [pltpu.make_async_copy(legendre_hbm.at[start + i], legendre_ref.at[i], sems.at[i]) for i in range(count)]
    for copy in copies:
        copy.start()
    for slot in range(count):
        copies[slot].wait()
        respond(legendre_ref[slot], gain_ref, order_ref, out_ref, slot)


def slot_order(slots, bins):
    out = np.zeros((slots * 2 * bins, slots * 2 * bins), np.float32)
    for b in range(bins):
        for c in range(2):
            for t in range(slots):
                out[(t * 2 + c) * bins + b, (b * slots + t) * 2 + c] = 1
    return out.astype(jnp.bfloat16)


def synthesis_kernel(arrivals, pieces, kept_ref, *refs):
    partials, refs = refs[:arrivals], refs[arrivals:]
    response_refs, (order_ref, out_ref) = refs[:pieces], refs[pieces:]
    cycles = response_refs[0].shape[1] // 2
    bins = kept_ref.shape[1] // cycles
    slots = kept_ref.shape[0] // 2
    responses = [ref.at[i] for ref in response_refs for i in range(ref.shape[0])]
    total = kept_ref[...]
    for ref in partials:
        total = total + ref[...].astype(jnp.float32)
    modes = jnp.concatenate([total[:, b * cycles : (b + 1) * cycles] for b in range(bins)], 0)
    high, low = high_low(modes)
    high = dot(order_ref[...], high)
    low = dot(order_ref[...], low)
    per_slot = 2 * bins
    parts = []
    for t in range(slots):
        rows = slice(t * per_slot, (t + 1) * per_slot)
        left = jnp.concatenate([high[rows, :], low[rows, :]], 0).astype(jnp.bfloat16)
        part = dot(twice(left), responses[t][...])
        parts.append(part[:per_slot, :] + part[per_slot:, :])
    parts.append(jnp.zeros((128 - slots * per_slot, 2 * cycles), jnp.float32))
    result = jnp.concatenate(parts, 0)
    out_ref[...] = jnp.transpose(result).astype(jnp.bfloat16)


def order_classes(orders):
    return [np.arange(0, orders, 4), np.arange(2, orders, 4), np.arange(1, orders, 2)]


def inverse_tables(orders):
    quarter = NPHI // 4
    k = np.arange(quarter, dtype=np.int64)[None, :]
    rows = []
    for m in order_classes(orders):
        angle = (m[:, None] * k % NPHI) * (2 * np.pi / NPHI)
        rows += [np.cos(angle), -np.sin(angle)]
    return np.concatenate(np.split(np.concatenate(rows), quarter // 512, axis=1)).astype(np.float32).astype(jnp.bfloat16)


def padded(count):
    return -(-count // LANES) * LANES


def order_lanes(orders):
    out = []
    for m in order_classes(orders):
        out.append(np.concatenate([m, np.full(padded(len(m)) - len(m), -1)]))
    return np.concatenate(out).astype(np.int32)[None, :]


def turn_rows(order_row):
    m = np.maximum(order_row[0], 0).astype(np.float64)
    weight = np.where(order_row[0] == 0, 1.0, 2.0)
    sign = np.where(order_row[0] % 4 == 3, 1.0, -1.0)
    parts = np_high_low(np.cos(np.pi * m / NPHI) * weight) + np_high_low(np.sin(np.pi * m / NPHI) * weight)
    parts = parts + (weight.astype(jnp.bfloat16), sign.astype(jnp.bfloat16))
    return np.stack(parts + (np.zeros_like(parts[0]),) * 10)


def part_rows(part, bins, cycles_here):
    shape = (2 * bins * cycles_here, 4 * bins * cycles_here)
    row = lax.broadcasted_iota(jnp.int32, shape, 0)
    column = lax.broadcasted_iota(jnp.int32, shape, 1)
    cycle = lax.rem(row, cycles_here)
    bin_number = lax.rem(lax.div(row, cycles_here), bins)
    filter_number = lax.div(row, cycles_here * bins)
    return hot(column == ((filter_number * cycles_here + cycle) * 2 + part) * bins + bin_number)


def inverse_kernel(arrived_ref, slots_ref, turn_hbm, table_hbm, kappa_hbm, potential_hbm,
                   turn_ref, table_ref, wide_ref, kappa_ref, potential_ref, sems, out_sems):
    copies = [pltpu.make_async_copy(turn_hbm, turn_ref, sems.at[0])]
    quarter = NPHI // 4
    chunk = table_ref.shape[1]
    chunks = quarter // chunk
    part = table_ref.shape[0] // chunks
    for i in range(chunks):
        rows = pl.ds(i * part, part)
        copies.append(pltpu.make_async_copy(table_hbm.at[rows], table_ref.at[rows], sems.at[1 + i]))
    for copy in copies:
        copy.start()
    devices, slots = slots_ref.shape
    bins, cycles_here, _ = kappa_ref.shape
    order_count = part // 2
    per_slot = 2 * bins
    per_source = 2 * cycles_here
    wide_ref[...] = arrived_ref[...].astype(jnp.float32)
    turned = [jnp.transpose(wide_ref[pl.ds(i, devices, stride=per_source), :]) for i in range(per_source)]
    few, many = order_count // 4, order_count // 2
    starts = [0, padded(few), 2 * padded(few)]
    lane = lax.broadcasted_iota(jnp.int32, (1, turn_ref.shape[1]), 1)
    orders = jnp.where(lane < few, 4 * lane, -1)
    within = lane - starts[1]
    orders = jnp.where((within >= 0) & (within < few), 4 * within + 2, orders)
    within = lane - starts[2]
    orders = jnp.where((within >= 0) & (within < many), 2 * within + 1, orders)
    lefts, picks = [], []
    for t in range(slots):
        lefts.append(jnp.concatenate([x[t * per_slot : (t + 1) * per_slot, :] for x in turned], 0))
        picks.append(hot(slots_ref[:, t : t + 1] == orders))
    spectrum = dot(jnp.concatenate(lefts, 1).astype(jnp.bfloat16), jnp.concatenate(picks, 0))
    spectrum = spectrum.astype(jnp.bfloat16)
    real_in = dot(part_rows(0, bins, cycles_here), spectrum)
    imag_in = dot(part_rows(1, bins, cycles_here), spectrum)
    copies[0].wait()
    turn = turn_ref[...].astype(jnp.float32)
    odd = lax.rem(lax.rem(lax.broadcasted_iota(jnp.int32, real_in.shape, 0), cycles_here), 2) == 1
    turn_cos = jnp.where(odd, turn[0:1, :] + turn[1:2, :], turn[4:5, :])
    turn_sin = jnp.where(odd, turn[2:3, :] + turn[3:4, :], 0.0)
    real = real_in * turn_cos - imag_in * turn_sin
    imag = real_in * turn_sin + imag_in * turn_cos
    sign = turn[5:6, starts[2] :]
    count = real.shape[0]
    lefts = []
    for index, start in enumerate(starts):
        lanes = slice(start, start + (few if index < 2 else many))
        cos_rows, sin_rows = [real[:, lanes]], [imag[:, lanes]]
        if index == 2:
            cos_rows.append(imag[:, lanes] * sign[:, :many])
            sin_rows.append(-real[:, lanes] * sign[:, :many])
        for rows in (cos_rows, sin_rows):
            lefts.append(jnp.concatenate([y for x in rows for y in high_low(x)], 0))
    results = []
    for index in range(chunks):
        copies[1 + index].wait()
        row = index * part
        sums = []
        for at in range(3):
            height = few if at < 2 else many
            both = dot(lefts[2 * at], table_ref[row : row + height, :])
            both = both + dot(lefts[2 * at + 1], table_ref[row + height : row + 2 * height, :])
            row += 2 * height
            sums += [both[i : i + count, :] + both[i + count : i + 2 * count, :] for i in range(0, both.shape[0], 2 * count)]
        even, other = sums[0] + sums[1], sums[0] - sums[1]
        values = (even + sums[2], other + sums[3], even - sums[2], other - sums[3])
        for j, value in enumerate(values):
            lanes = pl.ds(j * quarter + index * chunk, chunk)
            for f, (out_ref, out_hbm) in enumerate(((kappa_ref, kappa_hbm), (potential_ref, potential_hbm))):
                for b in range(bins):
                    at = (f * bins + b) * cycles_here
                    out_ref[b, :, lanes] = value[at : at + cycles_here, :]
                copy = pltpu.make_async_copy(out_ref.at[:, :, lanes], out_hbm.at[:, :, lanes], out_sems.at[len(results)])
                copy.start()
                results.append(copy)
    for copy in results:
        copy.wait()


def in_hbm(x):
    return pltpu.with_memory_space_constraint(jnp.asarray(x), pltpu.HBM)


def params(orders):
    small = 14 if orders <= 512 else 56
    return pltpu.CompilerParams(vmem_limit_bytes=small * 1024 * 1024)


def per_device(weights, offsets, counts, block_ids, m_table, legendre):
    axes = ("blk", "y", "core")
    _, devices, capacity, bins, _ = weights.shape
    slots, degrees, cycles = legendre.shape
    orders = m_table.shape[0]
    groups = devices * capacity
    cycles_here = cycles // devices
    width = bins * cycles
    staged = legendre.size <= 4 * 1024 * 1024
    limits = params(orders)
    hbm = pl.BlockSpec(memory_space=pltpu.HBM)
    vmem = pl.BlockSpec(memory_space=pltpu.VMEM)

    def shaped(*shape, dtype=jnp.bfloat16):
        return jax.ShapeDtypeStruct(shape, dtype)

    rows = slot_rows(orders, slots)
    inner, outer = analysis_tables(orders)
    live = (capacity + 1) * devices // 2
    key_rows = -(-live // LANES) * 16
    shapes = [
        shaped(bins * live + key_rows, BLOCK),
        shaped(1, orders, dtype=jnp.int32),
        shaped(*rows.shape),
        shaped(*inner.shape),
        shaped(*outer.shape),
    ]
    operands = [
        weights.reshape(groups * bins, BLOCK),
        offsets.reshape(groups, BLOCK),
        counts,
        jnp.transpose(block_ids[0]),
        m_table,
        rows,
        inner,
        outer,
    ]
    ahead = slots * 5 // 6 if staged else 0
    if staged:
        shapes.append(shaped(ahead, degrees, cycles))
        operands.append(legendre)
    deposits, *shared = pl.pallas_call(
        functools.partial(first_kernel, slots, cycles_here * SEGMENTS, ahead),
        in_specs=[hbm] * len(operands),
        out_specs=(vmem,) * len(shapes),
        out_shape=tuple(shapes),
        scratch_shapes=[
            pltpu.VMEM((groups * bins, BLOCK), jnp.bfloat16),
            pltpu.VMEM((groups, BLOCK), jnp.int32),
            pltpu.VMEM((1, devices), jnp.int32),
            pltpu.VMEM((capacity, devices), jnp.int32),
            pltpu.VMEM((orders,), jnp.int32),
            pltpu.VMEM((groups * bins, BLOCK), jnp.float32),
            pltpu.VMEM((bins, live, BLOCK), jnp.bfloat16),
            pltpu.VMEM((live, BLOCK), jnp.float32),
            pltpu.SemaphoreType.DMA((len(operands),)),
        ],
        compiler_params=limits,
        name="deposit",
    )(*[in_hbm(x) for x in operands])
    early = shared.pop() if staged else None

    def swap(x, mask, odd_mask=None):
        masks = (mask, mask if odd_mask is None else odd_mask)
        return lax.ppermute(x, axes, [(i, i ^ masks[i % 2]) for i in range(devices)])

    other = swap(deposits, 1)
    cost = pl.CostEstimate(flops=8 * orders * 256 * bins * live, bytes_accessed=4 * orders * width, transcendentals=0)
    modes_shape = (width // LANES, orders, LANES)
    own, own_inner, own_outer, *late = pl.pallas_call(
        functools.partial(own_kernel, bins, live, cycles, ahead),
        in_specs=[vmem] * 5 + [hbm] * staged,
        out_specs=(vmem,) * (3 + staged),
        out_shape=(
            shaped(*modes_shape, dtype=jnp.float32),
            shaped(orders, inner.shape[1] // 2),
            shaped(orders, outer.shape[1] // 2),
        ) + (shaped(slots - ahead, degrees, cycles),) * staged,
        scratch_shapes=[pltpu.SemaphoreType.DMA] * staged,
        compiler_params=limits,
        cost_estimate=cost,
        name="own_groups",
    )(deposits, *shared, *[in_hbm(legendre)] * staged)

    basis = [early, *late] if staged else [legendre]

    groups_of_bits = bit_groups(devices)
    stages = len(groups_of_bits)
    gain, order = gain_column(degrees), interleave(cycles, cycles_here)
    blocks = devices // 2
    kernel, inputs = functools.partial(other_kernel, bins, live, cycles), (other, own_inner, own_outer, own)
    scratch = [pltpu.VMEM(modes_shape, jnp.float32)]
    responses = []
    for stage, bits in enumerate(groups_of_bits):
        ways = 1 << len(bits)
        blocks //= ways
        rows_here = blocks * 2 * slots
        kept, *sends = pl.pallas_call(
            kernel,
            in_specs=[vmem] * len(inputs),
            out_specs=(vmem,) * ways,
            out_shape=(shaped(rows_here, width, dtype=jnp.float32),) + (shaped(rows_here, width),) * (ways - 1),
            scratch_shapes=scratch,
            compiler_params=limits,
            name="merge" if stage else "other_groups",
        )(*inputs)
        sends, basis = lax.optimization_barrier((sends, basis))
        if stage == 0:
            order_of = send_order(ways)
            arrived = [swap(x, even << bits[0], odd << bits[0]) for x, (even, odd) in zip(sends, order_of)]
        else:
            arrived = [swap(x, (i + 1) << bits[0]) for i, x in reversed(list(enumerate(sends)))]
        first, last = (min(slots, slots * 2 * k * (2 * stages - k) // (2 * stages * stages)) for k in (stage, stage + 1))
        count = last - first
        shape = shaped(count, 2 * cycles, 2 * cycles)
        cost = pl.CostEstimate(
            flops=6 * count * degrees * cycles * cycles, bytes_accessed=2 * count * degrees * cycles, transcendentals=0
        )
        if staged:
            kernel, scratch = functools.partial(staged_response_kernel, first), []
        else:
            kernel = functools.partial(response_kernel, first)
            scratch = [pltpu.VMEM((count, degrees, cycles), jnp.bfloat16), pltpu.SemaphoreType.DMA((count,))]
        response = pl.pallas_call(
            kernel,
            in_specs=[vmem if staged else hbm] * len(basis) + [vmem] * 2,
            out_specs=vmem,
            out_shape=shape,
            scratch_shapes=scratch,
            compiler_params=limits,
            cost_estimate=cost,
            name="response",
        )(*basis if staged else [in_hbm(x) for x in basis], gain, order)
        *arrived, response = lax.optimization_barrier((*arrived, response))
        responses.append(response)
        kernel, inputs, scratch = functools.partial(merge_kernel, len(arrived)), (kept, *arrived), []

    outgoing = pl.pallas_call(
        functools.partial(synthesis_kernel, len(inputs) - 1, len(responses)),
        in_specs=[vmem] * (len(inputs) + len(responses) + 1),
        out_specs=vmem,
        out_shape=shaped(2 * cycles, 128),
        compiler_params=limits,
        name="synthesis",
    )(*inputs, *responses, slot_order(slots, bins))
    outgoing = outgoing.reshape(devices, 2 * cycles_here, 128)
    outgoing, held = lax.optimization_barrier((outgoing, m_table))
    arrived = lax.all_to_all(outgoing, axes, split_axis=0, concat_axis=0, tiled=True)
    arrived = arrived.reshape(2 * cycles, 128)
    if staged:
        arrived = pltpu.with_memory_space_constraint(arrived, pltpu.VMEM)

    lanes = order_lanes(orders)
    constants = [turn_rows(lanes), inverse_tables(orders)]
    chunks = NPHI // 4 // constants[-1].shape[1]
    map_shape = shaped(bins, cycles_here, NPHI, dtype=jnp.float32)
    return pl.pallas_call(
        inverse_kernel,
        in_specs=[vmem] * 2 + [hbm] * 2,
        out_specs=(hbm, hbm),
        out_shape=(map_shape, map_shape),
        scratch_shapes=[
            *[pltpu.VMEM(x.shape, x.dtype) for x in constants],
            pltpu.VMEM((2 * cycles, 128), jnp.float32),
            pltpu.VMEM(map_shape.shape, jnp.float32),
            pltpu.VMEM(map_shape.shape, jnp.float32),
            pltpu.SemaphoreType.DMA((1 + chunks,)),
            pltpu.SemaphoreType.DMA((8 * chunks,)),
        ],
        compiler_params=limits,
        name="inverse",
    )(arrived, held.reshape(devices, slots), *[in_hbm(x) for x in constants])


def solution(mesh):
    blocks, columns = mesh.devices.shape
    fine = Mesh(mesh.devices.reshape(blocks, columns // 2, 2), ("blk", "y", "core"))
    axes = ("blk", "y", "core")
    placed = (
        P(axes, None, None, None, None),
        P(axes, None, None, None),
        P(axes, None),
        P(axes, None, None),
        P(),
        P(axes, None, None),
    )
    return jax.shard_map(
        per_device,
        mesh=fine,
        in_specs=placed,
        out_specs=(P(None, axes, None), P(None, axes, None)),
        check_vma=False,
    )
```

```python
import functools

import jax
import jax.numpy as jnp
import numpy as np
from jax import lax
from jax.experimental import pallas as pl
from jax.experimental.pallas import tpu as pltpu
from jax.sharding import Mesh, PartitionSpec as P

NPHI = 4096
BLOCK = 128
SEGMENTS = NPHI // BLOCK
LANES = 128
CHUNK = 192

NT = (((1,), (1,)), ((), ()))
TN = (((0,), (0,)), ((), ()))


def dot(a, b, dims=(((1,), (0,)), ((), ()))):
    return lax.dot_general(a, b, dims, preferred_element_type=jnp.float32)


def high_low(x):
    high = x.astype(jnp.bfloat16)
    return high, (x - high.astype(jnp.float32)).astype(jnp.bfloat16)


def np_high_low(x):
    high = x.astype(np.float32).astype(jnp.bfloat16)
    return high, (x - high.astype(np.float64)).astype(np.float32).astype(jnp.bfloat16)


def analysis_tables(orders):
    m = np.arange(orders, dtype=np.int64)[:, None]
    p = np.arange(BLOCK, dtype=np.int64)[None, :]
    angle = (m * p % NPHI) * (2 * np.pi / NPHI)
    inner = np.concatenate(np_high_low(np.cos(angle)) + np_high_low(-np.sin(angle)), 1)
    half = np.arange(2 * SEGMENTS, dtype=np.int64)[None, :]
    steps = 2 * BLOCK * (half % SEGMENTS) + half // SEGMENTS
    angle = (m * steps % (2 * NPHI)) * (np.pi / NPHI)
    outer = np.concatenate(np_high_low(np.cos(angle) / NPHI) + np_high_low(-np.sin(angle) / NPHI), 1)
    return inner, outer


def bit_groups(devices):
    bits = list(range(1, devices.bit_length() - 1))
    return [bits[i : i + 2] for i in range(0, len(bits), 2)]


def positions(devices):
    order = [0]
    for group in bit_groups(devices):
        order = [p | (v << group[0]) for p in order for v in range(1 << len(group))]
    return order


def slot_rows(orders, slots):
    out = np.zeros((orders // 2, orders), np.float32)
    for block, position in enumerate(positions(orders // slots)):
        for slot in range(slots):
            out[block * slots + slot, position * slots + slot] = 1
    return out.astype(jnp.bfloat16)


def rolled(x, shift):
    return jnp.concatenate([x[:, shift:], x[:, :shift]], 1)


def exclusive_or(table, me, slots):
    orders = table.shape[1]
    block = lax.div(lax.broadcasted_iota(jnp.int32, table.shape, 1), slots)
    for bit in range((orders // slots).bit_length() - 1):
        shift = slots << bit
        swapped = jnp.where((block >> bit) % 2 == 0, rolled(table, shift), rolled(table, orders - shift))
        table = jnp.where(jnp.broadcast_to((me >> bit) & 1, table.shape) == 1, swapped, table)
    return table


def hot(condition):
    return jnp.where(condition, 1.0, 0.0).astype(jnp.bfloat16)


def twice(x):
    return jnp.concatenate([x, x], 1)


def first_kernel(slots, blocks_here, staged, w_hbm, off_hbm, cnt_hbm, ids_hbm, table_hbm, rows_hbm, inner_hbm, outer_hbm, *refs):
    if staged:
        legendre_hbm, *refs = refs
    out_ref, table_ref, rows_ref, inner_ref, outer_ref, *refs = refs
    if staged:
        legendre_ref, *refs = refs
    w_ref, off_ref, cnt_ref, ids_ref, flat_ref, wide_ref, live_w_ref, live_off_ref, sems = refs
    pairs = (
        (cnt_hbm, cnt_ref), (ids_hbm, ids_ref), (off_hbm, off_ref), (w_hbm, w_ref),
        (table_hbm, flat_ref), (rows_hbm, rows_ref), (inner_hbm, inner_ref), (outer_hbm, outer_ref),
    )
    if staged:
        pairs = pairs + ((legendre_hbm.at[pl.ds(0, staged)], legendre_ref),)
    copies = [pltpu.make_async_copy(a, b, sems.at[i]) for i, (a, b) in enumerate(pairs)]
    for copy in copies[:4]:
        copy.start()
    groups = off_ref.shape[0]
    capacity, devices = ids_ref.shape
    bins, live, _ = live_w_ref.shape
    pack = 16
    key_tiles = (out_ref.shape[0] - bins * live) // pack

    owner = lax.div(lax.broadcasted_iota(jnp.int32, (devices, groups), 1), capacity)
    source = lax.broadcasted_iota(jnp.int32, (devices, groups), 0)
    member = lax.rem(lax.broadcasted_iota(jnp.int32, (capacity, groups), 1), capacity)
    own_row = lax.broadcasted_iota(jnp.int32, (capacity, groups), 0) == member
    for copy in copies[:2]:
        copy.wait()
    counts = jnp.broadcast_to(cnt_ref[...].astype(jnp.float32), (8, devices)).astype(jnp.bfloat16)
    count = dot(counts, hot(source == owner))[0:1, :]
    before = dot(counts, hot(source < owner))[0:1, :]
    number = member[0:1, :].astype(jnp.float32)
    place = jnp.where(number < count, before + number, -1.0).astype(jnp.int32)
    packing = hot(lax.broadcasted_iota(jnp.int32, (key_tiles * LANES, groups), 0) == place)

    ids = dot(ids_ref[...].astype(jnp.float32).astype(jnp.bfloat16), hot(source == owner))
    ids = jnp.sum(jnp.where(own_row, ids, 0.0), axis=0, keepdims=True)
    block = ids.astype(jnp.int32) + owner[0:1, :] * blocks_here
    cycle = lax.div(block, SEGMENTS)
    phase = lax.rem(cycle, 2) * SEGMENTS + lax.rem(block, SEGMENTS)
    row = lax.broadcasted_iota(jnp.int32, (pack, groups), 0)
    keys = jnp.where(row == 0, lax.div(cycle, 16), jnp.where(row == 1, lax.rem(cycle, 16), phase))
    keys = dot(keys.astype(jnp.float32).astype(jnp.bfloat16), packing, NT).astype(jnp.bfloat16)
    for tile in range(key_tiles):
        out_ref[bins * live + tile * pack : bins * live + (tile + 1) * pack, :] = keys[:, tile * LANES : (tile + 1) * LANES]

    for copy in copies[2:4]:
        copy.wait()
    for copy in copies[4:]:
        copy.start()
    packing = packing[:live, :]
    live_off_ref[...] = dot(packing, off_ref[...].astype(jnp.float32).astype(jnp.bfloat16))
    wide_ref[...] = w_ref[...].astype(jnp.float32)
    for b in range(bins):
        live_w_ref[b] = dot(packing, wide_ref[pl.ds(b, groups, stride=bins), :].astype(jnp.bfloat16)).astype(jnp.bfloat16)

    pixel = lax.broadcasted_iota(jnp.int32, (pack, BLOCK), 0)
    pixels = [(pixel + pack * k).astype(jnp.float32).astype(jnp.bfloat16) for k in range(BLOCK // pack)]
    alone = [hot(pixel == i) for i in range(pack)]
    one = jnp.ones((pack, BLOCK), jnp.bfloat16)
    zero = jnp.zeros((pack, BLOCK), jnp.bfloat16)

    def deposit(step, carry):
        start = pl.multiple_of(step * pack, pack)
        weights = [live_w_ref[b, pl.ds(start, pack), :] for b in range(bins)]
        left, right = [], []
        for i in range(pack):
            left.append(jnp.concatenate([w * alone[i] for w in weights], 0))
            at = jnp.broadcast_to(live_off_ref[pl.ds(start + i, 1), :], (pack, BLOCK)).astype(jnp.bfloat16)
            right.append(jnp.concatenate([jnp.where(at == x, one, zero) for x in pixels], 0))
        out = dot(jnp.concatenate(left, 1), jnp.concatenate(right, 1), NT).astype(jnp.bfloat16)
        for b in range(bins):
            out_ref[pl.ds(pl.multiple_of(b * live + start, pack), pack), :] = out[b * pack : (b + 1) * pack, :]
        return carry

    lax.fori_loop(0, live // pack, deposit, 0, unroll=9)
    for copy in copies[4:8]:
        copy.wait()
    me = lax.axis_index("blk")
    for axis in ("y", "core"):
        me = me * lax.axis_size(axis) + lax.axis_index(axis)
    table_ref[...] = exclusive_or(flat_ref[...].reshape(table_ref.shape), me, slots)
    for copy in copies[8:]:
        copy.wait()


def add_modes(bins, groups, cycles, groups_ref, inner_ref, outer_ref, add):
    pack = 16
    keys = groups_ref[bins * groups :, :].astype(jnp.float32)
    keys = jnp.concatenate([keys[i * pack : (i + 1) * pack, :] for i in range(keys.shape[0] // pack)], 1)
    cycle = (keys[0:1, :groups] * 16.0 + keys[1:2, :groups]).astype(jnp.int32)
    phase = keys[2:3, :groups].astype(jnp.int32)
    cycle_hot = hot(lax.broadcasted_iota(jnp.int32, (cycles, groups), 0) == cycle)
    half_hot = hot(lax.broadcasted_iota(jnp.int32, (2 * SEGMENTS, groups), 0) == phase)
    phase_hot = jnp.concatenate([half_hot, half_hot], 0)
    deposits = [twice(groups_ref[b * groups : (b + 1) * groups, :]) for b in range(bins)]
    for start in range(0, inner_ref.shape[0], 2 * CHUNK):
        rows = slice(start, start + 2 * CHUNK)
        outer = dot(outer_ref[rows, :], phase_hot)
        outer_cos, outer_sin = outer[:CHUNK, :], outer[CHUNK:, :]
        for b, deposit in enumerate(deposits):
            inner = dot(inner_ref[rows, :], deposit, NT)
            inner_cos, inner_sin = inner[:CHUNK, :], inner[CHUNK:, :]
            real = inner_cos * outer_cos - inner_sin * outer_sin
            imag = inner_cos * outer_sin + inner_sin * outer_cos
            both = dot(jnp.concatenate([real, imag], 0).astype(jnp.bfloat16), cycle_hot, NT)
            for part in range(2):
                value = both[part * CHUNK : (part + 1) * CHUNK, :]
                for tile in range(cycles // LANES):
                    add(b * (cycles // LANES) + tile, start + part, value[:, tile * LANES : (tile + 1) * LANES])


def own_kernel(bins, groups, cycles, staged, groups_ref, table_ref, rows_ref, inner_ref, outer_ref, *refs):
    if staged:
        legendre_hbm, out_ref, inner_out, outer_out, legendre_ref, sem = refs
        late = pltpu.make_async_copy(legendre_hbm.at[pl.ds(staged, legendre_ref.shape[0])], legendre_ref, sem)
        late.start()
    else:
        out_ref, inner_out, outer_out = refs
    count, orders = rows_ref.shape
    held = hot(lax.broadcasted_iota(jnp.int32, (orders, orders), 0) == table_ref[...])
    for start in range(0, count, CHUNK):
        pick = dot(rows_ref[start : start + CHUNK, :], held, NT).astype(jnp.bfloat16)
        inner = dot(pick, inner_ref[...]).astype(jnp.bfloat16)
        outer = dot(pick, outer_ref[...]).astype(jnp.bfloat16)
        for part in range(2):
            rows = slice(2 * start + part * CHUNK, 2 * start + (part + 1) * CHUNK)
            inner_out[rows, :] = inner[:, part * 2 * BLOCK : (part + 1) * 2 * BLOCK]
            outer_out[rows, :] = outer[:, part * BLOCK : (part + 1) * BLOCK]

    def add(tile, first, value):
        out_ref.at[tile][pl.ds(first, value.shape[0], stride=2), :] = value

    add_modes(bins, groups, cycles, groups_ref, inner_out, outer_out, add)
    if staged:
        late.wait()


def split_sum(parts, tile, keep_ref, send_refs):
    rows = keep_ref.shape[0]
    lanes = slice(tile * LANES, (tile + 1) * LANES)
    for i, out_ref in enumerate((keep_ref, *send_refs)):
        value = sum(part(slice(i * rows, (i + 1) * rows), lanes) for part in parts)
        out_ref[:, lanes] = value.astype(out_ref.dtype)


def send_order(ways):
    return [(3, 3), (1, 2), (2, 1)] if ways == 4 else [(i, i) for i in range(1, ways)]


def other_kernel(bins, groups, cycles, groups_ref, inner_ref, outer_ref, own_ref, keep_ref, *refs):
    *send_refs, other_ref = refs

    def add(tile, first, value):
        other_ref.at[tile][pl.ds(first, value.shape[0], stride=2), :] = value

    add_modes(bins, groups, cycles, groups_ref, inner_ref, outer_ref, add)
    rows = keep_ref.shape[0]
    core = lax.axis_index("core")
    blocks = [(0, 0)] + send_order(len(send_refs) + 1)
    for (even, odd), out_ref in zip(blocks, (keep_ref, *send_refs)):
        first = even * rows if even == odd else pl.multiple_of((even + core * (odd - even)) * rows, rows)
        for tile in range(own_ref.shape[0]):
            value = own_ref[tile, pl.ds(first, rows), :] + other_ref[tile, pl.ds(first, rows), :]
            out_ref[:, tile * LANES : (tile + 1) * LANES] = value.astype(out_ref.dtype)


def merge_kernel(count, kept_ref, *refs):
    arrived, outs = refs[:count], refs[count:]
    for tile in range(kept_ref.shape[1] // LANES):
        parts = [lambda rows, lanes, ref=ref: ref[rows, lanes].astype(jnp.float32) for ref in (kept_ref, *arrived)]
        split_sum(parts, tile, outs[0], outs[1:])


def gain_column(degrees):
    l = np.arange(degrees, dtype=np.float32)
    return np.where(l > 0.5, np.float32(-20000.0) / np.maximum(l * (l + 1), np.float32(1)), np.float32(0)).astype(np.float32)[:, None] * np.ones((1, BLOCK), np.float32)


def interleave(cycles, cycles_here):
    out = np.zeros((2 * cycles, 2 * cycles), np.float32)
    for f in range(2):
        for c in range(cycles):
            out[f * cycles + c, (c // cycles_here * 2 + f) * cycles_here + c % cycles_here] = 1
    return out.astype(jnp.bfloat16)


def respond(basis, gain_ref, out_ref, slot):
    cycles = basis.shape[1]
    gain = jnp.concatenate([gain_ref[...]] * (cycles // BLOCK), 1)
    gained = (basis.astype(jnp.float32) * gain).astype(jnp.bfloat16)
    high, low = high_low(dot(basis, jnp.concatenate([basis, gained], 1), TN))
    out_ref[slot, :cycles, :] = high
    out_ref[slot, cycles:, :] = low


def staged_response_kernel(start, early_ref, late_ref, gain_ref, out_ref):
    early = early_ref.shape[0]
    for slot in range(out_ref.shape[0]):
        at = start + slot
        respond(early_ref[at] if at < early else late_ref[at - early], gain_ref, out_ref, slot)


def response_kernel(start, legendre_hbm, gain_ref, out_ref, legendre_ref, sems):
    count = out_ref.shape[0]
    copies = [pltpu.make_async_copy(legendre_hbm.at[start + i], legendre_ref.at[i], sems.at[i]) for i in range(count)]
    for copy in copies:
        copy.start()
    for slot in range(count):
        copies[slot].wait()
        respond(legendre_ref[slot], gain_ref, out_ref, slot)


def slot_order(slots, bins):
    out = np.zeros((slots * 2 * bins, slots * 2 * bins), np.float32)
    for b in range(bins):
        for c in range(2):
            for t in range(slots):
                out[(t * 2 + c) * bins + b, (b * slots + t) * 2 + c] = 1
    return out.astype(jnp.bfloat16)


def synthesis_kernel(arrivals, pieces, kept_ref, *refs):
    partials, refs = refs[:arrivals], refs[arrivals:]
    response_refs, (order_ref, columns_ref, out_ref) = refs[:pieces], refs[pieces:]
    cycles = response_refs[0].shape[1] // 2
    bins = kept_ref.shape[1] // cycles
    slots = kept_ref.shape[0] // 2
    responses = [ref.at[i] for ref in response_refs for i in range(ref.shape[0])]
    total = kept_ref[...]
    for ref in partials:
        total = total + ref[...].astype(jnp.float32)
    modes = jnp.concatenate([total[:, b * cycles : (b + 1) * cycles] for b in range(bins)], 0)
    high, low = high_low(modes)
    high = dot(order_ref[...], high)
    low = dot(order_ref[...], low)
    per_slot = 2 * bins
    parts = []
    for t in range(slots):
        rows = slice(t * per_slot, (t + 1) * per_slot)
        left = jnp.concatenate([high[rows, :], low[rows, :]], 0).astype(jnp.bfloat16)
        part = dot(twice(left), responses[t][...])
        parts.append(part[:per_slot, :] + part[per_slot:, :])
    parts.append(jnp.zeros((128 - slots * per_slot, 2 * cycles), jnp.float32))
    result = jnp.concatenate(parts, 0)
    result = dot(result.astype(jnp.bfloat16), columns_ref[...])
    out_ref[...] = jnp.transpose(result).astype(jnp.bfloat16)


def order_classes(orders):
    return [np.arange(0, orders, 4), np.arange(2, orders, 4), np.arange(1, orders, 2)]


def inverse_tables(orders):
    quarter = NPHI // 4
    k = np.arange(quarter, dtype=np.int64)[None, :]
    rows = []
    for m in order_classes(orders):
        angle = (m[:, None] * k % NPHI) * (2 * np.pi / NPHI)
        rows += [np.cos(angle), -np.sin(angle)]
    return np.concatenate(np.split(np.concatenate(rows), quarter // 512, axis=1)).astype(np.float32).astype(jnp.bfloat16)


def padded(count):
    return -(-count // LANES) * LANES


def order_lanes(orders):
    out = []
    for m in order_classes(orders):
        out.append(np.concatenate([m, np.full(padded(len(m)) - len(m), -1)]))
    return np.concatenate(out).astype(np.int32)[None, :]


def turn_rows(order_row):
    m = np.maximum(order_row[0], 0).astype(np.float64)
    weight = np.where(order_row[0] == 0, 1.0, 2.0)
    sign = np.where(order_row[0] % 4 == 3, 1.0, -1.0)
    parts = np_high_low(np.cos(np.pi * m / NPHI) * weight) + np_high_low(np.sin(np.pi * m / NPHI) * weight)
    parts = parts + (weight.astype(jnp.bfloat16), sign.astype(jnp.bfloat16))
    return np.stack(parts + (np.zeros_like(parts[0]),) * 10)


def part_rows(part, bins, cycles_here):
    shape = (2 * bins * cycles_here, 4 * bins * cycles_here)
    row = lax.broadcasted_iota(jnp.int32, shape, 0)
    column = lax.broadcasted_iota(jnp.int32, shape, 1)
    cycle = lax.rem(row, cycles_here)
    bin_number = lax.rem(lax.div(row, cycles_here), bins)
    filter_number = lax.div(row, cycles_here * bins)
    return hot(column == ((filter_number * cycles_here + cycle) * 2 + part) * bins + bin_number)


def inverse_kernel(arrived_ref, slots_ref, turn_hbm, table_hbm, kappa_hbm, potential_hbm,
                   turn_ref, table_ref, wide_ref, kappa_ref, potential_ref, sems, out_sems):
    copies = [pltpu.make_async_copy(turn_hbm, turn_ref, sems.at[0])]
    quarter = NPHI // 4
    chunk = table_ref.shape[1]
    chunks = quarter // chunk
    part = table_ref.shape[0] // chunks
    for i in range(chunks):
        rows = pl.ds(i * part, part)
        copies.append(pltpu.make_async_copy(table_hbm.at[rows], table_ref.at[rows], sems.at[1 + i]))
    for copy in copies:
        copy.start()
    devices, slots = slots_ref.shape
    bins, cycles_here, _ = kappa_ref.shape
    order_count = part // 2
    per_slot = 2 * bins
    per_source = 2 * cycles_here
    wide_ref[...] = arrived_ref[...].astype(jnp.float32)
    turned = [jnp.transpose(wide_ref[pl.ds(i, devices, stride=per_source), :]) for i in range(per_source)]
    few, many = order_count // 4, order_count // 2
    starts = [0, padded(few), 2 * padded(few)]
    lane = lax.broadcasted_iota(jnp.int32, (1, turn_ref.shape[1]), 1)
    orders = jnp.where(lane < few, 4 * lane, -1)
    within = lane - starts[1]
    orders = jnp.where((within >= 0) & (within < few), 4 * within + 2, orders)
    within = lane - starts[2]
    orders = jnp.where((within >= 0) & (within < many), 2 * within + 1, orders)
    lefts, picks = [], []
    for t in range(slots):
        lefts.append(jnp.concatenate([x[t * per_slot : (t + 1) * per_slot, :] for x in turned], 0))
        picks.append(hot(slots_ref[:, t : t + 1] == orders))
    spectrum = dot(jnp.concatenate(lefts, 1).astype(jnp.bfloat16), jnp.concatenate(picks, 0))
    spectrum = spectrum.astype(jnp.bfloat16)
    real_in = dot(part_rows(0, bins, cycles_here), spectrum)
    imag_in = dot(part_rows(1, bins, cycles_here), spectrum)
    copies[0].wait()
    turn = turn_ref[...].astype(jnp.float32)
    odd = lax.rem(lax.rem(lax.broadcasted_iota(jnp.int32, real_in.shape, 0), cycles_here), 2) == 1
    turn_cos = jnp.where(odd, turn[0:1, :] + turn[1:2, :], turn[4:5, :])
    turn_sin = jnp.where(odd, turn[2:3, :] + turn[3:4, :], 0.0)
    real = real_in * turn_cos - imag_in * turn_sin
    imag = real_in * turn_sin + imag_in * turn_cos
    sign = turn[5:6, starts[2] :]
    count = real.shape[0]
    lefts = []
    for index, start in enumerate(starts):
        lanes = slice(start, start + (few if index < 2 else many))
        cos_rows, sin_rows = [real[:, lanes]], [imag[:, lanes]]
        if index == 2:
            cos_rows.append(imag[:, lanes] * sign[:, :many])
            sin_rows.append(-real[:, lanes] * sign[:, :many])
        for rows in (cos_rows, sin_rows):
            lefts.append(jnp.concatenate([y for x in rows for y in high_low(x)], 0))
    results = []
    for index in range(chunks):
        copies[1 + index].wait()
        row = index * part
        sums = []
        for at in range(3):
            height = few if at < 2 else many
            both = dot(lefts[2 * at], table_ref[row : row + height, :])
            both = both + dot(lefts[2 * at + 1], table_ref[row + height : row + 2 * height, :])
            row += 2 * height
            sums += [both[i : i + count, :] + both[i + count : i + 2 * count, :] for i in range(0, both.shape[0], 2 * count)]
        even, other = sums[0] + sums[1], sums[0] - sums[1]
        values = (even + sums[2], other + sums[3], even - sums[2], other - sums[3])
        for j, value in enumerate(values):
            lanes = pl.ds(j * quarter + index * chunk, chunk)
            for f, (out_ref, out_hbm) in enumerate(((kappa_ref, kappa_hbm), (potential_ref, potential_hbm))):
                for b in range(bins):
                    at = (f * bins + b) * cycles_here
                    out_ref[b, :, lanes] = value[at : at + cycles_here, :]
                copy = pltpu.make_async_copy(out_ref.at[:, :, lanes], out_hbm.at[:, :, lanes], out_sems.at[len(results)])
                copy.start()
                results.append(copy)
    for copy in results:
        copy.wait()


def in_hbm(x):
    return pltpu.with_memory_space_constraint(jnp.asarray(x), pltpu.HBM)


def params(orders):
    small = 14 if orders <= 512 else 56
    return pltpu.CompilerParams(vmem_limit_bytes=small * 1024 * 1024)


def per_device(weights, offsets, counts, block_ids, m_table, legendre):
    axes = ("blk", "y", "core")
    _, devices, capacity, bins, _ = weights.shape
    slots, degrees, cycles = legendre.shape
    orders = m_table.shape[0]
    groups = devices * capacity
    cycles_here = cycles // devices
    width = bins * cycles
    staged = legendre.size <= 4 * 1024 * 1024
    limits = params(orders)
    hbm = pl.BlockSpec(memory_space=pltpu.HBM)
    vmem = pl.BlockSpec(memory_space=pltpu.VMEM)

    def shaped(*shape, dtype=jnp.bfloat16):
        return jax.ShapeDtypeStruct(shape, dtype)

    rows = slot_rows(orders, slots)
    inner, outer = analysis_tables(orders)
    live = (capacity + 1) * devices // 2
    key_rows = -(-live // LANES) * 16
    shapes = [
        shaped(bins * live + key_rows, BLOCK),
        shaped(1, orders, dtype=jnp.int32),
        shaped(*rows.shape),
        shaped(*inner.shape),
        shaped(*outer.shape),
    ]
    operands = [
        weights.reshape(groups * bins, BLOCK),
        offsets.reshape(groups, BLOCK),
        counts,
        jnp.transpose(block_ids[0]),
        m_table,
        rows,
        inner,
        outer,
    ]
    ahead = slots * 5 // 6 if staged else 0
    if staged:
        shapes.append(shaped(ahead, degrees, cycles))
        operands.append(legendre)
    deposits, *shared = pl.pallas_call(
        functools.partial(first_kernel, slots, cycles_here * SEGMENTS, ahead),
        in_specs=[hbm] * len(operands),
        out_specs=(vmem,) * len(shapes),
        out_shape=tuple(shapes),
        scratch_shapes=[
            pltpu.VMEM((groups * bins, BLOCK), jnp.bfloat16),
            pltpu.VMEM((groups, BLOCK), jnp.int32),
            pltpu.VMEM((1, devices), jnp.int32),
            pltpu.VMEM((capacity, devices), jnp.int32),
            pltpu.VMEM((orders,), jnp.int32),
            pltpu.VMEM((groups * bins, BLOCK), jnp.float32),
            pltpu.VMEM((bins, live, BLOCK), jnp.bfloat16),
            pltpu.VMEM((live, BLOCK), jnp.float32),
            pltpu.SemaphoreType.DMA((len(operands),)),
        ],
        compiler_params=limits,
        name="deposit",
    )(*[in_hbm(x) for x in operands])
    early = shared.pop() if staged else None

    def swap(x, mask, odd_mask=None):
        masks = (mask, mask if odd_mask is None else odd_mask)
        return lax.ppermute(x, axes, [(i, i ^ masks[i % 2]) for i in range(devices)])

    other = swap(deposits, 1)
    cost = pl.CostEstimate(flops=8 * orders * 256 * bins * live, bytes_accessed=4 * orders * width, transcendentals=0)
    modes_shape = (width // LANES, orders, LANES)
    own, own_inner, own_outer, *late = pl.pallas_call(
        functools.partial(own_kernel, bins, live, cycles, ahead),
        in_specs=[vmem] * 5 + [hbm] * staged,
        out_specs=(vmem,) * (3 + staged),
        out_shape=(
            shaped(*modes_shape, dtype=jnp.float32),
            shaped(orders, inner.shape[1] // 2),
            shaped(orders, outer.shape[1] // 2),
        ) + (shaped(slots - ahead, degrees, cycles),) * staged,
        scratch_shapes=[pltpu.SemaphoreType.DMA] * staged,
        compiler_params=limits,
        cost_estimate=cost,
        name="own_groups",
    )(deposits, *shared, *[in_hbm(legendre)] * staged)

    basis = [early, *late] if staged else [legendre]

    groups_of_bits = bit_groups(devices)
    stages = len(groups_of_bits)
    gain, order = gain_column(degrees), interleave(cycles, cycles_here)
    blocks = devices // 2
    kernel, inputs = functools.partial(other_kernel, bins, live, cycles), (other, own_inner, own_outer, own)
    scratch = [pltpu.VMEM(modes_shape, jnp.float32)]
    responses = []
    for stage, bits in enumerate(groups_of_bits):
        ways = 1 << len(bits)
        blocks //= ways
        rows_here = blocks * 2 * slots
        kept, *sends = pl.pallas_call(
            kernel,
            in_specs=[vmem] * len(inputs),
            out_specs=(vmem,) * ways,
            out_shape=(shaped(rows_here, width, dtype=jnp.float32),) + (shaped(rows_here, width),) * (ways - 1),
            scratch_shapes=scratch,
            compiler_params=limits,
            name="merge" if stage else "other_groups",
        )(*inputs)
        sends, basis = lax.optimization_barrier((sends, basis))
        if stage == 0:
            order_of = send_order(ways)
            arrived = [swap(x, even << bits[0], odd << bits[0]) for x, (even, odd) in zip(sends, order_of)]
        else:
            arrived = [swap(x, (i + 1) << bits[0]) for i, x in reversed(list(enumerate(sends)))]
        first, last = (-(-slots * k * (2 * stages + 1 - k) // (stages * (stages + 1))) for k in (stage, stage + 1))
        count = last - first
        shape = shaped(count, 2 * cycles, 2 * cycles)
        cost = pl.CostEstimate(
            flops=6 * count * degrees * cycles * cycles, bytes_accessed=2 * count * degrees * cycles, transcendentals=0
        )
        if staged:
            kernel, scratch = functools.partial(staged_response_kernel, first), []
        else:
            kernel = functools.partial(response_kernel, first)
            scratch = [pltpu.VMEM((count, degrees, cycles), jnp.bfloat16), pltpu.SemaphoreType.DMA((count,))]
        response = pl.pallas_call(
            kernel,
            in_specs=[vmem if staged else hbm] * len(basis) + [vmem],
            out_specs=vmem,
            out_shape=shape,
            scratch_shapes=scratch,
            compiler_params=limits,
            cost_estimate=cost,
            name="response",
        )(*basis if staged else [in_hbm(x) for x in basis], gain)
        *arrived, response = lax.optimization_barrier((*arrived, response))
        responses.append(response)
        kernel, inputs, scratch = functools.partial(merge_kernel, len(arrived)), (kept, *arrived), []

    outgoing = pl.pallas_call(
        functools.partial(synthesis_kernel, len(inputs) - 1, len(responses)),
        in_specs=[vmem] * (len(inputs) + len(responses) + 2),
        out_specs=vmem,
        out_shape=shaped(2 * cycles, 128),
        compiler_params=limits,
        name="synthesis",
    )(*inputs, *responses, slot_order(slots, bins), order)
    outgoing = outgoing.reshape(devices, 2 * cycles_here, 128)
    outgoing, held = lax.optimization_barrier((outgoing, m_table))
    arrived = lax.all_to_all(outgoing, axes, split_axis=0, concat_axis=0, tiled=True)
    arrived = arrived.reshape(2 * cycles, 128)
    if staged:
        arrived = pltpu.with_memory_space_constraint(arrived, pltpu.VMEM)

    lanes = order_lanes(orders)
    constants = [turn_rows(lanes), inverse_tables(orders)]
    chunks = NPHI // 4 // constants[-1].shape[1]
    map_shape = shaped(bins, cycles_here, NPHI, dtype=jnp.float32)
    return pl.pallas_call(
        inverse_kernel,
        in_specs=[vmem] * 2 + [hbm] * 2,
        out_specs=(hbm, hbm),
        out_shape=(map_shape, map_shape),
        scratch_shapes=[
            *[pltpu.VMEM(x.shape, x.dtype) for x in constants],
            pltpu.VMEM((2 * cycles, 128), jnp.float32),
            pltpu.VMEM(map_shape.shape, jnp.float32),
            pltpu.VMEM(map_shape.shape, jnp.float32),
            pltpu.SemaphoreType.DMA((1 + chunks,)),
            pltpu.SemaphoreType.DMA((8 * chunks,)),
        ],
        compiler_params=limits,
        name="inverse",
    )(arrived, held.reshape(devices, slots), *[in_hbm(x) for x in constants])


def solution(mesh):
    blocks, columns = mesh.devices.shape
    fine = Mesh(mesh.devices.reshape(blocks, columns // 2, 2), ("blk", "y", "core"))
    axes = ("blk", "y", "core")
    placed = (
        P(axes, None, None, None, None),
        P(axes, None, None, None),
        P(axes, None),
        P(axes, None, None),
        P(),
        P(axes, None, None),
    )
    return jax.shard_map(
        per_device,
        mesh=fine,
        in_specs=placed,
        out_specs=(P(None, axes, None), P(None, axes, None)),
        check_vma=False,
    )
```

```python
import functools

import jax
import jax.numpy as jnp
import numpy as np
from jax import lax
from jax.experimental import pallas as pl
from jax.experimental.pallas import tpu as pltpu
from jax.sharding import Mesh, PartitionSpec as P

NPHI = 4096
BLOCK = 128
SEGMENTS = NPHI // BLOCK
LANES = 128
CHUNK = 192

NT = (((1,), (1,)), ((), ()))
TN = (((0,), (0,)), ((), ()))


def dot(a, b, dims=(((1,), (0,)), ((), ()))):
    return lax.dot_general(a, b, dims, preferred_element_type=jnp.float32)


def high_low(x):
    high = x.astype(jnp.bfloat16)
    return high, (x - high.astype(jnp.float32)).astype(jnp.bfloat16)


def np_high_low(x):
    high = x.astype(np.float32).astype(jnp.bfloat16)
    return high, (x - high.astype(np.float64)).astype(np.float32).astype(jnp.bfloat16)


def analysis_tables(orders):
    m = np.arange(orders, dtype=np.int64)[:, None]
    p = np.arange(BLOCK, dtype=np.int64)[None, :]
    angle = (m * p % NPHI) * (2 * np.pi / NPHI)
    inner = np.concatenate(np_high_low(np.cos(angle)) + np_high_low(-np.sin(angle)), 1)
    half = np.arange(2 * SEGMENTS, dtype=np.int64)[None, :]
    steps = 2 * BLOCK * (half % SEGMENTS) + half // SEGMENTS
    angle = (m * steps % (2 * NPHI)) * (np.pi / NPHI)
    outer = np.concatenate(np_high_low(np.cos(angle) / NPHI) + np_high_low(-np.sin(angle) / NPHI), 1)
    return inner, outer


def bit_groups(devices):
    bits = list(range(1, devices.bit_length() - 1))
    return [bits[i : i + 2] for i in range(0, len(bits), 2)]


def positions(devices):
    order = [0]
    for group in bit_groups(devices):
        order = [p | (v << group[0]) for p in order for v in range(1 << len(group))]
    return order


def slot_rows(orders, slots):
    out = np.zeros((orders // 2, orders), np.float32)
    for block, position in enumerate(positions(orders // slots)):
        for slot in range(slots):
            out[block * slots + slot, position * slots + slot] = 1
    return out.astype(jnp.bfloat16)


def rolled(x, shift):
    return jnp.concatenate([x[:, shift:], x[:, :shift]], 1)


def exclusive_or(table, me, slots):
    orders = table.shape[1]
    block = lax.div(lax.broadcasted_iota(jnp.int32, table.shape, 1), slots)
    for bit in range((orders // slots).bit_length() - 1):
        shift = slots << bit
        swapped = jnp.where((block >> bit) % 2 == 0, rolled(table, shift), rolled(table, orders - shift))
        table = jnp.where(jnp.broadcast_to((me >> bit) & 1, table.shape) == 1, swapped, table)
    return table


def hot(condition):
    return jnp.where(condition, 1.0, 0.0).astype(jnp.bfloat16)


def twice(x):
    return jnp.concatenate([x, x], 1)


def first_kernel(slots, blocks_here, staged, w_hbm, off_hbm, cnt_hbm, ids_hbm, table_hbm, rows_hbm, inner_hbm, outer_hbm, *refs):
    if staged:
        legendre_hbm, *refs = refs
    out_ref, table_ref, rows_ref, inner_ref, outer_ref, *refs = refs
    if staged:
        legendre_ref, *refs = refs
    w_ref, off_ref, cnt_ref, ids_ref, flat_ref, wide_ref, live_w_ref, live_off_ref, sems = refs
    pairs = (
        (cnt_hbm, cnt_ref), (ids_hbm, ids_ref), (off_hbm, off_ref), (w_hbm, w_ref),
        (table_hbm, flat_ref), (rows_hbm, rows_ref), (inner_hbm, inner_ref), (outer_hbm, outer_ref),
    )
    if staged:
        pairs = pairs + ((legendre_hbm.at[pl.ds(0, staged)], legendre_ref),)
    copies = [pltpu.make_async_copy(a, b, sems.at[i]) for i, (a, b) in enumerate(pairs)]
    for copy in copies[:4]:
        copy.start()
    groups = off_ref.shape[0]
    capacity, devices = ids_ref.shape
    bins, live, _ = live_w_ref.shape
    pack = 16
    key_tiles = (out_ref.shape[0] - bins * live) // pack

    owner = lax.div(lax.broadcasted_iota(jnp.int32, (devices, groups), 1), capacity)
    source = lax.broadcasted_iota(jnp.int32, (devices, groups), 0)
    member = lax.rem(lax.broadcasted_iota(jnp.int32, (capacity, groups), 1), capacity)
    own_row = lax.broadcasted_iota(jnp.int32, (capacity, groups), 0) == member
    for copy in copies[:2]:
        copy.wait()
    counts = jnp.broadcast_to(cnt_ref[...].astype(jnp.float32), (8, devices)).astype(jnp.bfloat16)
    count = dot(counts, hot(source == owner))[0:1, :]
    before = dot(counts, hot(source < owner))[0:1, :]
    number = member[0:1, :].astype(jnp.float32)
    place = jnp.where(number < count, before + number, -1.0).astype(jnp.int32)
    packing = hot(lax.broadcasted_iota(jnp.int32, (key_tiles * LANES, groups), 0) == place)

    ids = dot(ids_ref[...].astype(jnp.float32).astype(jnp.bfloat16), hot(source == owner))
    ids = jnp.sum(jnp.where(own_row, ids, 0.0), axis=0, keepdims=True)
    block = ids.astype(jnp.int32) + owner[0:1, :] * blocks_here
    cycle = lax.div(block, SEGMENTS)
    phase = lax.rem(cycle, 2) * SEGMENTS + lax.rem(block, SEGMENTS)
    row = lax.broadcasted_iota(jnp.int32, (pack, groups), 0)
    keys = jnp.where(row == 0, lax.div(cycle, 16), jnp.where(row == 1, lax.rem(cycle, 16), phase))
    keys = dot(keys.astype(jnp.float32).astype(jnp.bfloat16), packing, NT).astype(jnp.bfloat16)
    for tile in range(key_tiles):
        out_ref[bins * live + tile * pack : bins * live + (tile + 1) * pack, :] = keys[:, tile * LANES : (tile + 1) * LANES]

    for copy in copies[2:4]:
        copy.wait()
    for copy in copies[4:]:
        copy.start()
    packing = packing[:live, :]
    live_off_ref[...] = dot(packing, off_ref[...].astype(jnp.float32).astype(jnp.bfloat16))
    wide_ref[...] = w_ref[...].astype(jnp.float32)
    for b in range(bins):
        live_w_ref[b] = dot(packing, wide_ref[pl.ds(b, groups, stride=bins), :].astype(jnp.bfloat16)).astype(jnp.bfloat16)

    pixel = lax.broadcasted_iota(jnp.int32, (pack, BLOCK), 0)
    pixels = [(pixel + pack * k).astype(jnp.float32).astype(jnp.bfloat16) for k in range(BLOCK // pack)]
    alone = [hot(pixel == i) for i in range(pack)]
    one = jnp.ones((pack, BLOCK), jnp.bfloat16)
    zero = jnp.zeros((pack, BLOCK), jnp.bfloat16)

    def deposit(step, carry):
        start = pl.multiple_of(step * pack, pack)
        weights = [live_w_ref[b, pl.ds(start, pack), :] for b in range(bins)]
        left, right = [], []
        for i in range(pack):
            left.append(jnp.concatenate([w * alone[i] for w in weights], 0))
            at = jnp.broadcast_to(live_off_ref[pl.ds(start + i, 1), :], (pack, BLOCK)).astype(jnp.bfloat16)
            right.append(jnp.concatenate([jnp.where(at == x, one, zero) for x in pixels], 0))
        out = dot(jnp.concatenate(left, 1), jnp.concatenate(right, 1), NT).astype(jnp.bfloat16)
        for b in range(bins):
            out_ref[pl.ds(pl.multiple_of(b * live + start, pack), pack), :] = out[b * pack : (b + 1) * pack, :]
        return carry

    lax.fori_loop(0, live // pack, deposit, 0, unroll=9)
    for copy in copies[4:8]:
        copy.wait()
    me = lax.axis_index("blk")
    for axis in ("y", "core"):
        me = me * lax.axis_size(axis) + lax.axis_index(axis)
    table_ref[...] = exclusive_or(flat_ref[...].reshape(table_ref.shape), me, slots)
    for copy in copies[8:]:
        copy.wait()


def add_modes(bins, groups, cycles, groups_ref, inner_ref, outer_ref, add):
    pack = 16
    keys = groups_ref[bins * groups :, :].astype(jnp.float32)
    keys = jnp.concatenate([keys[i * pack : (i + 1) * pack, :] for i in range(keys.shape[0] // pack)], 1)
    cycle = (keys[0:1, :groups] * 16.0 + keys[1:2, :groups]).astype(jnp.int32)
    phase = keys[2:3, :groups].astype(jnp.int32)
    cycle_hot = hot(lax.broadcasted_iota(jnp.int32, (cycles, groups), 0) == cycle)
    half_hot = hot(lax.broadcasted_iota(jnp.int32, (2 * SEGMENTS, groups), 0) == phase)
    phase_hot = jnp.concatenate([half_hot, half_hot], 0)
    deposits = [twice(groups_ref[b * groups : (b + 1) * groups, :]) for b in range(bins)]
    for start in range(0, inner_ref.shape[0], 2 * CHUNK):
        rows = slice(start, start + 2 * CHUNK)
        outer = dot(outer_ref[rows, :], phase_hot)
        outer_cos, outer_sin = outer[:CHUNK, :], outer[CHUNK:, :]
        for b, deposit in enumerate(deposits):
            inner = dot(inner_ref[rows, :], deposit, NT)
            inner_cos, inner_sin = inner[:CHUNK, :], inner[CHUNK:, :]
            real = inner_cos * outer_cos - inner_sin * outer_sin
            imag = inner_cos * outer_sin + inner_sin * outer_cos
            both = dot(jnp.concatenate([real, imag], 0).astype(jnp.bfloat16), cycle_hot, NT)
            for part in range(2):
                value = both[part * CHUNK : (part + 1) * CHUNK, :]
                for tile in range(cycles // LANES):
                    add(b * (cycles // LANES) + tile, start + part, value[:, tile * LANES : (tile + 1) * LANES])


def own_kernel(bins, groups, cycles, staged, groups_ref, table_ref, rows_ref, inner_ref, outer_ref, *refs):
    if staged:
        legendre_hbm, out_ref, inner_out, outer_out, legendre_ref, sem = refs
        late = pltpu.make_async_copy(legendre_hbm.at[pl.ds(staged, legendre_ref.shape[0])], legendre_ref, sem)
        late.start()
    else:
        out_ref, inner_out, outer_out = refs
    count, orders = rows_ref.shape
    held = hot(lax.broadcasted_iota(jnp.int32, (orders, orders), 0) == table_ref[...])
    for start in range(0, count, CHUNK):
        pick = dot(rows_ref[start : start + CHUNK, :], held, NT).astype(jnp.bfloat16)
        inner = dot(pick, inner_ref[...]).astype(jnp.bfloat16)
        outer = dot(pick, outer_ref[...]).astype(jnp.bfloat16)
        for part in range(2):
            rows = slice(2 * start + part * CHUNK, 2 * start + (part + 1) * CHUNK)
            inner_out[rows, :] = inner[:, part * 2 * BLOCK : (part + 1) * 2 * BLOCK]
            outer_out[rows, :] = outer[:, part * BLOCK : (part + 1) * BLOCK]

    def add(tile, first, value):
        out_ref.at[tile][pl.ds(first, value.shape[0], stride=2), :] = value

    add_modes(bins, groups, cycles, groups_ref, inner_out, outer_out, add)
    if staged:
        late.wait()


def split_sum(parts, tile, keep_ref, send_refs):
    rows = keep_ref.shape[0]
    lanes = slice(tile * LANES, (tile + 1) * LANES)
    for i, out_ref in enumerate((keep_ref, *send_refs)):
        value = sum(part(slice(i * rows, (i + 1) * rows), lanes) for part in parts)
        out_ref[:, lanes] = value.astype(out_ref.dtype)


def send_order(ways):
    return [(1, 2), (2, 1), (3, 3)] if ways == 4 else [(i, i) for i in range(1, ways)]


def other_kernel(bins, groups, cycles, groups_ref, inner_ref, outer_ref, own_ref, keep_ref, *refs):
    *send_refs, other_ref = refs

    def add(tile, first, value):
        other_ref.at[tile][pl.ds(first, value.shape[0], stride=2), :] = value

    add_modes(bins, groups, cycles, groups_ref, inner_ref, outer_ref, add)
    rows = keep_ref.shape[0]
    core = lax.axis_index("core")
    blocks = [(0, 0)] + send_order(len(send_refs) + 1)
    for (even, odd), out_ref in zip(blocks, (keep_ref, *send_refs)):
        first = even * rows if even == odd else pl.multiple_of((even + core * (odd - even)) * rows, rows)
        for tile in range(own_ref.shape[0]):
            value = own_ref[tile, pl.ds(first, rows), :] + other_ref[tile, pl.ds(first, rows), :]
            out_ref[:, tile * LANES : (tile + 1) * LANES] = value.astype(out_ref.dtype)


def merge_kernel(count, kept_ref, *refs):
    arrived, outs = refs[:count], refs[count:]
    for tile in range(kept_ref.shape[1] // LANES):
        parts = [lambda rows, lanes, ref=ref: ref[rows, lanes].astype(jnp.float32) for ref in (kept_ref, *arrived)]
        split_sum(parts, tile, outs[0], outs[1:])


def gain_column(degrees):
    l = np.arange(degrees, dtype=np.float32)
    return np.where(l > 0.5, np.float32(-20000.0) / np.maximum(l * (l + 1), np.float32(1)), np.float32(0)).astype(np.float32)[:, None] * np.ones((1, BLOCK), np.float32)


def interleave(cycles, cycles_here):
    out = np.zeros((2 * cycles, 2 * cycles), np.float32)
    for f in range(2):
        for c in range(cycles):
            out[f * cycles + c, (c // cycles_here * 2 + f) * cycles_here + c % cycles_here] = 1
    return out.astype(jnp.bfloat16)


def respond(basis, gain_ref, order_ref, out_ref, slot):
    cycles = basis.shape[1]
    gain = jnp.concatenate([gain_ref[...]] * (cycles // BLOCK), 1)
    gained = (basis.astype(jnp.float32) * gain).astype(jnp.bfloat16)
    high, low = high_low(dot(basis, jnp.concatenate([basis, gained], 1), TN))
    out_ref[slot] = dot(jnp.concatenate([high, low], 0), order_ref[...]).astype(jnp.bfloat16)


def staged_response_kernel(start, early_ref, late_ref, gain_ref, order_ref, out_ref):
    early = early_ref.shape[0]
    for slot in range(out_ref.shape[0]):
        at = start + slot
        respond(early_ref[at] if at < early else late_ref[at - early], gain_ref, order_ref, out_ref, slot)


def response_kernel(start, legendre_hbm, gain_ref, order_ref, out_ref, legendre_ref, sems):
    count = out_ref.shape[0]
    copies = [pltpu.make_async_copy(legendre_hbm.at[start + i], legendre_ref.at[i], sems.at[i]) for i in range(count)]
    for copy in copies:
        copy.start()
    for slot in range(count):
        copies[slot].wait()
        respond(legendre_ref[slot], gain_ref, order_ref, out_ref, slot)


def slot_order(slots, bins):
    out = np.zeros((slots * 2 * bins, slots * 2 * bins), np.float32)
    for b in range(bins):
        for c in range(2):
            for t in range(slots):
                out[(t * 2 + c) * bins + b, (b * slots + t) * 2 + c] = 1
    return out.astype(jnp.bfloat16)


def synthesis_kernel(arrivals, pieces, kept_ref, *refs):
    partials, refs = refs[:arrivals], refs[arrivals:]
    response_refs, (order_ref, out_ref) = refs[:pieces], refs[pieces:]
    cycles = response_refs[0].shape[1] // 2
    bins = kept_ref.shape[1] // cycles
    slots = kept_ref.shape[0] // 2
    responses = [ref.at[i] for ref in response_refs for i in range(ref.shape[0])]
    total = kept_ref[...]
    for ref in partials:
        total = total + ref[...].astype(jnp.float32)
    modes = jnp.concatenate([total[:, b * cycles : (b + 1) * cycles] for b in range(bins)], 0)
    high, low = high_low(modes)
    high = dot(order_ref[...], high)
    low = dot(order_ref[...], low)
    per_slot = 2 * bins
    parts = []
    for t in range(slots):
        rows = slice(t * per_slot, (t + 1) * per_slot)
        left = jnp.concatenate([high[rows, :], low[rows, :]], 0).astype(jnp.bfloat16)
        part = dot(twice(left), responses[t][...])
        parts.append(part[:per_slot, :] + part[per_slot:, :])
    parts.append(jnp.zeros((128 - slots * per_slot, 2 * cycles), jnp.float32))
    result = jnp.concatenate(parts, 0)
    out_ref[...] = jnp.transpose(result).astype(jnp.bfloat16)


def order_classes(orders):
    return [np.arange(0, orders, 4), np.arange(2, orders, 4), np.arange(1, orders, 2)]


def inverse_tables(orders):
    quarter = NPHI // 4
    k = np.arange(quarter, dtype=np.int64)[None, :]
    rows = []
    for m in order_classes(orders):
        angle = (m[:, None] * k % NPHI) * (2 * np.pi / NPHI)
        rows += [np.cos(angle), -np.sin(angle)]
    return np.concatenate(np.split(np.concatenate(rows), quarter // 512, axis=1)).astype(np.float32).astype(jnp.bfloat16)


def padded(count):
    return -(-count // LANES) * LANES


def order_lanes(orders):
    out = []
    for m in order_classes(orders):
        out.append(np.concatenate([m, np.full(padded(len(m)) - len(m), -1)]))
    return np.concatenate(out).astype(np.int32)[None, :]


def turn_rows(order_row):
    m = np.maximum(order_row[0], 0).astype(np.float64)
    weight = np.where(order_row[0] == 0, 1.0, 2.0)
    sign = np.where(order_row[0] % 4 == 3, 1.0, -1.0)
    parts = np_high_low(np.cos(np.pi * m / NPHI) * weight) + np_high_low(np.sin(np.pi * m / NPHI) * weight)
    parts = parts + (weight.astype(jnp.bfloat16), sign.astype(jnp.bfloat16))
    return np.stack(parts + (np.zeros_like(parts[0]),) * 10)


def part_rows(part, bins, cycles_here):
    shape = (2 * bins * cycles_here, 4 * bins * cycles_here)
    row = lax.broadcasted_iota(jnp.int32, shape, 0)
    column = lax.broadcasted_iota(jnp.int32, shape, 1)
    cycle = lax.rem(row, cycles_here)
    bin_number = lax.rem(lax.div(row, cycles_here), bins)
    filter_number = lax.div(row, cycles_here * bins)
    return hot(column == ((filter_number * cycles_here + cycle) * 2 + part) * bins + bin_number)


def inverse_kernel(arrived_ref, slots_ref, turn_hbm, table_hbm, kappa_hbm, potential_hbm,
                   turn_ref, table_ref, wide_ref, kappa_ref, potential_ref, sems, out_sems):
    copies = [pltpu.make_async_copy(turn_hbm, turn_ref, sems.at[0])]
    quarter = NPHI // 4
    chunk = table_ref.shape[1]
    chunks = quarter // chunk
    part = table_ref.shape[0] // chunks
    for i in range(chunks):
        rows = pl.ds(i * part, part)
        copies.append(pltpu.make_async_copy(table_hbm.at[rows], table_ref.at[rows], sems.at[1 + i]))
    for copy in copies:
        copy.start()
    devices, slots = slots_ref.shape
    bins, cycles_here, _ = kappa_ref.shape
    order_count = part // 2
    per_slot = 2 * bins
    per_source = 2 * cycles_here
    wide_ref[...] = arrived_ref[...].astype(jnp.float32)
    turned = [jnp.transpose(wide_ref[pl.ds(i, devices, stride=per_source), :]) for i in range(per_source)]
    few, many = order_count // 4, order_count // 2
    starts = [0, padded(few), 2 * padded(few)]
    lane = lax.broadcasted_iota(jnp.int32, (1, turn_ref.shape[1]), 1)
    orders = jnp.where(lane < few, 4 * lane, -1)
    within = lane - starts[1]
    orders = jnp.where((within >= 0) & (within < few), 4 * within + 2, orders)
    within = lane - starts[2]
    orders = jnp.where((within >= 0) & (within < many), 2 * within + 1, orders)
    lefts, picks = [], []
    for t in range(slots):
        lefts.append(jnp.concatenate([x[t * per_slot : (t + 1) * per_slot, :] for x in turned], 0))
        picks.append(hot(slots_ref[:, t : t + 1] == orders))
    spectrum = dot(jnp.concatenate(lefts, 1).astype(jnp.bfloat16), jnp.concatenate(picks, 0))
    spectrum = spectrum.astype(jnp.bfloat16)
    real_in = dot(part_rows(0, bins, cycles_here), spectrum)
    imag_in = dot(part_rows(1, bins, cycles_here), spectrum)
    copies[0].wait()
    turn = turn_ref[...].astype(jnp.float32)
    odd = lax.rem(lax.rem(lax.broadcasted_iota(jnp.int32, real_in.shape, 0), cycles_here), 2) == 1
    turn_cos = jnp.where(odd, turn[0:1, :] + turn[1:2, :], turn[4:5, :])
    turn_sin = jnp.where(odd, turn[2:3, :] + turn[3:4, :], 0.0)
    real = real_in * turn_cos - imag_in * turn_sin
    imag = real_in * turn_sin + imag_in * turn_cos
    sign = turn[5:6, starts[2] :]
    count = real.shape[0]
    lefts = []
    for index, start in enumerate(starts):
        lanes = slice(start, start + (few if index < 2 else many))
        cos_rows, sin_rows = [real[:, lanes]], [imag[:, lanes]]
        if index == 2:
            cos_rows.append(imag[:, lanes] * sign[:, :many])
            sin_rows.append(-real[:, lanes] * sign[:, :many])
        for rows in (cos_rows, sin_rows):
            lefts.append(jnp.concatenate([y for x in rows for y in high_low(x)], 0))
    results = []
    for index in range(chunks):
        copies[1 + index].wait()
        row = index * part
        sums = []
        for at in range(3):
            height = few if at < 2 else many
            both = dot(lefts[2 * at], table_ref[row : row + height, :])
            both = both + dot(lefts[2 * at + 1], table_ref[row + height : row + 2 * height, :])
            row += 2 * height
            sums += [both[i : i + count, :] + both[i + count : i + 2 * count, :] for i in range(0, both.shape[0], 2 * count)]
        even, other = sums[0] + sums[1], sums[0] - sums[1]
        values = (even + sums[2], other + sums[3], even - sums[2], other - sums[3])
        for j, value in enumerate(values):
            lanes = pl.ds(j * quarter + index * chunk, chunk)
            for f, (out_ref, out_hbm) in enumerate(((kappa_ref, kappa_hbm), (potential_ref, potential_hbm))):
                for b in range(bins):
                    at = (f * bins + b) * cycles_here
                    out_ref[b, :, lanes] = value[at : at + cycles_here, :]
                copy = pltpu.make_async_copy(out_ref.at[:, :, lanes], out_hbm.at[:, :, lanes], out_sems.at[len(results)])
                copy.start()
                results.append(copy)
    for copy in results:
        copy.wait()


def in_hbm(x):
    return pltpu.with_memory_space_constraint(jnp.asarray(x), pltpu.HBM)


def params(orders):
    small = 14 if orders <= 512 else 56
    return pltpu.CompilerParams(vmem_limit_bytes=small * 1024 * 1024)


def per_device(weights, offsets, counts, block_ids, m_table, legendre):
    axes = ("blk", "y", "core")
    _, devices, capacity, bins, _ = weights.shape
    slots, degrees, cycles = legendre.shape
    orders = m_table.shape[0]
    groups = devices * capacity
    cycles_here = cycles // devices
    width = bins * cycles
    staged = legendre.size <= 4 * 1024 * 1024
    limits = params(orders)
    hbm = pl.BlockSpec(memory_space=pltpu.HBM)
    vmem = pl.BlockSpec(memory_space=pltpu.VMEM)

    def shaped(*shape, dtype=jnp.bfloat16):
        return jax.ShapeDtypeStruct(shape, dtype)

    rows = slot_rows(orders, slots)
    inner, outer = analysis_tables(orders)
    live = (capacity + 1) * devices // 2
    key_rows = -(-live // LANES) * 16
    shapes = [
        shaped(bins * live + key_rows, BLOCK),
        shaped(1, orders, dtype=jnp.int32),
        shaped(*rows.shape),
        shaped(*inner.shape),
        shaped(*outer.shape),
    ]
    operands = [
        weights.reshape(groups * bins, BLOCK),
        offsets.reshape(groups, BLOCK),
        counts,
        jnp.transpose(block_ids[0]),
        m_table,
        rows,
        inner,
        outer,
    ]
    ahead = slots * 5 // 6 if staged else 0
    if staged:
        shapes.append(shaped(ahead, degrees, cycles))
        operands.append(legendre)
    deposits, *shared = pl.pallas_call(
        functools.partial(first_kernel, slots, cycles_here * SEGMENTS, ahead),
        in_specs=[hbm] * len(operands),
        out_specs=(vmem,) * len(shapes),
        out_shape=tuple(shapes),
        scratch_shapes=[
            pltpu.VMEM((groups * bins, BLOCK), jnp.bfloat16),
            pltpu.VMEM((groups, BLOCK), jnp.int32),
            pltpu.VMEM((1, devices), jnp.int32),
            pltpu.VMEM((capacity, devices), jnp.int32),
            pltpu.VMEM((orders,), jnp.int32),
            pltpu.VMEM((groups * bins, BLOCK), jnp.float32),
            pltpu.VMEM((bins, live, BLOCK), jnp.bfloat16),
            pltpu.VMEM((live, BLOCK), jnp.float32),
            pltpu.SemaphoreType.DMA((len(operands),)),
        ],
        compiler_params=limits,
        name="deposit",
    )(*[in_hbm(x) for x in operands])
    early = shared.pop() if staged else None

    def swap(x, mask, odd_mask=None):
        masks = (mask, mask if odd_mask is None else odd_mask)
        return lax.ppermute(x, axes, [(i, i ^ masks[i % 2]) for i in range(devices)])

    other = swap(deposits, 1)
    cost = pl.CostEstimate(flops=8 * orders * 256 * bins * live, bytes_accessed=4 * orders * width, transcendentals=0)
    modes_shape = (width // LANES, orders, LANES)
    own, own_inner, own_outer, *late = pl.pallas_call(
        functools.partial(own_kernel, bins, live, cycles, ahead),
        in_specs=[vmem] * 5 + [hbm] * staged,
        out_specs=(vmem,) * (3 + staged),
        out_shape=(
            shaped(*modes_shape, dtype=jnp.float32),
            shaped(orders, inner.shape[1] // 2),
            shaped(orders, outer.shape[1] // 2),
        ) + (shaped(slots - ahead, degrees, cycles),) * staged,
        scratch_shapes=[pltpu.SemaphoreType.DMA] * staged,
        compiler_params=limits,
        cost_estimate=cost,
        name="own_groups",
    )(deposits, *shared, *[in_hbm(legendre)] * staged)

    basis = [early, *late] if staged else [legendre]

    groups_of_bits = bit_groups(devices)
    stages = len(groups_of_bits)
    gain, order = gain_column(degrees), interleave(cycles, cycles_here)
    blocks = devices // 2
    kernel, inputs = functools.partial(other_kernel, bins, live, cycles), (other, own_inner, own_outer, own)
    scratch = [pltpu.VMEM(modes_shape, jnp.float32)]
    responses = []
    for stage, bits in enumerate(groups_of_bits):
        ways = 1 << len(bits)
        blocks //= ways
        rows_here = blocks * 2 * slots
        kept, *sends = pl.pallas_call(
            kernel,
            in_specs=[vmem] * len(inputs),
            out_specs=(vmem,) * ways,
            out_shape=(shaped(rows_here, width, dtype=jnp.float32),) + (shaped(rows_here, width),) * (ways - 1),
            scratch_shapes=scratch,
            compiler_params=limits,
            name="merge" if stage else "other_groups",
        )(*inputs)
        sends, basis = lax.optimization_barrier((sends, basis))
        if stage == 0:
            order_of = send_order(ways)
            arrived = [swap(x, even << bits[0], odd << bits[0]) for x, (even, odd) in zip(sends, order_of)]
        else:
            line = [2, 3, 1] if ways == 4 else range(ways - 1, 0, -1)
            arrived = [swap(sends[i - 1], i << bits[0]) for i in line]
        first, last = (min(slots, slots * 2 * k * (2 * stages - k) // (2 * stages * stages)) for k in (stage, stage + 1))
        count = last - first
        shape = shaped(count, 2 * cycles, 2 * cycles)
        cost = pl.CostEstimate(
            flops=6 * count * degrees * cycles * cycles, bytes_accessed=2 * count * degrees * cycles, transcendentals=0
        )
        if staged:
            kernel, scratch = functools.partial(staged_response_kernel, first), []
        else:
            kernel = functools.partial(response_kernel, first)
            scratch = [pltpu.VMEM((count, degrees, cycles), jnp.bfloat16), pltpu.SemaphoreType.DMA((count,))]
        response = pl.pallas_call(
            kernel,
            in_specs=[vmem if staged else hbm] * len(basis) + [vmem] * 2,
            out_specs=vmem,
            out_shape=shape,
            scratch_shapes=scratch,
            compiler_params=limits,
            cost_estimate=cost,
            name="response",
        )(*basis if staged else [in_hbm(x) for x in basis], gain, order)
        *arrived, response = lax.optimization_barrier((*arrived, response))
        responses.append(response)
        kernel, inputs, scratch = functools.partial(merge_kernel, len(arrived)), (kept, *arrived), []

    outgoing = pl.pallas_call(
        functools.partial(synthesis_kernel, len(inputs) - 1, len(responses)),
        in_specs=[vmem] * (len(inputs) + len(responses) + 1),
        out_specs=vmem,
        out_shape=shaped(2 * cycles, 128),
        compiler_params=limits,
        name="synthesis",
    )(*inputs, *responses, slot_order(slots, bins))
    outgoing = outgoing.reshape(devices, 2 * cycles_here, 128)
    outgoing, held = lax.optimization_barrier((outgoing, m_table))
    arrived = lax.all_to_all(outgoing, axes, split_axis=0, concat_axis=0, tiled=True)
    arrived = arrived.reshape(2 * cycles, 128)
    if staged:
        arrived = pltpu.with_memory_space_constraint(arrived, pltpu.VMEM)

    lanes = order_lanes(orders)
    constants = [turn_rows(lanes), inverse_tables(orders)]
    chunks = NPHI // 4 // constants[-1].shape[1]
    map_shape = shaped(bins, cycles_here, NPHI, dtype=jnp.float32)
    return pl.pallas_call(
        inverse_kernel,
        in_specs=[vmem] * 2 + [hbm] * 2,
        out_specs=(hbm, hbm),
        out_shape=(map_shape, map_shape),
        scratch_shapes=[
            *[pltpu.VMEM(x.shape, x.dtype) for x in constants],
            pltpu.VMEM((2 * cycles, 128), jnp.float32),
            pltpu.VMEM(map_shape.shape, jnp.float32),
            pltpu.VMEM(map_shape.shape, jnp.float32),
            pltpu.SemaphoreType.DMA((1 + chunks,)),
            pltpu.SemaphoreType.DMA((8 * chunks,)),
        ],
        compiler_params=limits,
        name="inverse",
    )(arrived, held.reshape(devices, slots), *[in_hbm(x) for x in constants])


def solution(mesh):
    blocks, columns = mesh.devices.shape
    fine = Mesh(mesh.devices.reshape(blocks, columns // 2, 2), ("blk", "y", "core"))
    axes = ("blk", "y", "core")
    placed = (
        P(axes, None, None, None, None),
        P(axes, None, None, None),
        P(axes, None),
        P(axes, None, None),
        P(),
        P(axes, None, None),
    )
    return jax.shard_map(
        per_device,
        mesh=fine,
        in_specs=placed,
        out_specs=(P(None, axes, None), P(None, axes, None)),
        check_vma=False,
    )
```

```python
import functools

import jax
import jax.numpy as jnp
import numpy as np
from jax import lax
from jax.experimental import pallas as pl
from jax.experimental.pallas import tpu as pltpu
from jax.sharding import Mesh, PartitionSpec as P

NPHI = 4096
BLOCK = 128
SEGMENTS = NPHI // BLOCK
LANES = 128
CHUNK = 192

NT = (((1,), (1,)), ((), ()))
TN = (((0,), (0,)), ((), ()))


def dot(a, b, dims=(((1,), (0,)), ((), ()))):
    return lax.dot_general(a, b, dims, preferred_element_type=jnp.float32)


def high_low(x):
    high = x.astype(jnp.bfloat16)
    return high, (x - high.astype(jnp.float32)).astype(jnp.bfloat16)


def np_high_low(x):
    high = x.astype(np.float32).astype(jnp.bfloat16)
    return high, (x - high.astype(np.float64)).astype(np.float32).astype(jnp.bfloat16)


def analysis_tables(orders):
    m = np.arange(orders, dtype=np.int64)[:, None]
    p = np.arange(BLOCK, dtype=np.int64)[None, :]
    angle = (m * p % NPHI) * (2 * np.pi / NPHI)
    inner = np.concatenate(np_high_low(np.cos(angle)) + np_high_low(-np.sin(angle)), 1)
    half = np.arange(2 * SEGMENTS, dtype=np.int64)[None, :]
    steps = 2 * BLOCK * (half % SEGMENTS) + half // SEGMENTS
    angle = (m * steps % (2 * NPHI)) * (np.pi / NPHI)
    outer = np.concatenate(np_high_low(np.cos(angle) / NPHI) + np_high_low(-np.sin(angle) / NPHI), 1)
    return inner, outer


def bit_groups(devices):
    bits = list(range(1, devices.bit_length() - 1))
    return [bits[i : i + 2] for i in range(0, len(bits), 2)]


def positions(devices):
    order = [0]
    for group in bit_groups(devices):
        order = [p | (v << group[0]) for p in order for v in range(1 << len(group))]
    return order


def slot_rows(orders, slots):
    out = np.zeros((orders // 2, orders), np.float32)
    for block, position in enumerate(positions(orders // slots)):
        for slot in range(slots):
            out[block * slots + slot, position * slots + slot] = 1
    return out.astype(jnp.bfloat16)


def rolled(x, shift):
    return jnp.concatenate([x[:, shift:], x[:, :shift]], 1)


def exclusive_or(table, me, slots):
    orders = table.shape[1]
    block = lax.div(lax.broadcasted_iota(jnp.int32, table.shape, 1), slots)
    for bit in range((orders // slots).bit_length() - 1):
        shift = slots << bit
        swapped = jnp.where((block >> bit) % 2 == 0, rolled(table, shift), rolled(table, orders - shift))
        table = jnp.where(jnp.broadcast_to((me >> bit) & 1, table.shape) == 1, swapped, table)
    return table


def hot(condition):
    return jnp.where(condition, 1.0, 0.0).astype(jnp.bfloat16)


def twice(x):
    return jnp.concatenate([x, x], 1)


def first_kernel(slots, blocks_here, staged, w_hbm, off_hbm, cnt_hbm, ids_hbm, table_hbm, rows_hbm, inner_hbm, outer_hbm, *refs):
    if staged:
        legendre_hbm, *refs = refs
    out_ref, table_ref, rows_ref, inner_ref, outer_ref, *refs = refs
    if staged:
        legendre_ref, *refs = refs
    w_ref, off_ref, cnt_ref, ids_ref, flat_ref, wide_ref, live_w_ref, live_off_ref, sems = refs
    pairs = (
        (cnt_hbm, cnt_ref), (ids_hbm, ids_ref), (off_hbm, off_ref), (w_hbm, w_ref),
        (table_hbm, flat_ref), (rows_hbm, rows_ref), (inner_hbm, inner_ref), (outer_hbm, outer_ref),
    )
    if staged:
        pairs = pairs + ((legendre_hbm.at[pl.ds(0, staged)], legendre_ref),)
    copies = [pltpu.make_async_copy(a, b, sems.at[i]) for i, (a, b) in enumerate(pairs)]
    for copy in copies[:4]:
        copy.start()
    groups = off_ref.shape[0]
    capacity, devices = ids_ref.shape
    bins, live, _ = live_w_ref.shape
    pack = 16
    key_tiles = (out_ref.shape[0] - bins * live) // pack

    owner = lax.div(lax.broadcasted_iota(jnp.int32, (devices, groups), 1), capacity)
    source = lax.broadcasted_iota(jnp.int32, (devices, groups), 0)
    member = lax.rem(lax.broadcasted_iota(jnp.int32, (capacity, groups), 1), capacity)
    own_row = lax.broadcasted_iota(jnp.int32, (capacity, groups), 0) == member
    for copy in copies[:2]:
        copy.wait()
    counts = jnp.broadcast_to(cnt_ref[...].astype(jnp.float32), (8, devices)).astype(jnp.bfloat16)
    count = dot(counts, hot(source == owner))[0:1, :]
    before = dot(counts, hot(source < owner))[0:1, :]
    number = member[0:1, :].astype(jnp.float32)
    place = jnp.where(number < count, before + number, -1.0).astype(jnp.int32)
    packing = hot(lax.broadcasted_iota(jnp.int32, (key_tiles * LANES, groups), 0) == place)

    ids = dot(ids_ref[...].astype(jnp.float32).astype(jnp.bfloat16), hot(source == owner))
    ids = jnp.sum(jnp.where(own_row, ids, 0.0), axis=0, keepdims=True)
    block = ids.astype(jnp.int32) + owner[0:1, :] * blocks_here
    cycle = lax.div(block, SEGMENTS)
    phase = lax.rem(cycle, 2) * SEGMENTS + lax.rem(block, SEGMENTS)
    row = lax.broadcasted_iota(jnp.int32, (pack, groups), 0)
    keys = jnp.where(row == 0, lax.div(cycle, 16), jnp.where(row == 1, lax.rem(cycle, 16), phase))
    keys = dot(keys.astype(jnp.float32).astype(jnp.bfloat16), packing, NT).astype(jnp.bfloat16)
    for tile in range(key_tiles):
        out_ref[bins * live + tile * pack : bins * live + (tile + 1) * pack, :] = keys[:, tile * LANES : (tile + 1) * LANES]

    for copy in copies[2:4]:
        copy.wait()
    for copy in copies[4:]:
        copy.start()
    packing = packing[:live, :]
    live_off_ref[...] = dot(packing, off_ref[...].astype(jnp.float32).astype(jnp.bfloat16))
    wide_ref[...] = w_ref[...].astype(jnp.float32)
    for b in range(bins):
        live_w_ref[b] = dot(packing, wide_ref[pl.ds(b, groups, stride=bins), :].astype(jnp.bfloat16)).astype(jnp.bfloat16)

    pixel = lax.broadcasted_iota(jnp.int32, (pack, BLOCK), 0)
    pixels = [(pixel + pack * k).astype(jnp.float32).astype(jnp.bfloat16) for k in range(BLOCK // pack)]
    alone = [hot(pixel == i) for i in range(pack)]
    one = jnp.ones((pack, BLOCK), jnp.bfloat16)
    zero = jnp.zeros((pack, BLOCK), jnp.bfloat16)

    def deposit(step, carry):
        start = pl.multiple_of(step * pack, pack)
        weights = [live_w_ref[b, pl.ds(start, pack), :] for b in range(bins)]
        left, right = [], []
        for i in range(pack):
            left.append(jnp.concatenate([w * alone[i] for w in weights], 0))
            at = jnp.broadcast_to(live_off_ref[pl.ds(start + i, 1), :], (pack, BLOCK)).astype(jnp.bfloat16)
            right.append(jnp.concatenate([jnp.where(at == x, one, zero) for x in pixels], 0))
        out = dot(jnp.concatenate(left, 1), jnp.concatenate(right, 1), NT).astype(jnp.bfloat16)
        for b in range(bins):
            out_ref[pl.ds(pl.multiple_of(b * live + start, pack), pack), :] = out[b * pack : (b + 1) * pack, :]
        return carry

    lax.fori_loop(0, live // pack, deposit, 0, unroll=9)
    for copy in copies[4:8]:
        copy.wait()
    me = lax.axis_index("blk")
    for axis in ("y", "core"):
        me = me * lax.axis_size(axis) + lax.axis_index(axis)
    table_ref[...] = exclusive_or(flat_ref[...].reshape(table_ref.shape), me, slots)
    for copy in copies[8:]:
        copy.wait()


def add_modes(bins, groups, cycles, groups_ref, pieces, add):
    pack = 16
    keys = groups_ref[bins * groups :, :].astype(jnp.float32)
    keys = jnp.concatenate([keys[i * pack : (i + 1) * pack, :] for i in range(keys.shape[0] // pack)], 1)
    cycle = (keys[0:1, :groups] * 16.0 + keys[1:2, :groups]).astype(jnp.int32)
    phase = keys[2:3, :groups].astype(jnp.int32)
    cycle_hot = hot(lax.broadcasted_iota(jnp.int32, (cycles, groups), 0) == cycle)
    half_hot = hot(lax.broadcasted_iota(jnp.int32, (2 * SEGMENTS, groups), 0) == phase)
    phase_hot = jnp.concatenate([half_hot, half_hot], 0)
    deposits = [twice(groups_ref[b * groups : (b + 1) * groups, :]) for b in range(bins)]
    for start, inner_rows, outer_rows in pieces:
        count = inner_rows.shape[0] // 2
        outer = dot(outer_rows, phase_hot)
        outer_cos, outer_sin = outer[:count, :], outer[count:, :]
        for b, deposit in enumerate(deposits):
            inner = dot(inner_rows, deposit, NT)
            inner_cos, inner_sin = inner[:count, :], inner[count:, :]
            real = inner_cos * outer_cos - inner_sin * outer_sin
            imag = inner_cos * outer_sin + inner_sin * outer_cos
            both = dot(jnp.concatenate([real, imag], 0).astype(jnp.bfloat16), cycle_hot, NT)
            for part in range(2):
                value = both[part * count : (part + 1) * count, :]
                for tile in range(cycles // LANES):
                    add(b * (cycles // LANES) + tile, start + part, value[:, tile * LANES : (tile + 1) * LANES])


def all_pieces(inner_ref, outer_ref):
    for start in range(0, inner_ref.shape[0], 2 * CHUNK):
        yield start, inner_ref[start : start + 2 * CHUNK, :], outer_ref[start : start + 2 * CHUNK, :]


def block_piece(inner_ref, outer_ref, ways, even, odd):
    count = inner_ref.shape[0] // 2 // ways
    core = lax.axis_index("core")
    starts = [block * count // CHUNK * 2 * CHUNK + block * count % CHUNK for block in (even, odd)]
    tables = []
    for ref in (inner_ref, outer_ref):
        parts = []
        for shift in (0, CHUNK):
            first = pl.multiple_of(starts[0] + shift + core * (starts[1] - starts[0]), 16)
            parts.append(ref[pl.ds(first, count), :])
        tables.append(jnp.concatenate(parts, 0))
    return [(0, *tables)]


def own_kernel(bins, groups, cycles, staged, groups_ref, table_ref, rows_ref, inner_ref, outer_ref, *refs):
    if staged:
        legendre_hbm, out_ref, inner_out, outer_out, legendre_ref, sem = refs
        late = pltpu.make_async_copy(legendre_hbm.at[pl.ds(staged, legendre_ref.shape[0])], legendre_ref, sem)
        late.start()
    else:
        out_ref, inner_out, outer_out = refs
    count, orders = rows_ref.shape
    held = hot(lax.broadcasted_iota(jnp.int32, (orders, orders), 0) == table_ref[...])
    for start in range(0, count, CHUNK):
        pick = dot(rows_ref[start : start + CHUNK, :], held, NT).astype(jnp.bfloat16)
        inner = dot(pick, inner_ref[...]).astype(jnp.bfloat16)
        outer = dot(pick, outer_ref[...]).astype(jnp.bfloat16)
        for part in range(2):
            rows = slice(2 * start + part * CHUNK, 2 * start + (part + 1) * CHUNK)
            inner_out[rows, :] = inner[:, part * 2 * BLOCK : (part + 1) * 2 * BLOCK]
            outer_out[rows, :] = outer[:, part * BLOCK : (part + 1) * BLOCK]

    def add(tile, first, value):
        out_ref.at[tile][pl.ds(first, value.shape[0], stride=2), :] = value

    add_modes(bins, groups, cycles, groups_ref, all_pieces(inner_out, outer_out), add)
    if staged:
        late.wait()


def split_sum(parts, tile, keep_ref, send_refs):
    rows = keep_ref.shape[0]
    lanes = slice(tile * LANES, (tile + 1) * LANES)
    for i, out_ref in enumerate((keep_ref, *send_refs)):
        value = sum(part(slice(i * rows, (i + 1) * rows), lanes) for part in parts)
        out_ref[:, lanes] = value.astype(out_ref.dtype)


def send_order(ways):
    return [(1, 2), (2, 1), (3, 3)] if ways == 4 else [(i, i) for i in range(1, ways)]


def sum_block(own_ref, other_ref, other_rows, blocks, out_ref):
    rows = out_ref.shape[0]
    even, odd = blocks
    first = even * rows if even == odd else pl.multiple_of((even + lax.axis_index("core") * (odd - even)) * rows, rows)
    for tile in range(own_ref.shape[0]):
        value = own_ref[tile, pl.ds(first, rows), :] + other_ref[tile, other_rows or pl.ds(first, rows), :]
        out_ref[:, tile * LANES : (tile + 1) * LANES] = value.astype(out_ref.dtype)


def first_block_kernel(bins, groups, cycles, ways, groups_ref, inner_ref, outer_ref, own_ref, send_ref, other_ref):
    def add(tile, first, value):
        other_ref.at[tile][pl.ds(first, value.shape[0], stride=2), :] = value

    blocks = send_order(ways)[0]
    add_modes(bins, groups, cycles, groups_ref, block_piece(inner_ref, outer_ref, ways, *blocks), add)
    sum_block(own_ref, other_ref, slice(0, send_ref.shape[0]), blocks, send_ref)


def other_kernel(bins, groups, cycles, ways, groups_ref, inner_ref, outer_ref, own_ref, keep_ref, *refs):
    *send_refs, other_ref = refs

    def add(tile, first, value):
        other_ref.at[tile][pl.ds(first, value.shape[0], stride=2), :] = value

    add_modes(bins, groups, cycles, groups_ref, all_pieces(inner_ref, outer_ref), add)
    for blocks, out_ref in zip([(0, 0)] + send_order(ways)[1:], (keep_ref, *send_refs)):
        sum_block(own_ref, other_ref, None, blocks, out_ref)


def merge_kernel(count, kept_ref, *refs):
    arrived, outs = refs[:count], refs[count:]
    for tile in range(kept_ref.shape[1] // LANES):
        parts = [lambda rows, lanes, ref=ref: ref[rows, lanes].astype(jnp.float32) for ref in (kept_ref, *arrived)]
        split_sum(parts, tile, outs[0], outs[1:])


def gain_column(degrees):
    l = np.arange(degrees, dtype=np.float32)
    return np.where(l > 0.5, np.float32(-20000.0) / np.maximum(l * (l + 1), np.float32(1)), np.float32(0)).astype(np.float32)[:, None] * np.ones((1, BLOCK), np.float32)


def interleave(cycles, cycles_here):
    out = np.zeros((2 * cycles, 2 * cycles), np.float32)
    for f in range(2):
        for c in range(cycles):
            out[f * cycles + c, (c // cycles_here * 2 + f) * cycles_here + c % cycles_here] = 1
    return out.astype(jnp.bfloat16)


def respond(basis, gain_ref, order_ref, out_ref, slot):
    cycles = basis.shape[1]
    gain = jnp.concatenate([gain_ref[...]] * (cycles // BLOCK), 1)
    gained = (basis.astype(jnp.float32) * gain).astype(jnp.bfloat16)
    high, low = high_low(dot(basis, jnp.concatenate([basis, gained], 1), TN))
    out_ref[slot] = dot(jnp.concatenate([high, low], 0), order_ref[...]).astype(jnp.bfloat16)


def staged_response_kernel(start, early_ref, late_ref, gain_ref, order_ref, out_ref):
    early = early_ref.shape[0]
    for slot in range(out_ref.shape[0]):
        at = start + slot
        respond(early_ref[at] if at < early else late_ref[at - early], gain_ref, order_ref, out_ref, slot)


def response_kernel(start, legendre_hbm, gain_ref, order_ref, out_ref, legendre_ref, sems):
    count = out_ref.shape[0]
    copies = [pltpu.make_async_copy(legendre_hbm.at[start + i], legendre_ref.at[i], sems.at[i]) for i in range(count)]
    for copy in copies:
        copy.start()
    for slot in range(count):
        copies[slot].wait()
        respond(legendre_ref[slot], gain_ref, order_ref, out_ref, slot)


def slot_order(slots, bins):
    out = np.zeros((slots * 2 * bins, slots * 2 * bins), np.float32)
    for b in range(bins):
        for c in range(2):
            for t in range(slots):
                out[(t * 2 + c) * bins + b, (b * slots + t) * 2 + c] = 1
    return out.astype(jnp.bfloat16)


def synthesis_kernel(arrivals, pieces, kept_ref, *refs):
    partials, refs = refs[:arrivals], refs[arrivals:]
    response_refs, (order_ref, out_ref) = refs[:pieces], refs[pieces:]
    cycles = response_refs[0].shape[1] // 2
    bins = kept_ref.shape[1] // cycles
    slots = kept_ref.shape[0] // 2
    responses = [ref.at[i] for ref in response_refs for i in range(ref.shape[0])]
    total = kept_ref[...]
    for ref in partials:
        total = total + ref[...].astype(jnp.float32)
    modes = jnp.concatenate([total[:, b * cycles : (b + 1) * cycles] for b in range(bins)], 0)
    high, low = high_low(modes)
    high = dot(order_ref[...], high)
    low = dot(order_ref[...], low)
    per_slot = 2 * bins
    parts = []
    for t in range(slots):
        rows = slice(t * per_slot, (t + 1) * per_slot)
        left = jnp.concatenate([high[rows, :], low[rows, :]], 0).astype(jnp.bfloat16)
        part = dot(twice(left), responses[t][...])
        parts.append(part[:per_slot, :] + part[per_slot:, :])
    parts.append(jnp.zeros((128 - slots * per_slot, 2 * cycles), jnp.float32))
    result = jnp.concatenate(parts, 0)
    out_ref[...] = jnp.transpose(result).astype(jnp.bfloat16)


def order_classes(orders):
    return [np.arange(0, orders, 4), np.arange(2, orders, 4), np.arange(1, orders, 2)]


def inverse_tables(orders):
    quarter = NPHI // 4
    k = np.arange(quarter, dtype=np.int64)[None, :]
    rows = []
    for m in order_classes(orders):
        angle = (m[:, None] * k % NPHI) * (2 * np.pi / NPHI)
        rows += [np.cos(angle), -np.sin(angle)]
    return np.concatenate(np.split(np.concatenate(rows), quarter // 512, axis=1)).astype(np.float32).astype(jnp.bfloat16)


def padded(count):
    return -(-count // LANES) * LANES


def order_lanes(orders):
    out = []
    for m in order_classes(orders):
        out.append(np.concatenate([m, np.full(padded(len(m)) - len(m), -1)]))
    return np.concatenate(out).astype(np.int32)[None, :]


def turn_rows(order_row):
    m = np.maximum(order_row[0], 0).astype(np.float64)
    weight = np.where(order_row[0] == 0, 1.0, 2.0)
    sign = np.where(order_row[0] % 4 == 3, 1.0, -1.0)
    parts = np_high_low(np.cos(np.pi * m / NPHI) * weight) + np_high_low(np.sin(np.pi * m / NPHI) * weight)
    parts = parts + (weight.astype(jnp.bfloat16), sign.astype(jnp.bfloat16))
    return np.stack(parts + (np.zeros_like(parts[0]),) * 10)


def part_rows(part, bins, cycles_here):
    shape = (2 * bins * cycles_here, 4 * bins * cycles_here)
    row = lax.broadcasted_iota(jnp.int32, shape, 0)
    column = lax.broadcasted_iota(jnp.int32, shape, 1)
    cycle = lax.rem(row, cycles_here)
    bin_number = lax.rem(lax.div(row, cycles_here), bins)
    filter_number = lax.div(row, cycles_here * bins)
    return hot(column == ((filter_number * cycles_here + cycle) * 2 + part) * bins + bin_number)


def inverse_kernel(arrived_ref, slots_ref, turn_hbm, table_hbm, kappa_hbm, potential_hbm,
                   turn_ref, table_ref, wide_ref, kappa_ref, potential_ref, sems, out_sems):
    copies = [pltpu.make_async_copy(turn_hbm, turn_ref, sems.at[0])]
    quarter = NPHI // 4
    chunk = table_ref.shape[1]
    chunks = quarter // chunk
    part = table_ref.shape[0] // chunks
    for i in range(chunks):
        rows = pl.ds(i * part, part)
        copies.append(pltpu.make_async_copy(table_hbm.at[rows], table_ref.at[rows], sems.at[1 + i]))
    for copy in copies:
        copy.start()
    devices, slots = slots_ref.shape
    bins, cycles_here, _ = kappa_ref.shape
    order_count = part // 2
    per_slot = 2 * bins
    per_source = 2 * cycles_here
    wide_ref[...] = arrived_ref[...].astype(jnp.float32)
    turned = [jnp.transpose(wide_ref[pl.ds(i, devices, stride=per_source), :]) for i in range(per_source)]
    few, many = order_count // 4, order_count // 2
    starts = [0, padded(few), 2 * padded(few)]
    lane = lax.broadcasted_iota(jnp.int32, (1, turn_ref.shape[1]), 1)
    orders = jnp.where(lane < few, 4 * lane, -1)
    within = lane - starts[1]
    orders = jnp.where((within >= 0) & (within < few), 4 * within + 2, orders)
    within = lane - starts[2]
    orders = jnp.where((within >= 0) & (within < many), 2 * within + 1, orders)
    lefts, picks = [], []
    for t in range(slots):
        lefts.append(jnp.concatenate([x[t * per_slot : (t + 1) * per_slot, :] for x in turned], 0))
        picks.append(hot(slots_ref[:, t : t + 1] == orders))
    spectrum = dot(jnp.concatenate(lefts, 1).astype(jnp.bfloat16), jnp.concatenate(picks, 0))
    spectrum = spectrum.astype(jnp.bfloat16)
    real_in = dot(part_rows(0, bins, cycles_here), spectrum)
    imag_in = dot(part_rows(1, bins, cycles_here), spectrum)
    copies[0].wait()
    turn = turn_ref[...].astype(jnp.float32)
    odd = lax.rem(lax.rem(lax.broadcasted_iota(jnp.int32, real_in.shape, 0), cycles_here), 2) == 1
    turn_cos = jnp.where(odd, turn[0:1, :] + turn[1:2, :], turn[4:5, :])
    turn_sin = jnp.where(odd, turn[2:3, :] + turn[3:4, :], 0.0)
    real = real_in * turn_cos - imag_in * turn_sin
    imag = real_in * turn_sin + imag_in * turn_cos
    sign = turn[5:6, starts[2] :]
    count = real.shape[0]
    lefts = []
    for index, start in enumerate(starts):
        lanes = slice(start, start + (few if index < 2 else many))
        cos_rows, sin_rows = [real[:, lanes]], [imag[:, lanes]]
        if index == 2:
            cos_rows.append(imag[:, lanes] * sign[:, :many])
            sin_rows.append(-real[:, lanes] * sign[:, :many])
        for rows in (cos_rows, sin_rows):
            lefts.append(jnp.concatenate([y for x in rows for y in high_low(x)], 0))
    results = []
    for index in range(chunks):
        copies[1 + index].wait()
        row = index * part
        sums = []
        for at in range(3):
            height = few if at < 2 else many
            both = dot(lefts[2 * at], table_ref[row : row + height, :])
            both = both + dot(lefts[2 * at + 1], table_ref[row + height : row + 2 * height, :])
            row += 2 * height
            sums += [both[i : i + count, :] + both[i + count : i + 2 * count, :] for i in range(0, both.shape[0], 2 * count)]
        even, other = sums[0] + sums[1], sums[0] - sums[1]
        values = (even + sums[2], other + sums[3], even - sums[2], other - sums[3])
        for j, value in enumerate(values):
            lanes = pl.ds(j * quarter + index * chunk, chunk)
            for f, (out_ref, out_hbm) in enumerate(((kappa_ref, kappa_hbm), (potential_ref, potential_hbm))):
                for b in range(bins):
                    at = (f * bins + b) * cycles_here
                    out_ref[b, :, lanes] = value[at : at + cycles_here, :]
                copy = pltpu.make_async_copy(out_ref.at[:, :, lanes], out_hbm.at[:, :, lanes], out_sems.at[len(results)])
                copy.start()
                results.append(copy)
    for copy in results:
        copy.wait()


def in_hbm(x):
    return pltpu.with_memory_space_constraint(jnp.asarray(x), pltpu.HBM)


def params(orders):
    small = 14 if orders <= 512 else 56
    return pltpu.CompilerParams(vmem_limit_bytes=small * 1024 * 1024)


def per_device(weights, offsets, counts, block_ids, m_table, legendre):
    axes = ("blk", "y", "core")
    _, devices, capacity, bins, _ = weights.shape
    slots, degrees, cycles = legendre.shape
    orders = m_table.shape[0]
    groups = devices * capacity
    cycles_here = cycles // devices
    width = bins * cycles
    staged = legendre.size <= 4 * 1024 * 1024
    limits = params(orders)
    hbm = pl.BlockSpec(memory_space=pltpu.HBM)
    vmem = pl.BlockSpec(memory_space=pltpu.VMEM)

    def shaped(*shape, dtype=jnp.bfloat16):
        return jax.ShapeDtypeStruct(shape, dtype)

    rows = slot_rows(orders, slots)
    inner, outer = analysis_tables(orders)
    live = (capacity + 1) * devices // 2
    key_rows = -(-live // LANES) * 16
    shapes = [
        shaped(bins * live + key_rows, BLOCK),
        shaped(1, orders, dtype=jnp.int32),
        shaped(*rows.shape),
        shaped(*inner.shape),
        shaped(*outer.shape),
    ]
    operands = [
        weights.reshape(groups * bins, BLOCK),
        offsets.reshape(groups, BLOCK),
        counts,
        jnp.transpose(block_ids[0]),
        m_table,
        rows,
        inner,
        outer,
    ]
    ahead = slots * 5 // 6 if staged else 0
    if staged:
        shapes.append(shaped(ahead, degrees, cycles))
        operands.append(legendre)
    deposits, *shared = pl.pallas_call(
        functools.partial(first_kernel, slots, cycles_here * SEGMENTS, ahead),
        in_specs=[hbm] * len(operands),
        out_specs=(vmem,) * len(shapes),
        out_shape=tuple(shapes),
        scratch_shapes=[
            pltpu.VMEM((groups * bins, BLOCK), jnp.bfloat16),
            pltpu.VMEM((groups, BLOCK), jnp.int32),
            pltpu.VMEM((1, devices), jnp.int32),
            pltpu.VMEM((capacity, devices), jnp.int32),
            pltpu.VMEM((orders,), jnp.int32),
            pltpu.VMEM((groups * bins, BLOCK), jnp.float32),
            pltpu.VMEM((bins, live, BLOCK), jnp.bfloat16),
            pltpu.VMEM((live, BLOCK), jnp.float32),
            pltpu.SemaphoreType.DMA((len(operands),)),
        ],
        compiler_params=limits,
        name="deposit",
    )(*[in_hbm(x) for x in operands])
    early = shared.pop() if staged else None

    def swap(x, mask, odd_mask=None):
        masks = (mask, mask if odd_mask is None else odd_mask)
        return lax.ppermute(x, axes, [(i, i ^ masks[i % 2]) for i in range(devices)])

    other = swap(deposits, 1)
    modes_cost = pl.CostEstimate(flops=8 * orders * 256 * bins * live, bytes_accessed=4 * orders * width, transcendentals=0)
    modes_shape = (width // LANES, orders, LANES)
    own, own_inner, own_outer, *late = pl.pallas_call(
        functools.partial(own_kernel, bins, live, cycles, ahead),
        in_specs=[vmem] * 5 + [hbm] * staged,
        out_specs=(vmem,) * (3 + staged),
        out_shape=(
            shaped(*modes_shape, dtype=jnp.float32),
            shaped(orders, inner.shape[1] // 2),
            shaped(orders, outer.shape[1] // 2),
        ) + (shaped(slots - ahead, degrees, cycles),) * staged,
        scratch_shapes=[pltpu.SemaphoreType.DMA] * staged,
        compiler_params=limits,
        cost_estimate=modes_cost,
        name="own_groups",
    )(deposits, *shared, *[in_hbm(legendre)] * staged)

    basis = [early, *late] if staged else [legendre]

    groups_of_bits = bit_groups(devices)
    stages = len(groups_of_bits)
    gain, order = gain_column(degrees), interleave(cycles, cycles_here)
    blocks = devices // 2
    ways = 1 << len(groups_of_bits[0])
    block_rows = orders // ways
    first_send = pl.pallas_call(
        functools.partial(first_block_kernel, bins, live, cycles, ways),
        in_specs=[vmem] * 4,
        out_specs=vmem,
        out_shape=shaped(block_rows, width),
        scratch_shapes=[pltpu.VMEM((width // LANES, block_rows, LANES), jnp.float32)],
        compiler_params=limits,
        name="first_block",
    )(other, own_inner, own_outer, own)
    first_send, other = lax.optimization_barrier((first_send, other))
    even, odd = send_order(ways)[0]
    low_bit = groups_of_bits[0][0]
    first_arrived = swap(first_send, even << low_bit, odd << low_bit)
    kernel, inputs = functools.partial(other_kernel, bins, live, cycles, ways), (other, own_inner, own_outer, own)
    scratch = [pltpu.VMEM(modes_shape, jnp.float32)]
    responses = []
    for stage, bits in enumerate(groups_of_bits):
        ways = 1 << len(bits)
        blocks //= ways
        rows_here = blocks * 2 * slots
        kept, *sends = pl.pallas_call(
            kernel,
            in_specs=[vmem] * len(inputs),
            out_specs=(vmem,) * (ways if stage else ways - 1),
            out_shape=(shaped(rows_here, width, dtype=jnp.float32),) + (shaped(rows_here, width),) * (ways - 1 if stage else ways - 2),
            scratch_shapes=scratch,
            compiler_params=limits,
            cost_estimate=None if stage else modes_cost,
            name="merge" if stage else "other_groups",
        )(*inputs)
        sends, basis = lax.optimization_barrier((sends, basis))
        if stage == 0:
            order_of = send_order(ways)[1:]
            arrived = [first_arrived] + [swap(x, even << bits[0], odd << bits[0]) for x, (even, odd) in zip(sends, order_of)]
            basis, arrived[0] = lax.optimization_barrier((basis, arrived[0]))
        else:
            line = [2, 3, 1] if ways == 4 else range(ways - 1, 0, -1)
            arrived = [swap(sends[i - 1], i << bits[0]) for i in line]
        first, last = (min(slots, slots * 2 * k * (2 * stages - k) // (2 * stages * stages)) for k in (stage, stage + 1))
        count = last - first
        shape = shaped(count, 2 * cycles, 2 * cycles)
        cost = pl.CostEstimate(
            flops=6 * count * degrees * cycles if stage == 0 else 6 * count * degrees * cycles * cycles,
            bytes_accessed=0 if stage == 0 else 2 * count * degrees * cycles,
            transcendentals=0,
        )
        if staged:
            kernel, scratch = functools.partial(staged_response_kernel, first), []
        else:
            kernel = functools.partial(response_kernel, first)
            scratch = [pltpu.VMEM((count, degrees, cycles), jnp.bfloat16), pltpu.SemaphoreType.DMA((count,))]
        response = pl.pallas_call(
            kernel,
            in_specs=[vmem if staged else hbm] * len(basis) + [vmem] * 2,
            out_specs=vmem,
            out_shape=shape,
            scratch_shapes=scratch,
            compiler_params=limits,
            cost_estimate=cost,
            name="response",
        )(*basis if staged else [in_hbm(x) for x in basis], gain, order)
        *arrived, response = lax.optimization_barrier((*arrived, response))
        responses.append(response)
        kernel, inputs, scratch = functools.partial(merge_kernel, len(arrived)), (kept, *arrived), []

    outgoing = pl.pallas_call(
        functools.partial(synthesis_kernel, len(inputs) - 1, len(responses)),
        in_specs=[vmem] * (len(inputs) + len(responses) + 1),
        out_specs=vmem,
        out_shape=shaped(2 * cycles, 128),
        compiler_params=limits,
        name="synthesis",
    )(*inputs, *responses, slot_order(slots, bins))
    outgoing = outgoing.reshape(devices, 2 * cycles_here, 128)
    outgoing, held = lax.optimization_barrier((outgoing, m_table))
    arrived = lax.all_to_all(outgoing, axes, split_axis=0, concat_axis=0, tiled=True)
    arrived = arrived.reshape(2 * cycles, 128)
    if staged:
        arrived = pltpu.with_memory_space_constraint(arrived, pltpu.VMEM)

    lanes = order_lanes(orders)
    constants = [turn_rows(lanes), inverse_tables(orders)]
    chunks = NPHI // 4 // constants[-1].shape[1]
    map_shape = shaped(bins, cycles_here, NPHI, dtype=jnp.float32)
    return pl.pallas_call(
        inverse_kernel,
        in_specs=[vmem] * 2 + [hbm] * 2,
        out_specs=(hbm, hbm),
        out_shape=(map_shape, map_shape),
        scratch_shapes=[
            *[pltpu.VMEM(x.shape, x.dtype) for x in constants],
            pltpu.VMEM((2 * cycles, 128), jnp.float32),
            pltpu.VMEM(map_shape.shape, jnp.float32),
            pltpu.VMEM(map_shape.shape, jnp.float32),
            pltpu.SemaphoreType.DMA((1 + chunks,)),
            pltpu.SemaphoreType.DMA((8 * chunks,)),
        ],
        compiler_params=limits,
        name="inverse",
    )(arrived, held.reshape(devices, slots), *[in_hbm(x) for x in constants])


def solution(mesh):
    blocks, columns = mesh.devices.shape
    fine = Mesh(mesh.devices.reshape(blocks, columns // 2, 2), ("blk", "y", "core"))
    axes = ("blk", "y", "core")
    placed = (
        P(axes, None, None, None, None),
        P(axes, None, None, None),
        P(axes, None),
        P(axes, None, None),
        P(),
        P(axes, None, None),
    )
    return jax.shard_map(
        per_device,
        mesh=fine,
        in_specs=placed,
        out_specs=(P(None, axes, None), P(None, axes, None)),
        check_vma=False,
    )
```

```python
import functools

import jax
import jax.numpy as jnp
import numpy as np
from jax import lax
from jax.experimental import pallas as pl
from jax.experimental.pallas import tpu as pltpu
from jax.sharding import Mesh, PartitionSpec as P

NPHI = 4096
BLOCK = 128
SEGMENTS = NPHI // BLOCK
LANES = 128
CHUNK = 192

NT = (((1,), (1,)), ((), ()))
TN = (((0,), (0,)), ((), ()))


def dot(a, b, dims=(((1,), (0,)), ((), ()))):
    return lax.dot_general(a, b, dims, preferred_element_type=jnp.float32)


def high_low(x):
    high = x.astype(jnp.bfloat16)
    return high, (x - high.astype(jnp.float32)).astype(jnp.bfloat16)


def np_high_low(x):
    high = x.astype(np.float32).astype(jnp.bfloat16)
    return high, (x - high.astype(np.float64)).astype(np.float32).astype(jnp.bfloat16)


def analysis_tables(orders):
    m = np.arange(orders, dtype=np.int64)[:, None]
    p = np.arange(BLOCK, dtype=np.int64)[None, :]
    angle = (m * p % NPHI) * (2 * np.pi / NPHI)
    inner = np.concatenate(np_high_low(np.cos(angle)) + np_high_low(-np.sin(angle)), 1)
    half = np.arange(2 * SEGMENTS, dtype=np.int64)[None, :]
    steps = 2 * BLOCK * (half % SEGMENTS) + half // SEGMENTS
    angle = (m * steps % (2 * NPHI)) * (np.pi / NPHI)
    outer = np.concatenate(np_high_low(np.cos(angle) / NPHI) + np_high_low(-np.sin(angle) / NPHI), 1)
    return inner, outer


def bit_groups(devices):
    bits = list(range(1, devices.bit_length() - 1))
    return [bits[i : i + 2] for i in range(0, len(bits), 2)]


def positions(devices):
    order = [0]
    for group in bit_groups(devices):
        order = [p | (v << group[0]) for p in order for v in range(1 << len(group))]
    return order


def slot_rows(orders, slots):
    out = np.zeros((orders // 2, orders), np.float32)
    for block, position in enumerate(positions(orders // slots)):
        for slot in range(slots):
            out[block * slots + slot, position * slots + slot] = 1
    return out.astype(jnp.bfloat16)


def rolled(x, shift):
    return jnp.concatenate([x[:, shift:], x[:, :shift]], 1)


def exclusive_or(table, me, slots):
    orders = table.shape[1]
    block = lax.div(lax.broadcasted_iota(jnp.int32, table.shape, 1), slots)
    for bit in range((orders // slots).bit_length() - 1):
        shift = slots << bit
        swapped = jnp.where((block >> bit) % 2 == 0, rolled(table, shift), rolled(table, orders - shift))
        table = jnp.where(jnp.broadcast_to((me >> bit) & 1, table.shape) == 1, swapped, table)
    return table


def hot(condition):
    return jnp.where(condition, 1.0, 0.0).astype(jnp.bfloat16)


def twice(x):
    return jnp.concatenate([x, x], 1)


def first_kernel(slots, blocks_here, staged, w_hbm, off_hbm, cnt_hbm, ids_hbm, table_hbm, rows_hbm, inner_hbm, outer_hbm, *refs):
    if staged:
        legendre_hbm, *refs = refs
    out_ref, table_ref, rows_ref, inner_ref, outer_ref, *refs = refs
    if staged:
        legendre_ref, *refs = refs
    w_ref, off_ref, cnt_ref, ids_ref, flat_ref, wide_ref, live_w_ref, live_off_ref, sems = refs
    pairs = (
        (cnt_hbm, cnt_ref), (ids_hbm, ids_ref), (off_hbm, off_ref), (w_hbm, w_ref),
        (table_hbm, flat_ref), (rows_hbm, rows_ref), (inner_hbm, inner_ref), (outer_hbm, outer_ref),
    )
    if staged:
        pairs = pairs + ((legendre_hbm.at[pl.ds(0, staged)], legendre_ref),)
    copies = [pltpu.make_async_copy(a, b, sems.at[i]) for i, (a, b) in enumerate(pairs)]
    for copy in copies[:4]:
        copy.start()
    groups = off_ref.shape[0]
    capacity, devices = ids_ref.shape
    bins, live, _ = live_w_ref.shape
    pack = 16
    key_tiles = (out_ref.shape[0] - bins * live) // pack

    owner = lax.div(lax.broadcasted_iota(jnp.int32, (devices, groups), 1), capacity)
    source = lax.broadcasted_iota(jnp.int32, (devices, groups), 0)
    member = lax.rem(lax.broadcasted_iota(jnp.int32, (capacity, groups), 1), capacity)
    own_row = lax.broadcasted_iota(jnp.int32, (capacity, groups), 0) == member
    for copy in copies[:2]:
        copy.wait()
    counts = jnp.broadcast_to(cnt_ref[...].astype(jnp.float32), (8, devices)).astype(jnp.bfloat16)
    count = dot(counts, hot(source == owner))[0:1, :]
    before = dot(counts, hot(source < owner))[0:1, :]
    number = member[0:1, :].astype(jnp.float32)
    place = jnp.where(number < count, before + number, -1.0).astype(jnp.int32)
    packing = hot(lax.broadcasted_iota(jnp.int32, (key_tiles * LANES, groups), 0) == place)

    ids = dot(ids_ref[...].astype(jnp.float32).astype(jnp.bfloat16), hot(source == owner))
    ids = jnp.sum(jnp.where(own_row, ids, 0.0), axis=0, keepdims=True)
    block = ids.astype(jnp.int32) + owner[0:1, :] * blocks_here
    cycle = lax.div(block, SEGMENTS)
    phase = lax.rem(cycle, 2) * SEGMENTS + lax.rem(block, SEGMENTS)
    row = lax.broadcasted_iota(jnp.int32, (pack, groups), 0)
    keys = jnp.where(row == 0, lax.div(cycle, 16), jnp.where(row == 1, lax.rem(cycle, 16), phase))
    keys = dot(keys.astype(jnp.float32).astype(jnp.bfloat16), packing, NT).astype(jnp.bfloat16)
    for tile in range(key_tiles):
        out_ref[bins * live + tile * pack : bins * live + (tile + 1) * pack, :] = keys[:, tile * LANES : (tile + 1) * LANES]

    for copy in copies[2:4]:
        copy.wait()
    for copy in copies[4:]:
        copy.start()
    packing = packing[:live, :]
    live_off_ref[...] = dot(packing, off_ref[...].astype(jnp.float32).astype(jnp.bfloat16))
    wide_ref[...] = w_ref[...].astype(jnp.float32)
    for b in range(bins):
        live_w_ref[b] = dot(packing, wide_ref[pl.ds(b, groups, stride=bins), :].astype(jnp.bfloat16)).astype(jnp.bfloat16)

    pixel = lax.broadcasted_iota(jnp.int32, (pack, BLOCK), 0)
    pixels = [(pixel + pack * k).astype(jnp.float32).astype(jnp.bfloat16) for k in range(BLOCK // pack)]
    alone = [hot(pixel == i) for i in range(pack)]
    one = jnp.ones((pack, BLOCK), jnp.bfloat16)
    zero = jnp.zeros((pack, BLOCK), jnp.bfloat16)

    def deposit(step, carry):
        start = pl.multiple_of(step * pack, pack)
        weights = [live_w_ref[b, pl.ds(start, pack), :] for b in range(bins)]
        left, right = [], []
        for i in range(pack):
            left.append(jnp.concatenate([w * alone[i] for w in weights], 0))
            at = jnp.broadcast_to(live_off_ref[pl.ds(start + i, 1), :], (pack, BLOCK)).astype(jnp.bfloat16)
            right.append(jnp.concatenate([jnp.where(at == x, one, zero) for x in pixels], 0))
        out = dot(jnp.concatenate(left, 1), jnp.concatenate(right, 1), NT).astype(jnp.bfloat16)
        for b in range(bins):
            out_ref[pl.ds(pl.multiple_of(b * live + start, pack), pack), :] = out[b * pack : (b + 1) * pack, :]
        return carry

    lax.fori_loop(0, live // pack, deposit, 0, unroll=9)
    for copy in copies[4:8]:
        copy.wait()
    me = lax.axis_index("blk")
    for axis in ("y", "core"):
        me = me * lax.axis_size(axis) + lax.axis_index(axis)
    table_ref[...] = exclusive_or(flat_ref[...].reshape(table_ref.shape), me, slots)
    for copy in copies[8:]:
        copy.wait()


def add_modes(bins, groups, cycles, groups_ref, inner_ref, outer_ref, add):
    pack = 16
    keys = groups_ref[bins * groups :, :].astype(jnp.float32)
    keys = jnp.concatenate([keys[i * pack : (i + 1) * pack, :] for i in range(keys.shape[0] // pack)], 1)
    cycle = (keys[0:1, :groups] * 16.0 + keys[1:2, :groups]).astype(jnp.int32)
    phase = keys[2:3, :groups].astype(jnp.int32)
    cycle_hot = hot(lax.broadcasted_iota(jnp.int32, (cycles, groups), 0) == cycle)
    half_hot = hot(lax.broadcasted_iota(jnp.int32, (2 * SEGMENTS, groups), 0) == phase)
    phase_hot = jnp.concatenate([half_hot, half_hot], 0)
    deposits = [twice(groups_ref[b * groups : (b + 1) * groups, :]) for b in range(bins)]
    for start in range(0, inner_ref.shape[0], 2 * CHUNK):
        rows = slice(start, start + 2 * CHUNK)
        outer = dot(outer_ref[rows, :], phase_hot)
        outer_cos, outer_sin = outer[:CHUNK, :], outer[CHUNK:, :]
        for b, deposit in enumerate(deposits):
            inner = dot(inner_ref[rows, :], deposit, NT)
            inner_cos, inner_sin = inner[:CHUNK, :], inner[CHUNK:, :]
            real = inner_cos * outer_cos - inner_sin * outer_sin
            imag = inner_cos * outer_sin + inner_sin * outer_cos
            both = dot(jnp.concatenate([real, imag], 0).astype(jnp.bfloat16), cycle_hot, NT)
            for part in range(2):
                value = both[part * CHUNK : (part + 1) * CHUNK, :]
                for tile in range(cycles // LANES):
                    add(b * (cycles // LANES) + tile, start + part, value[:, tile * LANES : (tile + 1) * LANES])


def own_kernel(bins, groups, cycles, staged, groups_ref, table_ref, rows_ref, inner_ref, outer_ref, *refs):
    if staged:
        legendre_hbm, out_ref, inner_out, outer_out, legendre_ref, sem = refs
        late = pltpu.make_async_copy(legendre_hbm.at[pl.ds(staged, legendre_ref.shape[0])], legendre_ref, sem)
        late.start()
    else:
        out_ref, inner_out, outer_out = refs
    count, orders = rows_ref.shape
    held = hot(lax.broadcasted_iota(jnp.int32, (orders, orders), 0) == table_ref[...])
    for start in range(0, count, CHUNK):
        pick = dot(rows_ref[start : start + CHUNK, :], held, NT).astype(jnp.bfloat16)
        inner = dot(pick, inner_ref[...]).astype(jnp.bfloat16)
        outer = dot(pick, outer_ref[...]).astype(jnp.bfloat16)
        for part in range(2):
            rows = slice(2 * start + part * CHUNK, 2 * start + (part + 1) * CHUNK)
            inner_out[rows, :] = inner[:, part * 2 * BLOCK : (part + 1) * 2 * BLOCK]
            outer_out[rows, :] = outer[:, part * BLOCK : (part + 1) * BLOCK]

    def add(tile, first, value):
        out_ref.at[tile][pl.ds(first, value.shape[0], stride=2), :] = value

    add_modes(bins, groups, cycles, groups_ref, inner_out, outer_out, add)
    if staged:
        late.wait()


def split_sum(parts, tile, keep_ref, send_refs):
    rows = keep_ref.shape[0]
    lanes = slice(tile * LANES, (tile + 1) * LANES)
    for i, out_ref in enumerate((keep_ref, *send_refs)):
        value = sum(part(slice(i * rows, (i + 1) * rows), lanes) for part in parts)
        out_ref[:, lanes] = value.astype(out_ref.dtype)


def send_order(ways):
    return [(1, 2), (3, 3), (2, 1)] if ways == 4 else [(i, i) for i in range(1, ways)]


def other_kernel(bins, groups, cycles, groups_ref, inner_ref, outer_ref, own_ref, keep_ref, *refs):
    *send_refs, other_ref = refs

    def add(tile, first, value):
        other_ref.at[tile][pl.ds(first, value.shape[0], stride=2), :] = value

    add_modes(bins, groups, cycles, groups_ref, inner_ref, outer_ref, add)
    rows = keep_ref.shape[0]
    core = lax.axis_index("core")
    blocks = [(0, 0)] + send_order(len(send_refs) + 1)
    for (even, odd), out_ref in zip(blocks, (keep_ref, *send_refs)):
        first = even * rows if even == odd else pl.multiple_of((even + core * (odd - even)) * rows, rows)
        for tile in range(own_ref.shape[0]):
            value = own_ref[tile, pl.ds(first, rows), :] + other_ref[tile, pl.ds(first, rows), :]
            out_ref[:, tile * LANES : (tile + 1) * LANES] = value.astype(out_ref.dtype)


def merge_kernel(count, kept_ref, *refs):
    arrived, outs = refs[:count], refs[count:]
    for tile in range(kept_ref.shape[1] // LANES):
        parts = [lambda rows, lanes, ref=ref: ref[rows, lanes].astype(jnp.float32) for ref in (kept_ref, *arrived)]
        split_sum(parts, tile, outs[0], outs[1:])


def gain_column(degrees):
    l = np.arange(degrees, dtype=np.float32)
    return np.where(l > 0.5, np.float32(-20000.0) / np.maximum(l * (l + 1), np.float32(1)), np.float32(0)).astype(np.float32)[:, None] * np.ones((1, BLOCK), np.float32)


def interleave(cycles, cycles_here):
    out = np.zeros((2 * cycles, 2 * cycles), np.float32)
    for f in range(2):
        for c in range(cycles):
            out[f * cycles + c, (c // cycles_here * 2 + f) * cycles_here + c % cycles_here] = 1
    return out.astype(jnp.bfloat16)


def respond(basis, gain_ref, order_ref, out_ref, slot):
    cycles = basis.shape[1]
    gain = jnp.concatenate([gain_ref[...]] * (cycles // BLOCK), 1)
    gained = (basis.astype(jnp.float32) * gain).astype(jnp.bfloat16)
    high, low = high_low(dot(basis, jnp.concatenate([basis, gained], 1), TN))
    out_ref[slot] = dot(jnp.concatenate([high, low], 0), order_ref[...]).astype(jnp.bfloat16)


def staged_response_kernel(start, early_ref, late_ref, gain_ref, order_ref, out_ref):
    early = early_ref.shape[0]
    for slot in range(out_ref.shape[0]):
        at = start + slot
        respond(early_ref[at] if at < early else late_ref[at - early], gain_ref, order_ref, out_ref, slot)


def response_kernel(start, legendre_hbm, gain_ref, order_ref, out_ref, legendre_ref, sems):
    count = out_ref.shape[0]
    copies = [pltpu.make_async_copy(legendre_hbm.at[start + i], legendre_ref.at[i], sems.at[i]) for i in range(count)]
    for copy in copies:
        copy.start()
    for slot in range(count):
        copies[slot].wait()
        respond(legendre_ref[slot], gain_ref, order_ref, out_ref, slot)


def slot_order(slots, bins):
    out = np.zeros((slots * 2 * bins, slots * 2 * bins), np.float32)
    for b in range(bins):
        for c in range(2):
            for t in range(slots):
                out[(t * 2 + c) * bins + b, (b * slots + t) * 2 + c] = 1
    return out.astype(jnp.bfloat16)


def synthesis_kernel(arrivals, pieces, kept_ref, *refs):
    partials, refs = refs[:arrivals], refs[arrivals:]
    response_refs, (order_ref, out_ref) = refs[:pieces], refs[pieces:]
    cycles = response_refs[0].shape[1] // 2
    bins = kept_ref.shape[1] // cycles
    slots = kept_ref.shape[0] // 2
    responses = [ref.at[i] for ref in response_refs for i in range(ref.shape[0])]
    total = kept_ref[...]
    for ref in partials:
        total = total + ref[...].astype(jnp.float32)
    modes = jnp.concatenate([total[:, b * cycles : (b + 1) * cycles] for b in range(bins)], 0)
    high, low = high_low(modes)
    high = dot(order_ref[...], high)
    low = dot(order_ref[...], low)
    per_slot = 2 * bins
    parts = []
    for t in range(slots):
        rows = slice(t * per_slot, (t + 1) * per_slot)
        left = jnp.concatenate([high[rows, :], low[rows, :]], 0).astype(jnp.bfloat16)
        part = dot(twice(left), responses[t][...])
        parts.append(part[:per_slot, :] + part[per_slot:, :])
    parts.append(jnp.zeros((128 - slots * per_slot, 2 * cycles), jnp.float32))
    result = jnp.concatenate(parts, 0)
    out_ref[...] = jnp.transpose(result).astype(jnp.bfloat16)


def order_classes(orders):
    return [np.arange(0, orders, 4), np.arange(2, orders, 4), np.arange(1, orders, 2)]


def inverse_tables(orders):
    quarter = NPHI // 4
    k = np.arange(quarter, dtype=np.int64)[None, :]
    rows = []
    for m in order_classes(orders):
        angle = (m[:, None] * k % NPHI) * (2 * np.pi / NPHI)
        rows += [np.cos(angle), -np.sin(angle)]
    return np.concatenate(np.split(np.concatenate(rows), quarter // 512, axis=1)).astype(np.float32).astype(jnp.bfloat16)


def padded(count):
    return -(-count // LANES) * LANES


def order_lanes(orders):
    out = []
    for m in order_classes(orders):
        out.append(np.concatenate([m, np.full(padded(len(m)) - len(m), -1)]))
    return np.concatenate(out).astype(np.int32)[None, :]


def turn_rows(order_row):
    m = np.maximum(order_row[0], 0).astype(np.float64)
    weight = np.where(order_row[0] == 0, 1.0, 2.0)
    sign = np.where(order_row[0] % 4 == 3, 1.0, -1.0)
    parts = np_high_low(np.cos(np.pi * m / NPHI) * weight) + np_high_low(np.sin(np.pi * m / NPHI) * weight)
    parts = parts + (weight.astype(jnp.bfloat16), sign.astype(jnp.bfloat16))
    return np.stack(parts + (np.zeros_like(parts[0]),) * 10)


def part_rows(part, bins, cycles_here):
    shape = (2 * bins * cycles_here, 4 * bins * cycles_here)
    row = lax.broadcasted_iota(jnp.int32, shape, 0)
    column = lax.broadcasted_iota(jnp.int32, shape, 1)
    cycle = lax.rem(row, cycles_here)
    bin_number = lax.rem(lax.div(row, cycles_here), bins)
    filter_number = lax.div(row, cycles_here * bins)
    return hot(column == ((filter_number * cycles_here + cycle) * 2 + part) * bins + bin_number)


def inverse_kernel(arrived_ref, slots_ref, turn_hbm, table_hbm, kappa_hbm, potential_hbm,
                   turn_ref, table_ref, wide_ref, kappa_ref, potential_ref, sems, out_sems):
    copies = [pltpu.make_async_copy(turn_hbm, turn_ref, sems.at[0])]
    quarter = NPHI // 4
    chunk = table_ref.shape[1]
    chunks = quarter // chunk
    part = table_ref.shape[0] // chunks
    for i in range(chunks):
        rows = pl.ds(i * part, part)
        copies.append(pltpu.make_async_copy(table_hbm.at[rows], table_ref.at[rows], sems.at[1 + i]))
    for copy in copies:
        copy.start()
    devices, slots = slots_ref.shape
    bins, cycles_here, _ = kappa_ref.shape
    order_count = part // 2
    per_slot = 2 * bins
    per_source = 2 * cycles_here
    wide_ref[...] = arrived_ref[...].astype(jnp.float32)
    turned = [jnp.transpose(wide_ref[pl.ds(i, devices, stride=per_source), :]) for i in range(per_source)]
    few, many = order_count // 4, order_count // 2
    starts = [0, padded(few), 2 * padded(few)]
    lane = lax.broadcasted_iota(jnp.int32, (1, turn_ref.shape[1]), 1)
    orders = jnp.where(lane < few, 4 * lane, -1)
    within = lane - starts[1]
    orders = jnp.where((within >= 0) & (within < few), 4 * within + 2, orders)
    within = lane - starts[2]
    orders = jnp.where((within >= 0) & (within < many), 2 * within + 1, orders)
    lefts, picks = [], []
    for t in range(slots):
        lefts.append(jnp.concatenate([x[t * per_slot : (t + 1) * per_slot, :] for x in turned], 0))
        picks.append(hot(slots_ref[:, t : t + 1] == orders))
    spectrum = dot(jnp.concatenate(lefts, 1).astype(jnp.bfloat16), jnp.concatenate(picks, 0))
    spectrum = spectrum.astype(jnp.bfloat16)
    real_in = dot(part_rows(0, bins, cycles_here), spectrum)
    imag_in = dot(part_rows(1, bins, cycles_here), spectrum)
    copies[0].wait()
    turn = turn_ref[...].astype(jnp.float32)
    odd = lax.rem(lax.rem(lax.broadcasted_iota(jnp.int32, real_in.shape, 0), cycles_here), 2) == 1
    turn_cos = jnp.where(odd, turn[0:1, :] + turn[1:2, :], turn[4:5, :])
    turn_sin = jnp.where(odd, turn[2:3, :] + turn[3:4, :], 0.0)
    real = real_in * turn_cos - imag_in * turn_sin
    imag = real_in * turn_sin + imag_in * turn_cos
    sign = turn[5:6, starts[2] :]
    count = real.shape[0]
    lefts = []
    for index, start in enumerate(starts):
        lanes = slice(start, start + (few if index < 2 else many))
        cos_rows, sin_rows = [real[:, lanes]], [imag[:, lanes]]
        if index == 2:
            cos_rows.append(imag[:, lanes] * sign[:, :many])
            sin_rows.append(-real[:, lanes] * sign[:, :many])
        for rows in (cos_rows, sin_rows):
            lefts.append(jnp.concatenate([y for x in rows for y in high_low(x)], 0))
    results = []
    for index in range(chunks):
        copies[1 + index].wait()
        row = index * part
        sums = []
        for at in range(3):
            height = few if at < 2 else many
            both = dot(lefts[2 * at], table_ref[row : row + height, :])
            both = both + dot(lefts[2 * at + 1], table_ref[row + height : row + 2 * height, :])
            row += 2 * height
            sums += [both[i : i + count, :] + both[i + count : i + 2 * count, :] for i in range(0, both.shape[0], 2 * count)]
        even, other = sums[0] + sums[1], sums[0] - sums[1]
        values = (even + sums[2], other + sums[3], even - sums[2], other - sums[3])
        for j, value in enumerate(values):
            lanes = pl.ds(j * quarter + index * chunk, chunk)
            for f, (out_ref, out_hbm) in enumerate(((kappa_ref, kappa_hbm), (potential_ref, potential_hbm))):
                for b in range(bins):
                    at = (f * bins + b) * cycles_here
                    out_ref[b, :, lanes] = value[at : at + cycles_here, :]
                copy = pltpu.make_async_copy(out_ref.at[:, :, lanes], out_hbm.at[:, :, lanes], out_sems.at[len(results)])
                copy.start()
                results.append(copy)
    for copy in results:
        copy.wait()


def in_hbm(x):
    return pltpu.with_memory_space_constraint(jnp.asarray(x), pltpu.HBM)


def params(orders):
    small = 14 if orders <= 512 else 56
    return pltpu.CompilerParams(vmem_limit_bytes=small * 1024 * 1024)


def per_device(weights, offsets, counts, block_ids, m_table, legendre):
    axes = ("blk", "y", "core")
    _, devices, capacity, bins, _ = weights.shape
    slots, degrees, cycles = legendre.shape
    orders = m_table.shape[0]
    groups = devices * capacity
    cycles_here = cycles // devices
    width = bins * cycles
    staged = legendre.size <= 4 * 1024 * 1024
    limits = params(orders)
    hbm = pl.BlockSpec(memory_space=pltpu.HBM)
    vmem = pl.BlockSpec(memory_space=pltpu.VMEM)

    def shaped(*shape, dtype=jnp.bfloat16):
        return jax.ShapeDtypeStruct(shape, dtype)

    rows = slot_rows(orders, slots)
    inner, outer = analysis_tables(orders)
    live = (capacity + 1) * devices // 2
    key_rows = -(-live // LANES) * 16
    shapes = [
        shaped(bins * live + key_rows, BLOCK),
        shaped(1, orders, dtype=jnp.int32),
        shaped(*rows.shape),
        shaped(*inner.shape),
        shaped(*outer.shape),
    ]
    operands = [
        weights.reshape(groups * bins, BLOCK),
        offsets.reshape(groups, BLOCK),
        counts,
        jnp.transpose(block_ids[0]),
        m_table,
        rows,
        inner,
        outer,
    ]
    ahead = slots * 5 // 6 if staged else 0
    if staged:
        shapes.append(shaped(ahead, degrees, cycles))
        operands.append(legendre)
    deposits, *shared = pl.pallas_call(
        functools.partial(first_kernel, slots, cycles_here * SEGMENTS, ahead),
        in_specs=[hbm] * len(operands),
        out_specs=(vmem,) * len(shapes),
        out_shape=tuple(shapes),
        scratch_shapes=[
            pltpu.VMEM((groups * bins, BLOCK), jnp.bfloat16),
            pltpu.VMEM((groups, BLOCK), jnp.int32),
            pltpu.VMEM((1, devices), jnp.int32),
            pltpu.VMEM((capacity, devices), jnp.int32),
            pltpu.VMEM((orders,), jnp.int32),
            pltpu.VMEM((groups * bins, BLOCK), jnp.float32),
            pltpu.VMEM((bins, live, BLOCK), jnp.bfloat16),
            pltpu.VMEM((live, BLOCK), jnp.float32),
            pltpu.SemaphoreType.DMA((len(operands),)),
        ],
        compiler_params=limits,
        name="deposit",
    )(*[in_hbm(x) for x in operands])
    early = shared.pop() if staged else None

    def swap(x, mask, odd_mask=None):
        masks = (mask, mask if odd_mask is None else odd_mask)
        return lax.ppermute(x, axes, [(i, i ^ masks[i % 2]) for i in range(devices)])

    other = swap(deposits, 1)
    cost = pl.CostEstimate(flops=8 * orders * 256 * bins * live, bytes_accessed=4 * orders * width, transcendentals=0)
    modes_shape = (width // LANES, orders, LANES)
    own, own_inner, own_outer, *late = pl.pallas_call(
        functools.partial(own_kernel, bins, live, cycles, ahead),
        in_specs=[vmem] * 5 + [hbm] * staged,
        out_specs=(vmem,) * (3 + staged),
        out_shape=(
            shaped(*modes_shape, dtype=jnp.float32),
            shaped(orders, inner.shape[1] // 2),
            shaped(orders, outer.shape[1] // 2),
        ) + (shaped(slots - ahead, degrees, cycles),) * staged,
        scratch_shapes=[pltpu.SemaphoreType.DMA] * staged,
        compiler_params=limits,
        cost_estimate=cost,
        name="own_groups",
    )(deposits, *shared, *[in_hbm(legendre)] * staged)

    basis = [early, *late] if staged else [legendre]

    groups_of_bits = bit_groups(devices)
    stages = len(groups_of_bits)
    gain, order = gain_column(degrees), interleave(cycles, cycles_here)
    blocks = devices // 2
    kernel, inputs = functools.partial(other_kernel, bins, live, cycles), (other, own_inner, own_outer, own)
    scratch = [pltpu.VMEM(modes_shape, jnp.float32)]
    responses = []
    for stage, bits in enumerate(groups_of_bits):
        ways = 1 << len(bits)
        blocks //= ways
        rows_here = blocks * 2 * slots
        kept, *sends = pl.pallas_call(
            kernel,
            in_specs=[vmem] * len(inputs),
            out_specs=(vmem,) * ways,
            out_shape=(shaped(rows_here, width, dtype=jnp.float32),) + (shaped(rows_here, width),) * (ways - 1),
            scratch_shapes=scratch,
            compiler_params=limits,
            name="merge" if stage else "other_groups",
        )(*inputs)
        sends, basis = lax.optimization_barrier((sends, basis))
        if stage == 0:
            order_of = send_order(ways)
            arrived = [swap(x, even << bits[0], odd << bits[0]) for x, (even, odd) in zip(sends, order_of)]
        else:
            line = [2, 3, 1] if ways == 4 else range(ways - 1, 0, -1)
            arrived = [swap(sends[i - 1], i << bits[0]) for i in line]
        first, last = (-(-slots * k * (2 * stages + 1 - k) // (stages * (stages + 1))) for k in (stage, stage + 1))
        count = last - first
        shape = shaped(count, 2 * cycles, 2 * cycles)
        cost = pl.CostEstimate(
            flops=6 * count * degrees * cycles * cycles, bytes_accessed=2 * count * degrees * cycles, transcendentals=0
        )
        if staged:
            kernel, scratch = functools.partial(staged_response_kernel, first), []
        else:
            kernel = functools.partial(response_kernel, first)
            scratch = [pltpu.VMEM((count, degrees, cycles), jnp.bfloat16), pltpu.SemaphoreType.DMA((count,))]
        response = pl.pallas_call(
            kernel,
            in_specs=[vmem if staged else hbm] * len(basis) + [vmem] * 2,
            out_specs=vmem,
            out_shape=shape,
            scratch_shapes=scratch,
            compiler_params=limits,
            cost_estimate=cost,
            name="response",
        )(*basis if staged else [in_hbm(x) for x in basis], gain, order)
        *arrived, response = lax.optimization_barrier((*arrived, response))
        responses.append(response)
        kernel, inputs, scratch = functools.partial(merge_kernel, len(arrived)), (kept, *arrived), []

    outgoing = pl.pallas_call(
        functools.partial(synthesis_kernel, len(inputs) - 1, len(responses)),
        in_specs=[vmem] * (len(inputs) + len(responses) + 1),
        out_specs=vmem,
        out_shape=shaped(2 * cycles, 128),
        compiler_params=limits,
        name="synthesis",
    )(*inputs, *responses, slot_order(slots, bins))
    outgoing = outgoing.reshape(devices, 2 * cycles_here, 128)
    outgoing, held = lax.optimization_barrier((outgoing, m_table))
    arrived = lax.all_to_all(outgoing, axes, split_axis=0, concat_axis=0, tiled=True)
    arrived = arrived.reshape(2 * cycles, 128)
    if staged:
        arrived = pltpu.with_memory_space_constraint(arrived, pltpu.VMEM)

    lanes = order_lanes(orders)
    constants = [turn_rows(lanes), inverse_tables(orders)]
    chunks = NPHI // 4 // constants[-1].shape[1]
    map_shape = shaped(bins, cycles_here, NPHI, dtype=jnp.float32)
    return pl.pallas_call(
        inverse_kernel,
        in_specs=[vmem] * 2 + [hbm] * 2,
        out_specs=(hbm, hbm),
        out_shape=(map_shape, map_shape),
        scratch_shapes=[
            *[pltpu.VMEM(x.shape, x.dtype) for x in constants],
            pltpu.VMEM((2 * cycles, 128), jnp.float32),
            pltpu.VMEM(map_shape.shape, jnp.float32),
            pltpu.VMEM(map_shape.shape, jnp.float32),
            pltpu.SemaphoreType.DMA((1 + chunks,)),
            pltpu.SemaphoreType.DMA((8 * chunks,)),
        ],
        compiler_params=limits,
        name="inverse",
    )(arrived, held.reshape(devices, slots), *[in_hbm(x) for x in constants])


def solution(mesh):
    blocks, columns = mesh.devices.shape
    fine = Mesh(mesh.devices.reshape(blocks, columns // 2, 2), ("blk", "y", "core"))
    axes = ("blk", "y", "core")
    placed = (
        P(axes, None, None, None, None),
        P(axes, None, None, None),
        P(axes, None),
        P(axes, None, None),
        P(),
        P(axes, None, None),
    )
    return jax.shard_map(
        per_device,
        mesh=fine,
        in_specs=placed,
        out_specs=(P(None, axes, None), P(None, axes, None)),
        check_vma=False,
    )
```

```python
import functools

import jax
import jax.numpy as jnp
import numpy as np
from jax import lax
from jax.experimental import pallas as pl
from jax.experimental.pallas import tpu as pltpu
from jax.sharding import Mesh, PartitionSpec as P

NPHI = 4096
BLOCK = 128
SEGMENTS = NPHI // BLOCK
LANES = 128
CHUNK = 192

NT = (((1,), (1,)), ((), ()))
TN = (((0,), (0,)), ((), ()))


def dot(a, b, dims=(((1,), (0,)), ((), ()))):
    return lax.dot_general(a, b, dims, preferred_element_type=jnp.float32)


def high_low(x):
    high = x.astype(jnp.bfloat16)
    return high, (x - high.astype(jnp.float32)).astype(jnp.bfloat16)


def np_high_low(x):
    high = x.astype(np.float32).astype(jnp.bfloat16)
    return high, (x - high.astype(np.float64)).astype(np.float32).astype(jnp.bfloat16)


def analysis_tables(orders):
    m = np.arange(orders, dtype=np.int64)[:, None]
    p = np.arange(BLOCK, dtype=np.int64)[None, :]
    angle = (m * p % NPHI) * (2 * np.pi / NPHI)
    inner = np.concatenate(np_high_low(np.cos(angle)) + np_high_low(-np.sin(angle)), 1)
    half = np.arange(2 * SEGMENTS, dtype=np.int64)[None, :]
    steps = 2 * BLOCK * (half % SEGMENTS) + half // SEGMENTS
    angle = (m * steps % (2 * NPHI)) * (np.pi / NPHI)
    outer = np.concatenate(np_high_low(np.cos(angle) / NPHI) + np_high_low(-np.sin(angle) / NPHI), 1)
    return inner, outer


def bit_groups(devices):
    bits = list(range(1, devices.bit_length() - 1))
    return [bits[i : i + 2] for i in range(0, len(bits), 2)]


def positions(devices):
    order = [0]
    for group in bit_groups(devices):
        order = [p | (v << group[0]) for p in order for v in range(1 << len(group))]
    return order


def slot_rows(orders, slots):
    out = np.zeros((orders // 2, orders), np.float32)
    for block, position in enumerate(positions(orders // slots)):
        for slot in range(slots):
            out[block * slots + slot, position * slots + slot] = 1
    return out.astype(jnp.bfloat16)


def rolled(x, shift):
    return jnp.concatenate([x[:, shift:], x[:, :shift]], 1)


def exclusive_or(table, me, slots):
    orders = table.shape[1]
    block = lax.div(lax.broadcasted_iota(jnp.int32, table.shape, 1), slots)
    for bit in range((orders // slots).bit_length() - 1):
        shift = slots << bit
        swapped = jnp.where((block >> bit) % 2 == 0, rolled(table, shift), rolled(table, orders - shift))
        table = jnp.where(jnp.broadcast_to((me >> bit) & 1, table.shape) == 1, swapped, table)
    return table


def hot(condition):
    return jnp.where(condition, 1.0, 0.0).astype(jnp.bfloat16)


def twice(x):
    return jnp.concatenate([x, x], 1)


def first_kernel(slots, blocks_here, staged, w_hbm, off_hbm, cnt_hbm, ids_hbm, table_hbm, rows_hbm, inner_hbm, outer_hbm, *refs):
    if staged:
        legendre_hbm, *refs = refs
    out_ref, table_ref, rows_ref, inner_ref, outer_ref, *refs = refs
    if staged:
        legendre_ref, *refs = refs
    w_ref, off_ref, cnt_ref, ids_ref, flat_ref, wide_ref, live_w_ref, live_off_ref, sems = refs
    pairs = (
        (cnt_hbm, cnt_ref), (ids_hbm, ids_ref), (off_hbm, off_ref), (w_hbm, w_ref),
        (table_hbm, flat_ref), (rows_hbm, rows_ref), (inner_hbm, inner_ref), (outer_hbm, outer_ref),
    )
    if staged:
        pairs = pairs + ((legendre_hbm.at[pl.ds(0, staged)], legendre_ref),)
    copies = [pltpu.make_async_copy(a, b, sems.at[i]) for i, (a, b) in enumerate(pairs)]
    for copy in copies[:4]:
        copy.start()
    groups = off_ref.shape[0]
    capacity, devices = ids_ref.shape
    bins, live, _ = live_w_ref.shape
    pack = 16
    key_tiles = (out_ref.shape[0] - bins * live) // pack

    owner = lax.div(lax.broadcasted_iota(jnp.int32, (devices, groups), 1), capacity)
    source = lax.broadcasted_iota(jnp.int32, (devices, groups), 0)
    member = lax.rem(lax.broadcasted_iota(jnp.int32, (capacity, groups), 1), capacity)
    own_row = lax.broadcasted_iota(jnp.int32, (capacity, groups), 0) == member
    for copy in copies[:2]:
        copy.wait()
    counts = jnp.broadcast_to(cnt_ref[...].astype(jnp.float32), (8, devices)).astype(jnp.bfloat16)
    count = dot(counts, hot(source == owner))[0:1, :]
    before = dot(counts, hot(source < owner))[0:1, :]
    number = member[0:1, :].astype(jnp.float32)
    place = jnp.where(number < count, before + number, -1.0).astype(jnp.int32)
    packing = hot(lax.broadcasted_iota(jnp.int32, (key_tiles * LANES, groups), 0) == place)

    ids = dot(ids_ref[...].astype(jnp.float32).astype(jnp.bfloat16), hot(source == owner))
    ids = jnp.sum(jnp.where(own_row, ids, 0.0), axis=0, keepdims=True)
    block = ids.astype(jnp.int32) + owner[0:1, :] * blocks_here
    cycle = lax.div(block, SEGMENTS)
    phase = lax.rem(cycle, 2) * SEGMENTS + lax.rem(block, SEGMENTS)
    row = lax.broadcasted_iota(jnp.int32, (pack, groups), 0)
    keys = jnp.where(row == 0, lax.div(cycle, 16), jnp.where(row == 1, lax.rem(cycle, 16), phase))
    keys = dot(keys.astype(jnp.float32).astype(jnp.bfloat16), packing, NT).astype(jnp.bfloat16)
    for tile in range(key_tiles):
        out_ref[bins * live + tile * pack : bins * live + (tile + 1) * pack, :] = keys[:, tile * LANES : (tile + 1) * LANES]

    for copy in copies[2:4]:
        copy.wait()
    for copy in copies[4:]:
        copy.start()
    packing = packing[:live, :]
    live_off_ref[...] = dot(packing, off_ref[...].astype(jnp.float32).astype(jnp.bfloat16))
    wide_ref[...] = w_ref[...].astype(jnp.float32)
    for b in range(bins):
        live_w_ref[b] = dot(packing, wide_ref[pl.ds(b, groups, stride=bins), :].astype(jnp.bfloat16)).astype(jnp.bfloat16)

    pixel = lax.broadcasted_iota(jnp.int32, (pack, BLOCK), 0)
    pixels = [(pixel + pack * k).astype(jnp.float32).astype(jnp.bfloat16) for k in range(BLOCK // pack)]
    alone = [hot(pixel == i) for i in range(pack)]
    one = jnp.ones((pack, BLOCK), jnp.bfloat16)
    zero = jnp.zeros((pack, BLOCK), jnp.bfloat16)

    def deposit(step, carry):
        start = pl.multiple_of(step * pack, pack)
        weights = [live_w_ref[b, pl.ds(start, pack), :] for b in range(bins)]
        left, right = [], []
        for i in range(pack):
            left.append(jnp.concatenate([w * alone[i] for w in weights], 0))
            at = jnp.broadcast_to(live_off_ref[pl.ds(start + i, 1), :], (pack, BLOCK)).astype(jnp.bfloat16)
            right.append(jnp.concatenate([jnp.where(at == x, one, zero) for x in pixels], 0))
        out = dot(jnp.concatenate(left, 1), jnp.concatenate(right, 1), NT).astype(jnp.bfloat16)
        for b in range(bins):
            out_ref[pl.ds(pl.multiple_of(b * live + start, pack), pack), :] = out[b * pack : (b + 1) * pack, :]
        return carry

    lax.fori_loop(0, live // pack, deposit, 0, unroll=9)
    for copy in copies[4:8]:
        copy.wait()
    me = lax.axis_index("blk")
    for axis in ("y", "core"):
        me = me * lax.axis_size(axis) + lax.axis_index(axis)
    table_ref[...] = exclusive_or(flat_ref[...].reshape(table_ref.shape), me, slots)
    for copy in copies[8:]:
        copy.wait()


def add_modes(bins, groups, cycles, groups_ref, inner_ref, outer_ref, add):
    pack = 16
    keys = groups_ref[bins * groups :, :].astype(jnp.float32)
    keys = jnp.concatenate([keys[i * pack : (i + 1) * pack, :] for i in range(keys.shape[0] // pack)], 1)
    cycle = (keys[0:1, :groups] * 16.0 + keys[1:2, :groups]).astype(jnp.int32)
    phase = keys[2:3, :groups].astype(jnp.int32)
    cycle_hot = hot(lax.broadcasted_iota(jnp.int32, (cycles, groups), 0) == cycle)
    half_hot = hot(lax.broadcasted_iota(jnp.int32, (2 * SEGMENTS, groups), 0) == phase)
    phase_hot = jnp.concatenate([half_hot, half_hot], 0)
    deposits = [twice(groups_ref[b * groups : (b + 1) * groups, :]) for b in range(bins)]
    for start in range(0, inner_ref.shape[0], 2 * CHUNK):
        rows = slice(start, start + 2 * CHUNK)
        outer = dot(outer_ref[rows, :], phase_hot)
        outer_cos, outer_sin = outer[:CHUNK, :], outer[CHUNK:, :]
        for b, deposit in enumerate(deposits):
            inner = dot(inner_ref[rows, :], deposit, NT)
            inner_cos, inner_sin = inner[:CHUNK, :], inner[CHUNK:, :]
            real = inner_cos * outer_cos - inner_sin * outer_sin
            imag = inner_cos * outer_sin + inner_sin * outer_cos
            both = dot(jnp.concatenate([real, imag], 0).astype(jnp.bfloat16), cycle_hot, NT)
            for part in range(2):
                value = both[part * CHUNK : (part + 1) * CHUNK, :]
                for tile in range(cycles // LANES):
                    add(b * (cycles // LANES) + tile, start + part, value[:, tile * LANES : (tile + 1) * LANES])


def own_kernel(bins, groups, cycles, staged, groups_ref, table_ref, rows_ref, inner_ref, outer_ref, *refs):
    if staged:
        legendre_hbm, out_ref, inner_out, outer_out, legendre_ref, sem = refs
        late = pltpu.make_async_copy(legendre_hbm.at[pl.ds(staged, legendre_ref.shape[0])], legendre_ref, sem)
        late.start()
    else:
        out_ref, inner_out, outer_out = refs
    count, orders = rows_ref.shape
    held = hot(lax.broadcasted_iota(jnp.int32, (orders, orders), 0) == table_ref[...])
    for start in range(0, count, CHUNK):
        pick = dot(rows_ref[start : start + CHUNK, :], held, NT).astype(jnp.bfloat16)
        inner = dot(pick, inner_ref[...]).astype(jnp.bfloat16)
        outer = dot(pick, outer_ref[...]).astype(jnp.bfloat16)
        for part in range(2):
            rows = slice(2 * start + part * CHUNK, 2 * start + (part + 1) * CHUNK)
            inner_out[rows, :] = inner[:, part * 2 * BLOCK : (part + 1) * 2 * BLOCK]
            outer_out[rows, :] = outer[:, part * BLOCK : (part + 1) * BLOCK]

    def add(tile, first, value):
        out_ref.at[tile][pl.ds(first, value.shape[0], stride=2), :] = value

    add_modes(bins, groups, cycles, groups_ref, inner_out, outer_out, add)
    if staged:
        late.wait()


def split_sum(parts, tile, keep_ref, send_refs):
    rows = keep_ref.shape[0]
    lanes = slice(tile * LANES, (tile + 1) * LANES)
    for i, out_ref in enumerate((keep_ref, *send_refs)):
        value = sum(part(slice(i * rows, (i + 1) * rows), lanes) for part in parts)
        out_ref[:, lanes] = value.astype(out_ref.dtype)


def send_order(ways):
    return [(1, 2), (3, 3), (2, 1)] if ways == 4 else [(i, i) for i in range(1, ways)]


def other_kernel(bins, groups, cycles, groups_ref, inner_ref, outer_ref, own_ref, keep_ref, *refs):
    *send_refs, other_ref = refs

    def add(tile, first, value):
        other_ref.at[tile][pl.ds(first, value.shape[0], stride=2), :] = value

    add_modes(bins, groups, cycles, groups_ref, inner_ref, outer_ref, add)
    rows = keep_ref.shape[0]
    core = lax.axis_index("core")
    blocks = [(0, 0)] + send_order(len(send_refs) + 1)
    for (even, odd), out_ref in zip(blocks, (keep_ref, *send_refs)):
        first = even * rows if even == odd else pl.multiple_of((even + core * (odd - even)) * rows, rows)
        for tile in range(own_ref.shape[0]):
            value = own_ref[tile, pl.ds(first, rows), :] + other_ref[tile, pl.ds(first, rows), :]
            out_ref[:, tile * LANES : (tile + 1) * LANES] = value.astype(out_ref.dtype)


def merge_kernel(count, kept_ref, *refs):
    arrived, outs = refs[:count], refs[count:]
    for tile in range(kept_ref.shape[1] // LANES):
        parts = [lambda rows, lanes, ref=ref: ref[rows, lanes].astype(jnp.float32) for ref in (kept_ref, *arrived)]
        split_sum(parts, tile, outs[0], outs[1:])


def gain_column(degrees):
    l = np.arange(degrees, dtype=np.float32)
    return np.where(l > 0.5, np.float32(-20000.0) / np.maximum(l * (l + 1), np.float32(1)), np.float32(0)).astype(np.float32)[:, None] * np.ones((1, BLOCK), np.float32)


def interleave(cycles, cycles_here):
    out = np.zeros((2 * cycles, 2 * cycles), np.float32)
    for f in range(2):
        for c in range(cycles):
            out[f * cycles + c, (c // cycles_here * 2 + f) * cycles_here + c % cycles_here] = 1
    return out.astype(jnp.bfloat16)


def respond(basis, gain_ref, order_ref, out_ref, slot):
    cycles = basis.shape[1]
    gain = jnp.concatenate([gain_ref[...]] * (cycles // BLOCK), 1)
    gained = (basis.astype(jnp.float32) * gain).astype(jnp.bfloat16)
    high, low = high_low(dot(basis, jnp.concatenate([basis, gained], 1), TN))
    out_ref[slot] = dot(jnp.concatenate([high, low], 0), order_ref[...]).astype(jnp.bfloat16)


def staged_response_kernel(start, early_ref, late_ref, gain_ref, order_ref, out_ref):
    early = early_ref.shape[0]
    for slot in range(out_ref.shape[0]):
        at = start + slot
        respond(early_ref[at] if at < early else late_ref[at - early], gain_ref, order_ref, out_ref, slot)


def response_kernel(start, legendre_hbm, gain_ref, order_ref, out_ref, legendre_ref, sems):
    count = out_ref.shape[0]
    copies = [pltpu.make_async_copy(legendre_hbm.at[start + i], legendre_ref.at[i], sems.at[i]) for i in range(count)]
    for copy in copies:
        copy.start()
    for slot in range(count):
        copies[slot].wait()
        respond(legendre_ref[slot], gain_ref, order_ref, out_ref, slot)


def slot_order(slots, bins):
    out = np.zeros((slots * 2 * bins, slots * 2 * bins), np.float32)
    for b in range(bins):
        for c in range(2):
            for t in range(slots):
                out[(t * 2 + c) * bins + b, (b * slots + t) * 2 + c] = 1
    return out.astype(jnp.bfloat16)


def synthesis_kernel(arrivals, pieces, kept_ref, *refs):
    partials, refs = refs[:arrivals], refs[arrivals:]
    response_refs, (order_ref, out_ref) = refs[:pieces], refs[pieces:]
    cycles = response_refs[0].shape[1] // 2
    bins = kept_ref.shape[1] // cycles
    slots = kept_ref.shape[0] // 2
    responses = [ref.at[i] for ref in response_refs for i in range(ref.shape[0])]
    total = kept_ref[...]
    for ref in partials:
        total = total + ref[...].astype(jnp.float32)
    modes = jnp.concatenate([total[:, b * cycles : (b + 1) * cycles] for b in range(bins)], 0)
    high, low = high_low(modes)
    high = dot(order_ref[...], high)
    low = dot(order_ref[...], low)
    per_slot = 2 * bins
    parts = []
    for t in range(slots):
        rows = slice(t * per_slot, (t + 1) * per_slot)
        left = jnp.concatenate([high[rows, :], low[rows, :]], 0).astype(jnp.bfloat16)
        part = dot(twice(left), responses[t][...])
        parts.append(part[:per_slot, :] + part[per_slot:, :])
    parts.append(jnp.zeros((128 - slots * per_slot, 2 * cycles), jnp.float32))
    result = jnp.concatenate(parts, 0)
    out_ref[...] = jnp.transpose(result).astype(jnp.bfloat16)


def order_classes(orders):
    return [np.arange(0, orders, 4), np.arange(2, orders, 4), np.arange(1, orders, 2)]


def inverse_tables(orders):
    quarter = NPHI // 4
    k = np.arange(quarter, dtype=np.int64)[None, :]
    rows = []
    for m in order_classes(orders):
        angle = (m[:, None] * k % NPHI) * (2 * np.pi / NPHI)
        rows += [np.cos(angle), -np.sin(angle)]
    return np.concatenate(np.split(np.concatenate(rows), quarter // 512, axis=1)).astype(np.float32).astype(jnp.bfloat16)


def padded(count):
    return -(-count // LANES) * LANES


def order_lanes(orders):
    out = []
    for m in order_classes(orders):
        out.append(np.concatenate([m, np.full(padded(len(m)) - len(m), -1)]))
    return np.concatenate(out).astype(np.int32)[None, :]


def turn_rows(order_row):
    m = np.maximum(order_row[0], 0).astype(np.float64)
    weight = np.where(order_row[0] == 0, 1.0, 2.0)
    sign = np.where(order_row[0] % 4 == 3, 1.0, -1.0)
    parts = np_high_low(np.cos(np.pi * m / NPHI) * weight) + np_high_low(np.sin(np.pi * m / NPHI) * weight)
    parts = parts + (weight.astype(jnp.bfloat16), sign.astype(jnp.bfloat16))
    return np.stack(parts + (np.zeros_like(parts[0]),) * 10)


def part_rows(part, bins, cycles_here):
    shape = (2 * bins * cycles_here, 4 * bins * cycles_here)
    row = lax.broadcasted_iota(jnp.int32, shape, 0)
    column = lax.broadcasted_iota(jnp.int32, shape, 1)
    cycle = lax.rem(row, cycles_here)
    bin_number = lax.rem(lax.div(row, cycles_here), bins)
    filter_number = lax.div(row, cycles_here * bins)
    return hot(column == ((filter_number * cycles_here + cycle) * 2 + part) * bins + bin_number)


def inverse_kernel(arrived_ref, slots_ref, turn_hbm, table_hbm, kappa_hbm, potential_hbm,
                   turn_ref, table_ref, wide_ref, kappa_ref, potential_ref, sems, out_sems):
    copies = [pltpu.make_async_copy(turn_hbm, turn_ref, sems.at[0])]
    quarter = NPHI // 4
    chunk = table_ref.shape[1]
    chunks = quarter // chunk
    part = table_ref.shape[0] // chunks
    for i in range(chunks):
        rows = pl.ds(i * part, part)
        copies.append(pltpu.make_async_copy(table_hbm.at[rows], table_ref.at[rows], sems.at[1 + i]))
    for copy in copies:
        copy.start()
    devices, slots = slots_ref.shape
    bins, cycles_here, _ = kappa_ref.shape
    order_count = part // 2
    per_slot = 2 * bins
    per_source = 2 * cycles_here
    wide_ref[...] = arrived_ref[...].astype(jnp.float32)
    turned = [jnp.transpose(wide_ref[pl.ds(i, devices, stride=per_source), :]) for i in range(per_source)]
    few, many = order_count // 4, order_count // 2
    starts = [0, padded(few), 2 * padded(few)]
    lane = lax.broadcasted_iota(jnp.int32, (1, turn_ref.shape[1]), 1)
    orders = jnp.where(lane < few, 4 * lane, -1)
    within = lane - starts[1]
    orders = jnp.where((within >= 0) & (within < few), 4 * within + 2, orders)
    within = lane - starts[2]
    orders = jnp.where((within >= 0) & (within < many), 2 * within + 1, orders)
    lefts, picks = [], []
    for t in range(slots):
        lefts.append(jnp.concatenate([x[t * per_slot : (t + 1) * per_slot, :] for x in turned], 0))
        picks.append(hot(slots_ref[:, t : t + 1] == orders))
    spectrum = dot(jnp.concatenate(lefts, 1).astype(jnp.bfloat16), jnp.concatenate(picks, 0))
    spectrum = spectrum.astype(jnp.bfloat16)
    real_in = dot(part_rows(0, bins, cycles_here), spectrum)
    imag_in = dot(part_rows(1, bins, cycles_here), spectrum)
    copies[0].wait()
    turn = turn_ref[...].astype(jnp.float32)
    odd = lax.rem(lax.rem(lax.broadcasted_iota(jnp.int32, real_in.shape, 0), cycles_here), 2) == 1
    turn_cos = jnp.where(odd, turn[0:1, :] + turn[1:2, :], turn[4:5, :])
    turn_sin = jnp.where(odd, turn[2:3, :] + turn[3:4, :], 0.0)
    real = real_in * turn_cos - imag_in * turn_sin
    imag = real_in * turn_sin + imag_in * turn_cos
    sign = turn[5:6, starts[2] :]
    count = real.shape[0]
    lefts = []
    for index, start in enumerate(starts):
        lanes = slice(start, start + (few if index < 2 else many))
        cos_rows, sin_rows = [real[:, lanes]], [imag[:, lanes]]
        if index == 2:
            cos_rows.append(imag[:, lanes] * sign[:, :many])
            sin_rows.append(-real[:, lanes] * sign[:, :many])
        for rows in (cos_rows, sin_rows):
            lefts.append(jnp.concatenate([y for x in rows for y in high_low(x)], 0))
    results = []
    for index in range(chunks):
        copies[1 + index].wait()
        row = index * part
        sums = []
        for at in range(3):
            height = few if at < 2 else many
            both = dot(lefts[2 * at], table_ref[row : row + height, :])
            both = both + dot(lefts[2 * at + 1], table_ref[row + height : row + 2 * height, :])
            row += 2 * height
            sums += [both[i : i + count, :] + both[i + count : i + 2 * count, :] for i in range(0, both.shape[0], 2 * count)]
        even, other = sums[0] + sums[1], sums[0] - sums[1]
        values = (even + sums[2], other + sums[3], even - sums[2], other - sums[3])
        for j, value in enumerate(values):
            lanes = pl.ds(j * quarter + index * chunk, chunk)
            for f, (out_ref, out_hbm) in enumerate(((kappa_ref, kappa_hbm), (potential_ref, potential_hbm))):
                for b in range(bins):
                    at = (f * bins + b) * cycles_here
                    out_ref[b, :, lanes] = value[at : at + cycles_here, :]
                copy = pltpu.make_async_copy(out_ref.at[:, :, lanes], out_hbm.at[:, :, lanes], out_sems.at[len(results)])
                copy.start()
                results.append(copy)
    for copy in results:
        copy.wait()


def in_hbm(x):
    return pltpu.with_memory_space_constraint(jnp.asarray(x), pltpu.HBM)


def params(orders):
    small = 14 if orders <= 512 else 56
    return pltpu.CompilerParams(vmem_limit_bytes=small * 1024 * 1024)


def per_device(weights, offsets, counts, block_ids, m_table, legendre):
    axes = ("blk", "y", "core")
    _, devices, capacity, bins, _ = weights.shape
    slots, degrees, cycles = legendre.shape
    orders = m_table.shape[0]
    groups = devices * capacity
    cycles_here = cycles // devices
    width = bins * cycles
    staged = legendre.size <= 4 * 1024 * 1024
    limits = params(orders)
    hbm = pl.BlockSpec(memory_space=pltpu.HBM)
    vmem = pl.BlockSpec(memory_space=pltpu.VMEM)

    def shaped(*shape, dtype=jnp.bfloat16):
        return jax.ShapeDtypeStruct(shape, dtype)

    rows = slot_rows(orders, slots)
    inner, outer = analysis_tables(orders)
    live = (capacity + 1) * devices // 2
    key_rows = -(-live // LANES) * 16
    shapes = [
        shaped(bins * live + key_rows, BLOCK),
        shaped(1, orders, dtype=jnp.int32),
        shaped(*rows.shape),
        shaped(*inner.shape),
        shaped(*outer.shape),
    ]
    operands = [
        weights.reshape(groups * bins, BLOCK),
        offsets.reshape(groups, BLOCK),
        counts,
        jnp.transpose(block_ids[0]),
        m_table,
        rows,
        inner,
        outer,
    ]
    ahead = slots * 5 // 6 if staged else 0
    if staged:
        shapes.append(shaped(ahead, degrees, cycles))
        operands.append(legendre)
    deposits, *shared = pl.pallas_call(
        functools.partial(first_kernel, slots, cycles_here * SEGMENTS, ahead),
        in_specs=[hbm] * len(operands),
        out_specs=(vmem,) * len(shapes),
        out_shape=tuple(shapes),
        scratch_shapes=[
            pltpu.VMEM((groups * bins, BLOCK), jnp.bfloat16),
            pltpu.VMEM((groups, BLOCK), jnp.int32),
            pltpu.VMEM((1, devices), jnp.int32),
            pltpu.VMEM((capacity, devices), jnp.int32),
            pltpu.VMEM((orders,), jnp.int32),
            pltpu.VMEM((groups * bins, BLOCK), jnp.float32),
            pltpu.VMEM((bins, live, BLOCK), jnp.bfloat16),
            pltpu.VMEM((live, BLOCK), jnp.float32),
            pltpu.SemaphoreType.DMA((len(operands),)),
        ],
        compiler_params=limits,
        name="deposit",
    )(*[in_hbm(x) for x in operands])
    early = shared.pop() if staged else None

    def swap(x, mask, odd_mask=None):
        masks = (mask, mask if odd_mask is None else odd_mask)
        return lax.ppermute(x, axes, [(i, i ^ masks[i % 2]) for i in range(devices)])

    other = swap(deposits, 1)
    cost = pl.CostEstimate(flops=8 * orders * 256 * bins * live, bytes_accessed=4 * orders * width, transcendentals=0)
    modes_shape = (width // LANES, orders, LANES)
    own, own_inner, own_outer, *late = pl.pallas_call(
        functools.partial(own_kernel, bins, live, cycles, ahead),
        in_specs=[vmem] * 5 + [hbm] * staged,
        out_specs=(vmem,) * (3 + staged),
        out_shape=(
            shaped(*modes_shape, dtype=jnp.float32),
            shaped(orders, inner.shape[1] // 2),
            shaped(orders, outer.shape[1] // 2),
        ) + (shaped(slots - ahead, degrees, cycles),) * staged,
        scratch_shapes=[pltpu.SemaphoreType.DMA] * staged,
        compiler_params=limits,
        cost_estimate=cost,
        name="own_groups",
    )(deposits, *shared, *[in_hbm(legendre)] * staged)

    basis = [early, *late] if staged else [legendre]

    groups_of_bits = bit_groups(devices)
    stages = len(groups_of_bits)
    gain, order = gain_column(degrees), interleave(cycles, cycles_here)
    blocks = devices // 2
    kernel, inputs = functools.partial(other_kernel, bins, live, cycles), (other, own_inner, own_outer, own)
    scratch = [pltpu.VMEM(modes_shape, jnp.float32)]
    responses = []
    for stage, bits in enumerate(groups_of_bits):
        ways = 1 << len(bits)
        blocks //= ways
        rows_here = blocks * 2 * slots
        kept, *sends = pl.pallas_call(
            kernel,
            in_specs=[vmem] * len(inputs),
            out_specs=(vmem,) * ways,
            out_shape=(shaped(rows_here, width, dtype=jnp.float32),) + (shaped(rows_here, width),) * (ways - 1),
            scratch_shapes=scratch,
            compiler_params=limits,
            name="merge" if stage else "other_groups",
        )(*inputs)
        sends, basis = lax.optimization_barrier((sends, basis))
        if stage == 0:
            order_of = send_order(ways)
            arrived = [swap(x, even << bits[0], odd << bits[0]) for x, (even, odd) in zip(sends, order_of)]
        else:
            line = range(ways - 1, 0, -1)
            arrived = [swap(sends[i - 1], i << bits[0]) for i in line]
        first, last = (-(-slots * k * (2 * stages + 1 - k) // (stages * (stages + 1))) for k in (stage, stage + 1))
        count = last - first
        shape = shaped(count, 2 * cycles, 2 * cycles)
        cost = pl.CostEstimate(
            flops=6 * count * degrees * cycles * cycles, bytes_accessed=2 * count * degrees * cycles, transcendentals=0
        )
        if staged:
            kernel, scratch = functools.partial(staged_response_kernel, first), []
        else:
            kernel = functools.partial(response_kernel, first)
            scratch = [pltpu.VMEM((count, degrees, cycles), jnp.bfloat16), pltpu.SemaphoreType.DMA((count,))]
        response = pl.pallas_call(
            kernel,
            in_specs=[vmem if staged else hbm] * len(basis) + [vmem] * 2,
            out_specs=vmem,
            out_shape=shape,
            scratch_shapes=scratch,
            compiler_params=limits,
            cost_estimate=cost,
            name="response",
        )(*basis if staged else [in_hbm(x) for x in basis], gain, order)
        *arrived, response = lax.optimization_barrier((*arrived, response))
        responses.append(response)
        kernel, inputs, scratch = functools.partial(merge_kernel, len(arrived)), (kept, *arrived), []

    outgoing = pl.pallas_call(
        functools.partial(synthesis_kernel, len(inputs) - 1, len(responses)),
        in_specs=[vmem] * (len(inputs) + len(responses) + 1),
        out_specs=vmem,
        out_shape=shaped(2 * cycles, 128),
        compiler_params=limits,
        name="synthesis",
    )(*inputs, *responses, slot_order(slots, bins))
    outgoing = outgoing.reshape(devices, 2 * cycles_here, 128)
    outgoing, held = lax.optimization_barrier((outgoing, m_table))
    arrived = lax.all_to_all(outgoing, axes, split_axis=0, concat_axis=0, tiled=True)
    arrived = arrived.reshape(2 * cycles, 128)
    if staged:
        arrived = pltpu.with_memory_space_constraint(arrived, pltpu.VMEM)

    lanes = order_lanes(orders)
    constants = [turn_rows(lanes), inverse_tables(orders)]
    chunks = NPHI // 4 // constants[-1].shape[1]
    map_shape = shaped(bins, cycles_here, NPHI, dtype=jnp.float32)
    return pl.pallas_call(
        inverse_kernel,
        in_specs=[vmem] * 2 + [hbm] * 2,
        out_specs=(hbm, hbm),
        out_shape=(map_shape, map_shape),
        scratch_shapes=[
            *[pltpu.VMEM(x.shape, x.dtype) for x in constants],
            pltpu.VMEM((2 * cycles, 128), jnp.float32),
            pltpu.VMEM(map_shape.shape, jnp.float32),
            pltpu.VMEM(map_shape.shape, jnp.float32),
            pltpu.SemaphoreType.DMA((1 + chunks,)),
            pltpu.SemaphoreType.DMA((8 * chunks,)),
        ],
        compiler_params=limits,
        name="inverse",
    )(arrived, held.reshape(devices, slots), *[in_hbm(x) for x in constants])


def solution(mesh):
    blocks, columns = mesh.devices.shape
    fine = Mesh(mesh.devices.reshape(blocks, columns // 2, 2), ("blk", "y", "core"))
    axes = ("blk", "y", "core")
    placed = (
        P(axes, None, None, None, None),
        P(axes, None, None, None),
        P(axes, None),
        P(axes, None, None),
        P(),
        P(axes, None, None),
    )
    return jax.shard_map(
        per_device,
        mesh=fine,
        in_specs=placed,
        out_specs=(P(None, axes, None), P(None, axes, None)),
        check_vma=False,
    )
```

```python
import functools

import jax
import jax.numpy as jnp
import numpy as np
from jax import lax
from jax.experimental import pallas as pl
from jax.experimental.pallas import tpu as pltpu
from jax.sharding import Mesh, PartitionSpec as P

NPHI = 4096
BLOCK = 128
SEGMENTS = NPHI // BLOCK
LANES = 128
CHUNK = 192

NT = (((1,), (1,)), ((), ()))
TN = (((0,), (0,)), ((), ()))


def dot(a, b, dims=(((1,), (0,)), ((), ()))):
    return lax.dot_general(a, b, dims, preferred_element_type=jnp.float32)


def high_low(x):
    high = x.astype(jnp.bfloat16)
    return high, (x - high.astype(jnp.float32)).astype(jnp.bfloat16)


def np_high_low(x):
    high = x.astype(np.float32).astype(jnp.bfloat16)
    return high, (x - high.astype(np.float64)).astype(np.float32).astype(jnp.bfloat16)


def analysis_tables(orders):
    m = np.arange(orders, dtype=np.int64)[:, None]
    p = np.arange(BLOCK, dtype=np.int64)[None, :]
    angle = (m * p % NPHI) * (2 * np.pi / NPHI)
    inner = np.concatenate(np_high_low(np.cos(angle)) + np_high_low(-np.sin(angle)), 1)
    half = np.arange(2 * SEGMENTS, dtype=np.int64)[None, :]
    steps = 2 * BLOCK * (half % SEGMENTS) + half // SEGMENTS
    angle = (m * steps % (2 * NPHI)) * (np.pi / NPHI)
    outer = np.concatenate(np_high_low(np.cos(angle) / NPHI) + np_high_low(-np.sin(angle) / NPHI), 1)
    return inner, outer


def bit_groups(devices):
    bits = list(range(1, devices.bit_length() - 1))
    return [bits[i : i + 2] for i in range(0, len(bits), 2)]


def positions(devices):
    order = [0]
    for group in bit_groups(devices):
        order = [p | (v << group[0]) for p in order for v in range(1 << len(group))]
    return order


def slot_rows(orders, slots):
    out = np.zeros((orders // 2, orders), np.float32)
    for block, position in enumerate(positions(orders // slots)):
        for slot in range(slots):
            out[block * slots + slot, position * slots + slot] = 1
    return out.astype(jnp.bfloat16)


def rolled(x, shift):
    return jnp.concatenate([x[:, shift:], x[:, :shift]], 1)


def exclusive_or(table, me, slots):
    orders = table.shape[1]
    block = lax.div(lax.broadcasted_iota(jnp.int32, table.shape, 1), slots)
    for bit in range((orders // slots).bit_length() - 1):
        shift = slots << bit
        swapped = jnp.where((block >> bit) % 2 == 0, rolled(table, shift), rolled(table, orders - shift))
        table = jnp.where(jnp.broadcast_to((me >> bit) & 1, table.shape) == 1, swapped, table)
    return table


def hot(condition):
    return jnp.where(condition, 1.0, 0.0).astype(jnp.bfloat16)


def twice(x):
    return jnp.concatenate([x, x], 1)


def first_kernel(slots, blocks_here, staged, w_hbm, off_hbm, cnt_hbm, ids_hbm, table_hbm, rows_hbm, inner_hbm, outer_hbm, *refs):
    if staged:
        legendre_hbm, *refs = refs
    out_ref, table_ref, rows_ref, inner_ref, outer_ref, *refs = refs
    if staged:
        legendre_ref, *refs = refs
    w_ref, off_ref, cnt_ref, ids_ref, flat_ref, wide_ref, live_w_ref, live_off_ref, sems = refs
    pairs = (
        (cnt_hbm, cnt_ref), (ids_hbm, ids_ref), (off_hbm, off_ref), (w_hbm, w_ref),
        (table_hbm, flat_ref), (rows_hbm, rows_ref), (inner_hbm, inner_ref), (outer_hbm, outer_ref),
    )
    if staged:
        pairs = pairs + ((legendre_hbm.at[pl.ds(0, staged)], legendre_ref),)
    copies = [pltpu.make_async_copy(a, b, sems.at[i]) for i, (a, b) in enumerate(pairs)]
    for copy in copies[:4]:
        copy.start()
    groups = off_ref.shape[0]
    capacity, devices = ids_ref.shape
    bins, live, _ = live_w_ref.shape
    pack = 16
    key_tiles = (out_ref.shape[0] - bins * live) // pack

    owner = lax.div(lax.broadcasted_iota(jnp.int32, (devices, groups), 1), capacity)
    source = lax.broadcasted_iota(jnp.int32, (devices, groups), 0)
    member = lax.rem(lax.broadcasted_iota(jnp.int32, (capacity, groups), 1), capacity)
    own_row = lax.broadcasted_iota(jnp.int32, (capacity, groups), 0) == member
    for copy in copies[:2]:
        copy.wait()
    counts = jnp.broadcast_to(cnt_ref[...].astype(jnp.float32), (8, devices)).astype(jnp.bfloat16)
    count = dot(counts, hot(source == owner))[0:1, :]
    before = dot(counts, hot(source < owner))[0:1, :]
    number = member[0:1, :].astype(jnp.float32)
    place = jnp.where(number < count, before + number, -1.0).astype(jnp.int32)
    packing = hot(lax.broadcasted_iota(jnp.int32, (key_tiles * LANES, groups), 0) == place)

    ids = dot(ids_ref[...].astype(jnp.float32).astype(jnp.bfloat16), hot(source == owner))
    ids = jnp.sum(jnp.where(own_row, ids, 0.0), axis=0, keepdims=True)
    block = ids.astype(jnp.int32) + owner[0:1, :] * blocks_here
    cycle = lax.div(block, SEGMENTS)
    phase = lax.rem(cycle, 2) * SEGMENTS + lax.rem(block, SEGMENTS)
    row = lax.broadcasted_iota(jnp.int32, (pack, groups), 0)
    keys = jnp.where(row == 0, lax.div(cycle, 16), jnp.where(row == 1, lax.rem(cycle, 16), phase))
    keys = dot(keys.astype(jnp.float32).astype(jnp.bfloat16), packing, NT).astype(jnp.bfloat16)
    for tile in range(key_tiles):
        out_ref[bins * live + tile * pack : bins * live + (tile + 1) * pack, :] = keys[:, tile * LANES : (tile + 1) * LANES]

    for copy in copies[2:4]:
        copy.wait()
    for copy in copies[4:]:
        copy.start()
    packing = packing[:live, :]
    live_off_ref[...] = dot(packing, off_ref[...].astype(jnp.float32).astype(jnp.bfloat16))
    wide_ref[...] = w_ref[...].astype(jnp.float32)
    for b in range(bins):
        live_w_ref[b] = dot(packing, wide_ref[pl.ds(b, groups, stride=bins), :].astype(jnp.bfloat16)).astype(jnp.bfloat16)

    pixel = lax.broadcasted_iota(jnp.int32, (pack, BLOCK), 0)
    pixels = [(pixel + pack * k).astype(jnp.float32).astype(jnp.bfloat16) for k in range(BLOCK // pack)]
    alone = [hot(pixel == i) for i in range(pack)]
    one = jnp.ones((pack, BLOCK), jnp.bfloat16)
    zero = jnp.zeros((pack, BLOCK), jnp.bfloat16)

    def deposit(step, carry):
        start = pl.multiple_of(step * pack, pack)
        weights = [live_w_ref[b, pl.ds(start, pack), :] for b in range(bins)]
        left, right = [], []
        for i in range(pack):
            left.append(jnp.concatenate([w * alone[i] for w in weights], 0))
            at = jnp.broadcast_to(live_off_ref[pl.ds(start + i, 1), :], (pack, BLOCK)).astype(jnp.bfloat16)
            right.append(jnp.concatenate([jnp.where(at == x, one, zero) for x in pixels], 0))
        out = dot(jnp.concatenate(left, 1), jnp.concatenate(right, 1), NT).astype(jnp.bfloat16)
        for b in range(bins):
            out_ref[pl.ds(pl.multiple_of(b * live + start, pack), pack), :] = out[b * pack : (b + 1) * pack, :]
        return carry

    lax.fori_loop(0, live // pack, deposit, 0, unroll=9)
    for copy in copies[4:8]:
        copy.wait()
    me = lax.axis_index("blk")
    for axis in ("y", "core"):
        me = me * lax.axis_size(axis) + lax.axis_index(axis)
    table_ref[...] = exclusive_or(flat_ref[...].reshape(table_ref.shape), me, slots)
    for copy in copies[8:]:
        copy.wait()


def add_modes(bins, groups, cycles, groups_ref, inner_ref, outer_ref, add):
    pack = 16
    keys = groups_ref[bins * groups :, :].astype(jnp.float32)
    keys = jnp.concatenate([keys[i * pack : (i + 1) * pack, :] for i in range(keys.shape[0] // pack)], 1)
    cycle = (keys[0:1, :groups] * 16.0 + keys[1:2, :groups]).astype(jnp.int32)
    phase = keys[2:3, :groups].astype(jnp.int32)
    cycle_hot = hot(lax.broadcasted_iota(jnp.int32, (cycles, groups), 0) == cycle)
    half_hot = hot(lax.broadcasted_iota(jnp.int32, (2 * SEGMENTS, groups), 0) == phase)
    phase_hot = jnp.concatenate([half_hot, half_hot], 0)
    deposits = [twice(groups_ref[b * groups : (b + 1) * groups, :]) for b in range(bins)]
    for start in range(0, inner_ref.shape[0], 2 * CHUNK):
        rows = slice(start, start + 2 * CHUNK)
        outer = dot(outer_ref[rows, :], phase_hot)
        outer_cos, outer_sin = outer[:CHUNK, :], outer[CHUNK:, :]
        for b, deposit in enumerate(deposits):
            inner = dot(inner_ref[rows, :], deposit, NT)
            inner_cos, inner_sin = inner[:CHUNK, :], inner[CHUNK:, :]
            real = inner_cos * outer_cos - inner_sin * outer_sin
            imag = inner_cos * outer_sin + inner_sin * outer_cos
            both = dot(jnp.concatenate([real, imag], 0).astype(jnp.bfloat16), cycle_hot, NT)
            for part in range(2):
                value = both[part * CHUNK : (part + 1) * CHUNK, :]
                for tile in range(cycles // LANES):
                    add(b * (cycles // LANES) + tile, start + part, value[:, tile * LANES : (tile + 1) * LANES])


def own_kernel(bins, groups, cycles, staged, groups_ref, table_ref, rows_ref, inner_ref, outer_ref, *refs):
    if staged:
        legendre_hbm, out_ref, inner_out, outer_out, legendre_ref, sem = refs
        late = pltpu.make_async_copy(legendre_hbm.at[pl.ds(staged, legendre_ref.shape[0])], legendre_ref, sem)
        late.start()
    else:
        out_ref, inner_out, outer_out = refs
    count, orders = rows_ref.shape
    held = hot(lax.broadcasted_iota(jnp.int32, (orders, orders), 0) == table_ref[...])
    for start in range(0, count, CHUNK):
        pick = dot(rows_ref[start : start + CHUNK, :], held, NT).astype(jnp.bfloat16)
        inner = dot(pick, inner_ref[...]).astype(jnp.bfloat16)
        outer = dot(pick, outer_ref[...]).astype(jnp.bfloat16)
        for part in range(2):
            rows = slice(2 * start + part * CHUNK, 2 * start + (part + 1) * CHUNK)
            inner_out[rows, :] = inner[:, part * 2 * BLOCK : (part + 1) * 2 * BLOCK]
            outer_out[rows, :] = outer[:, part * BLOCK : (part + 1) * BLOCK]

    def add(tile, first, value):
        out_ref.at[tile][pl.ds(first, value.shape[0], stride=2), :] = value

    add_modes(bins, groups, cycles, groups_ref, inner_out, outer_out, add)
    if staged:
        late.wait()


def split_sum(parts, tile, keep_ref, send_refs):
    rows = keep_ref.shape[0]
    lanes = slice(tile * LANES, (tile + 1) * LANES)
    for i, out_ref in enumerate((keep_ref, *send_refs)):
        value = sum(part(slice(i * rows, (i + 1) * rows), lanes) for part in parts)
        out_ref[:, lanes] = value.astype(out_ref.dtype)


def send_order(ways):
    return [(1, 2), (3, 3), (2, 1)] if ways == 4 else [(i, i) for i in range(1, ways)]


def other_kernel(bins, groups, cycles, groups_ref, inner_ref, outer_ref, own_ref, keep_ref, *refs):
    *send_refs, other_ref = refs

    def add(tile, first, value):
        other_ref.at[tile][pl.ds(first, value.shape[0], stride=2), :] = value

    add_modes(bins, groups, cycles, groups_ref, inner_ref, outer_ref, add)
    rows = keep_ref.shape[0]
    core = lax.axis_index("core")
    blocks = [(0, 0)] + send_order(len(send_refs) + 1)
    for (even, odd), out_ref in zip(blocks, (keep_ref, *send_refs)):
        first = even * rows if even == odd else pl.multiple_of((even + core * (odd - even)) * rows, rows)
        for tile in range(own_ref.shape[0]):
            value = own_ref[tile, pl.ds(first, rows), :] + other_ref[tile, pl.ds(first, rows), :]
            out_ref[:, tile * LANES : (tile + 1) * LANES] = value.astype(out_ref.dtype)


def merge_kernel(count, kept_ref, *refs):
    arrived, outs = refs[:count], refs[count:]
    for tile in range(kept_ref.shape[1] // LANES):
        parts = [lambda rows, lanes, ref=ref: ref[rows, lanes].astype(jnp.float32) for ref in (kept_ref, *arrived)]
        split_sum(parts, tile, outs[0], outs[1:])


def gain_column(degrees):
    l = np.arange(degrees, dtype=np.float32)
    return np.where(l > 0.5, np.float32(-20000.0) / np.maximum(l * (l + 1), np.float32(1)), np.float32(0)).astype(np.float32)[:, None] * np.ones((1, BLOCK), np.float32)


def interleave(cycles, cycles_here):
    out = np.zeros((2 * cycles, 2 * cycles), np.float32)
    for f in range(2):
        for c in range(cycles):
            out[f * cycles + c, (c // cycles_here * 2 + f) * cycles_here + c % cycles_here] = 1
    return out.astype(jnp.bfloat16)


def respond(basis, gain_ref, order_ref, out_ref, slot):
    cycles = basis.shape[1]
    gain = jnp.concatenate([gain_ref[...]] * (cycles // BLOCK), 1)
    gained = (basis.astype(jnp.float32) * gain).astype(jnp.bfloat16)
    high, low = high_low(dot(basis, jnp.concatenate([basis, gained], 1), TN))
    out_ref[slot] = dot(jnp.concatenate([high, low], 0), order_ref[...]).astype(jnp.bfloat16)


def staged_response_kernel(start, early_ref, late_ref, gain_ref, order_ref, out_ref):
    early = early_ref.shape[0]
    for slot in range(out_ref.shape[0]):
        at = start + slot
        respond(early_ref[at] if at < early else late_ref[at - early], gain_ref, order_ref, out_ref, slot)


def response_kernel(start, legendre_hbm, gain_ref, order_ref, out_ref, legendre_ref, sems):
    count = out_ref.shape[0]
    copies = [pltpu.make_async_copy(legendre_hbm.at[start + i], legendre_ref.at[i], sems.at[i]) for i in range(count)]
    for copy in copies:
        copy.start()
    for slot in range(count):
        copies[slot].wait()
        respond(legendre_ref[slot], gain_ref, order_ref, out_ref, slot)


def slot_order(slots, bins):
    out = np.zeros((slots * 2 * bins, slots * 2 * bins), np.float32)
    for b in range(bins):
        for c in range(2):
            for t in range(slots):
                out[(t * 2 + c) * bins + b, (b * slots + t) * 2 + c] = 1
    return out.astype(jnp.bfloat16)


def synthesis_kernel(arrivals, pieces, kept_ref, *refs):
    partials, refs = refs[:arrivals], refs[arrivals:]
    response_refs, (order_ref, out_ref) = refs[:pieces], refs[pieces:]
    cycles = response_refs[0].shape[1] // 2
    bins = kept_ref.shape[1] // cycles
    slots = kept_ref.shape[0] // 2
    responses = [ref.at[i] for ref in response_refs for i in range(ref.shape[0])]
    total = kept_ref[...]
    for ref in partials:
        total = total + ref[...].astype(jnp.float32)
    modes = jnp.concatenate([total[:, b * cycles : (b + 1) * cycles] for b in range(bins)], 0)
    high, low = high_low(modes)
    high = dot(order_ref[...], high)
    low = dot(order_ref[...], low)
    per_slot = 2 * bins
    parts = []
    for t in range(slots):
        rows = slice(t * per_slot, (t + 1) * per_slot)
        left = jnp.concatenate([high[rows, :], low[rows, :]], 0).astype(jnp.bfloat16)
        part = dot(twice(left), responses[t][...])
        parts.append(part[:per_slot, :] + part[per_slot:, :])
    parts.append(jnp.zeros((128 - slots * per_slot, 2 * cycles), jnp.float32))
    result = jnp.concatenate(parts, 0)
    out_ref[...] = jnp.transpose(result).astype(jnp.bfloat16)


def order_classes(orders):
    return [np.arange(0, orders, 4), np.arange(2, orders, 4), np.arange(1, orders, 2)]


def inverse_tables(orders):
    quarter = NPHI // 4
    k = np.arange(quarter, dtype=np.int64)[None, :]
    rows = []
    for m in order_classes(orders):
        angle = (m[:, None] * k % NPHI) * (2 * np.pi / NPHI)
        rows += [np.cos(angle), -np.sin(angle)]
    return np.concatenate(np.split(np.concatenate(rows), quarter // 512, axis=1)).astype(np.float32).astype(jnp.bfloat16)


def padded(count):
    return -(-count // LANES) * LANES


def order_lanes(orders):
    out = []
    for m in order_classes(orders):
        out.append(np.concatenate([m, np.full(padded(len(m)) - len(m), -1)]))
    return np.concatenate(out).astype(np.int32)[None, :]


def turn_rows(order_row):
    m = np.maximum(order_row[0], 0).astype(np.float64)
    weight = np.where(order_row[0] == 0, 1.0, 2.0)
    sign = np.where(order_row[0] % 4 == 3, 1.0, -1.0)
    parts = np_high_low(np.cos(np.pi * m / NPHI) * weight) + np_high_low(np.sin(np.pi * m / NPHI) * weight)
    parts = parts + (weight.astype(jnp.bfloat16), sign.astype(jnp.bfloat16))
    return np.stack(parts + (np.zeros_like(parts[0]),) * 10)


def part_rows(part, bins, cycles_here):
    shape = (2 * bins * cycles_here, 4 * bins * cycles_here)
    row = lax.broadcasted_iota(jnp.int32, shape, 0)
    column = lax.broadcasted_iota(jnp.int32, shape, 1)
    cycle = lax.rem(row, cycles_here)
    bin_number = lax.rem(lax.div(row, cycles_here), bins)
    filter_number = lax.div(row, cycles_here * bins)
    return hot(column == ((filter_number * cycles_here + cycle) * 2 + part) * bins + bin_number)


def inverse_kernel(arrived_ref, slots_ref, turn_hbm, table_hbm, kappa_hbm, potential_hbm,
                   turn_ref, table_ref, wide_ref, kappa_ref, potential_ref, sems, out_sems):
    copies = [pltpu.make_async_copy(turn_hbm, turn_ref, sems.at[0])]
    quarter = NPHI // 4
    chunk = table_ref.shape[1]
    chunks = quarter // chunk
    part = table_ref.shape[0] // chunks
    for i in range(chunks):
        rows = pl.ds(i * part, part)
        copies.append(pltpu.make_async_copy(table_hbm.at[rows], table_ref.at[rows], sems.at[1 + i]))
    for copy in copies:
        copy.start()
    devices, slots = slots_ref.shape
    bins, cycles_here, _ = kappa_ref.shape
    order_count = part // 2
    per_slot = 2 * bins
    per_source = 2 * cycles_here
    wide_ref[...] = arrived_ref[...].astype(jnp.float32)
    turned = [jnp.transpose(wide_ref[pl.ds(i, devices, stride=per_source), :]) for i in range(per_source)]
    few, many = order_count // 4, order_count // 2
    starts = [0, padded(few), 2 * padded(few)]
    lane = lax.broadcasted_iota(jnp.int32, (1, turn_ref.shape[1]), 1)
    orders = jnp.where(lane < few, 4 * lane, -1)
    within = lane - starts[1]
    orders = jnp.where((within >= 0) & (within < few), 4 * within + 2, orders)
    within = lane - starts[2]
    orders = jnp.where((within >= 0) & (within < many), 2 * within + 1, orders)
    lefts, picks = [], []
    for t in range(slots):
        lefts.append(jnp.concatenate([x[t * per_slot : (t + 1) * per_slot, :] for x in turned], 0))
        picks.append(hot(slots_ref[:, t : t + 1] == orders))
    spectrum = dot(jnp.concatenate(lefts, 1).astype(jnp.bfloat16), jnp.concatenate(picks, 0))
    spectrum = spectrum.astype(jnp.bfloat16)
    real_in = dot(part_rows(0, bins, cycles_here), spectrum)
    imag_in = dot(part_rows(1, bins, cycles_here), spectrum)
    copies[0].wait()
    turn = turn_ref[...].astype(jnp.float32)
    odd = lax.rem(lax.rem(lax.broadcasted_iota(jnp.int32, real_in.shape, 0), cycles_here), 2) == 1
    turn_cos = jnp.where(odd, turn[0:1, :] + turn[1:2, :], turn[4:5, :])
    turn_sin = jnp.where(odd, turn[2:3, :] + turn[3:4, :], 0.0)
    real = real_in * turn_cos - imag_in * turn_sin
    imag = real_in * turn_sin + imag_in * turn_cos
    sign = turn[5:6, starts[2] :]
    count = real.shape[0]
    lefts = []
    for index, start in enumerate(starts):
        lanes = slice(start, start + (few if index < 2 else many))
        cos_rows, sin_rows = [real[:, lanes]], [imag[:, lanes]]
        if index == 2:
            cos_rows.append(imag[:, lanes] * sign[:, :many])
            sin_rows.append(-real[:, lanes] * sign[:, :many])
        for rows in (cos_rows, sin_rows):
            lefts.append(jnp.concatenate([y for x in rows for y in high_low(x)], 0))
    results = []
    for index in range(chunks):
        copies[1 + index].wait()
        row = index * part
        sums = []
        for at in range(3):
            height = few if at < 2 else many
            both = dot(lefts[2 * at], table_ref[row : row + height, :])
            both = both + dot(lefts[2 * at + 1], table_ref[row + height : row + 2 * height, :])
            row += 2 * height
            sums += [both[i : i + count, :] + both[i + count : i + 2 * count, :] for i in range(0, both.shape[0], 2 * count)]
        even, other = sums[0] + sums[1], sums[0] - sums[1]
        values = (even + sums[2], other + sums[3], even - sums[2], other - sums[3])
        for j, value in enumerate(values):
            lanes = pl.ds(j * quarter + index * chunk, chunk)
            for f, (out_ref, out_hbm) in enumerate(((kappa_ref, kappa_hbm), (potential_ref, potential_hbm))):
                for b in range(bins):
                    at = (f * bins + b) * cycles_here
                    out_ref[b, :, lanes] = value[at : at + cycles_here, :]
                copy = pltpu.make_async_copy(out_ref.at[:, :, lanes], out_hbm.at[:, :, lanes], out_sems.at[len(results)])
                copy.start()
                results.append(copy)
    for copy in results:
        copy.wait()


def in_hbm(x):
    return pltpu.with_memory_space_constraint(jnp.asarray(x), pltpu.HBM)


def params(orders):
    small = 14 if orders <= 512 else 56
    return pltpu.CompilerParams(vmem_limit_bytes=small * 1024 * 1024)


def per_device(weights, offsets, counts, block_ids, m_table, legendre):
    axes = ("blk", "y", "core")
    _, devices, capacity, bins, _ = weights.shape
    slots, degrees, cycles = legendre.shape
    orders = m_table.shape[0]
    groups = devices * capacity
    cycles_here = cycles // devices
    width = bins * cycles
    staged = legendre.size <= 4 * 1024 * 1024
    limits = params(orders)
    hbm = pl.BlockSpec(memory_space=pltpu.HBM)
    vmem = pl.BlockSpec(memory_space=pltpu.VMEM)

    def shaped(*shape, dtype=jnp.bfloat16):
        return jax.ShapeDtypeStruct(shape, dtype)

    rows = slot_rows(orders, slots)
    inner, outer = analysis_tables(orders)
    live = (capacity + 1) * devices // 2
    key_rows = -(-live // LANES) * 16
    shapes = [
        shaped(bins * live + key_rows, BLOCK),
        shaped(1, orders, dtype=jnp.int32),
        shaped(*rows.shape),
        shaped(*inner.shape),
        shaped(*outer.shape),
    ]
    operands = [
        weights.reshape(groups * bins, BLOCK),
        offsets.reshape(groups, BLOCK),
        counts,
        jnp.transpose(block_ids[0]),
        m_table,
        rows,
        inner,
        outer,
    ]
    ahead = slots * 5 // 6 if staged else 0
    if staged:
        shapes.append(shaped(ahead, degrees, cycles))
        operands.append(legendre)
    deposits, *shared = pl.pallas_call(
        functools.partial(first_kernel, slots, cycles_here * SEGMENTS, ahead),
        in_specs=[hbm] * len(operands),
        out_specs=(vmem,) * len(shapes),
        out_shape=tuple(shapes),
        scratch_shapes=[
            pltpu.VMEM((groups * bins, BLOCK), jnp.bfloat16),
            pltpu.VMEM((groups, BLOCK), jnp.int32),
            pltpu.VMEM((1, devices), jnp.int32),
            pltpu.VMEM((capacity, devices), jnp.int32),
            pltpu.VMEM((orders,), jnp.int32),
            pltpu.VMEM((groups * bins, BLOCK), jnp.float32),
            pltpu.VMEM((bins, live, BLOCK), jnp.bfloat16),
            pltpu.VMEM((live, BLOCK), jnp.float32),
            pltpu.SemaphoreType.DMA((len(operands),)),
        ],
        compiler_params=limits,
        name="deposit",
    )(*[in_hbm(x) for x in operands])
    early = shared.pop() if staged else None

    def swap(x, mask, odd_mask=None):
        masks = (mask, mask if odd_mask is None else odd_mask)
        return lax.ppermute(x, axes, [(i, i ^ masks[i % 2]) for i in range(devices)])

    other = swap(deposits, 1)
    cost = pl.CostEstimate(flops=8 * orders * 256 * bins * live, bytes_accessed=4 * orders * width, transcendentals=0)
    modes_shape = (width // LANES, orders, LANES)
    own, own_inner, own_outer, *late = pl.pallas_call(
        functools.partial(own_kernel, bins, live, cycles, ahead),
        in_specs=[vmem] * 5 + [hbm] * staged,
        out_specs=(vmem,) * (3 + staged),
        out_shape=(
            shaped(*modes_shape, dtype=jnp.float32),
            shaped(orders, inner.shape[1] // 2),
            shaped(orders, outer.shape[1] // 2),
        ) + (shaped(slots - ahead, degrees, cycles),) * staged,
        scratch_shapes=[pltpu.SemaphoreType.DMA] * staged,
        compiler_params=limits,
        cost_estimate=cost,
        name="own_groups",
    )(deposits, *shared, *[in_hbm(legendre)] * staged)

    basis = [early, *late] if staged else [legendre]

    groups_of_bits = bit_groups(devices)
    stages = len(groups_of_bits)
    gain, order = gain_column(degrees), interleave(cycles, cycles_here)
    blocks = devices // 2
    kernel, inputs = functools.partial(other_kernel, bins, live, cycles), (other, own_inner, own_outer, own)
    scratch = [pltpu.VMEM(modes_shape, jnp.float32)]
    responses = []
    for stage, bits in enumerate(groups_of_bits):
        ways = 1 << len(bits)
        blocks //= ways
        rows_here = blocks * 2 * slots
        kept, *sends = pl.pallas_call(
            kernel,
            in_specs=[vmem] * len(inputs),
            out_specs=(vmem,) * ways,
            out_shape=(shaped(rows_here, width, dtype=jnp.float32),) + (shaped(rows_here, width),) * (ways - 1),
            scratch_shapes=scratch,
            compiler_params=limits,
            name="merge" if stage else "other_groups",
        )(*inputs)
        sends, basis = lax.optimization_barrier((sends, basis))
        if stage == 0:
            order_of = send_order(ways)
            arrived = [swap(x, even << bits[0], odd << bits[0]) for x, (even, odd) in zip(sends, order_of)]
        else:
            line = [2, 3, 1] if ways == 4 else range(ways - 1, 0, -1)
            arrived = [swap(sends[i - 1], i << bits[0]) for i in line]
        first, last = (slots * k * (4 * stages - k) // (stages * (3 * stages)) for k in (stage, stage + 1))
        count = last - first
        shape = shaped(count, 2 * cycles, 2 * cycles)
        cost = pl.CostEstimate(
            flops=6 * count * degrees * cycles * cycles, bytes_accessed=2 * count * degrees * cycles, transcendentals=0
        )
        if staged:
            kernel, scratch = functools.partial(staged_response_kernel, first), []
        else:
            kernel = functools.partial(response_kernel, first)
            scratch = [pltpu.VMEM((count, degrees, cycles), jnp.bfloat16), pltpu.SemaphoreType.DMA((count,))]
        response = pl.pallas_call(
            kernel,
            in_specs=[vmem if staged else hbm] * len(basis) + [vmem] * 2,
            out_specs=vmem,
            out_shape=shape,
            scratch_shapes=scratch,
            compiler_params=limits,
            cost_estimate=cost,
            name="response",
        )(*basis if staged else [in_hbm(x) for x in basis], gain, order)
        *arrived, response = lax.optimization_barrier((*arrived, response))
        responses.append(response)
        kernel, inputs, scratch = functools.partial(merge_kernel, len(arrived)), (kept, *arrived), []

    outgoing = pl.pallas_call(
        functools.partial(synthesis_kernel, len(inputs) - 1, len(responses)),
        in_specs=[vmem] * (len(inputs) + len(responses) + 1),
        out_specs=vmem,
        out_shape=shaped(2 * cycles, 128),
        compiler_params=limits,
        name="synthesis",
    )(*inputs, *responses, slot_order(slots, bins))
    outgoing = outgoing.reshape(devices, 2 * cycles_here, 128)
    outgoing, held = lax.optimization_barrier((outgoing, m_table))
    arrived = lax.all_to_all(outgoing, axes, split_axis=0, concat_axis=0, tiled=True)
    arrived = arrived.reshape(2 * cycles, 128)
    if staged:
        arrived = pltpu.with_memory_space_constraint(arrived, pltpu.VMEM)

    lanes = order_lanes(orders)
    constants = [turn_rows(lanes), inverse_tables(orders)]
    chunks = NPHI // 4 // constants[-1].shape[1]
    map_shape = shaped(bins, cycles_here, NPHI, dtype=jnp.float32)
    return pl.pallas_call(
        inverse_kernel,
        in_specs=[vmem] * 2 + [hbm] * 2,
        out_specs=(hbm, hbm),
        out_shape=(map_shape, map_shape),
        scratch_shapes=[
            *[pltpu.VMEM(x.shape, x.dtype) for x in constants],
            pltpu.VMEM((2 * cycles, 128), jnp.float32),
            pltpu.VMEM(map_shape.shape, jnp.float32),
            pltpu.VMEM(map_shape.shape, jnp.float32),
            pltpu.SemaphoreType.DMA((1 + chunks,)),
            pltpu.SemaphoreType.DMA((8 * chunks,)),
        ],
        compiler_params=limits,
        name="inverse",
    )(arrived, held.reshape(devices, slots), *[in_hbm(x) for x in constants])


def solution(mesh):
    blocks, columns = mesh.devices.shape
    fine = Mesh(mesh.devices.reshape(blocks, columns // 2, 2), ("blk", "y", "core"))
    axes = ("blk", "y", "core")
    placed = (
        P(axes, None, None, None, None),
        P(axes, None, None, None),
        P(axes, None),
        P(axes, None, None),
        P(),
        P(axes, None, None),
    )
    return jax.shard_map(
        per_device,
        mesh=fine,
        in_specs=placed,
        out_specs=(P(None, axes, None), P(None, axes, None)),
        check_vma=False,
    )
```
